512 devices in a mesh: segment: 8 (over z_lo), wide: 64 (over y, z_hi, x, core).
Axes of the slice: x: 4, y: 4, z: 16 (z_hi: 2, z_lo: 8; z = z_hi * 8 + z_lo), core: 2. Of those that a mesh axis runs over, the one named last changes fastest.
Arguments:
- hidden_in: bfloat16 [256, 8192], P(None, 'wide'), may hold values from -9 to 9
- gain: float32 [8, 8192], P('segment'), may hold values from 0.25 to 1.75
- w_query: bfloat16 [8, 8192, 8192], P('segment', None, 'wide'), may hold values from -1 to 1
- w_key: bfloat16 [8, 8192, 1024], P('segment', None, 'wide'), may hold values from -1 to 1
- w_value: bfloat16 [8, 8192, 1024], P('segment', None, 'wide'), may hold values from -0.0625 to 0.0625
- w_out: bfloat16 [8, 8192, 8192], P('segment', None, 'wide'), may hold values from -0.1875 to 0.1875
- length: int32 [1], replicated, may hold values from 129 to 256
- placement: int32 [256, 1], replicated, may hold values from 0 to 63, as said below
Outputs:
- layer_out: bfloat16 [8, 256, 8192], P('segment', None, 'wide')
- kv_cache: bfloat16 [8, 512, 8, 256], P('segment', 'wide')
The draws below stay inside these ranges and needn't reach their ends.
Inputs may be any that keep to these rules, and one draw needn't show every extreme that they name: `placement`: no owner holds more than 8 pairs; some owner holds exactly 8; every owner holds at least one.
All inputs are finite; a program needn't handle non-finite values.
Results may differ from the reference program's by a relative error of at most 0.02.
Values may be sent and summed in bfloat16 or wider, within the bound.
No kernel may reach another device: no remote copies, remote signals or barrier semaphores. Data moves between devices by JAX's collectives and lax.ppermute only.
A program may use at most 64 MiB of HBM per device.

```python
import math
import jax
import jax.numpy as jnp
from jax import lax

D = 8192
HD = 128
KVH = 8
SPAN = 128
NSPAN = 2
BLOCK = 8
HQ = 64
NBLK = 32
NITEM = 256
CAP = 8
N_SEGMENT = 8
N_WIDE = 64


def drawn_weight(key, columns_total):
    return jnp.clip(jax.random.normal(key, (N_SEGMENT, D, columns_total), jnp.float32), -4.0, 4.0) * D ** (-0.5)


def draw_hidden_in(key, part):
    key = jax.random.fold_in(key, 21)
    row_total = NSPAN * SPAN
    noise = jnp.clip(jax.random.normal(key, (row_total, D), jnp.float32), -4.0, 4.0)
    return noise.astype(jnp.bfloat16)


def draw_w_query(key, part):
    key = jax.random.fold_in(key, 22)
    values = drawn_weight(key, HQ * HD)
    return values.astype(jnp.bfloat16)


def draw_w_key(key, part):
    key = jax.random.fold_in(key, 23)
    values = drawn_weight(key, KVH * HD)
    return values.astype(jnp.bfloat16)


def draw_placement(key, part):
    key = jax.random.fold_in(key, 31)
    busy_key, pool_key = jax.random.split(key)
    group_count = N_WIDE // KVH
    items = jnp.arange(NITEM, dtype=jnp.int32)
    block_id = items // KVH
    head_id = items % KVH
    member = block_id % group_count
    turn_id = block_id // group_count
    source = head_id * group_count + member
    far_owner = (source + N_WIDE // 2) % N_WIDE
    busy_owner = jax.random.randint(busy_key, (), 0, N_WIDE)
    rest_rank = items - N_WIDE
    pool_size = (N_WIDE - 1) * (CAP - 1)
    shuffled = jax.random.permutation(pool_key, pool_size)
    picked = shuffled[jnp.clip(rest_rank - (CAP - 1), 0, pool_size - 1)]
    other_owner = (busy_owner + 1 + picked // (CAP - 1)) % N_WIDE
    owner = jnp.where(turn_id == 0, far_owner, jnp.where(rest_rank < CAP - 1, busy_owner, other_owner))
    return owner[:, None].astype(jnp.int32)


def raised(entries, own_key, source, target, shards_of, factor):
    def block_of(dim):
        return (jnp.arange(entries.shape[dim]) // (entries.shape[dim] // shards_of)).reshape((-1,) + (1,) * (entries.ndim - 1 - dim))

    one_side = jax.random.permutation(own_key, shards_of)[block_of(target)]
    other_side = (block_of(target) + shards_of // 2) % shards_of
    return jnp.where((block_of(source) == one_side) | (block_of(source) == other_side), factor * entries, entries)


def block_scale(stream_key, shape, pieces, smallest, high):
    def one(position, blocks):
        heights = jax.random.uniform(jax.random.fold_in(jax.random.fold_in(stream_key, 6), position), (blocks,), jnp.float32, smallest / len(pieces), high / len(pieces))
        return jnp.repeat(jnp.exp(heights), shape[position] // blocks).reshape((-1,) + (1,) * (len(shape) - position - 1))

    level = one(*pieces[0])
    for cut in pieces[1:]:
        level = level * one(*cut)
    return level


def bell_draw(own_key, extent, spread, bound, shards=(), kind=jnp.bfloat16):
    result = jax.random.normal(own_key, extent, jnp.float32) * spread
    if len(shards) > 0:
        result = block_scale(own_key, extent, shards, -0.22, 0.18) * result
    return jnp.clip(result, min=-bound, max=bound).astype(kind)


def gaussian_with(own_key, dims, scale, most, pieces, heavy, kind=jnp.bfloat16):
    values = scale * jax.random.normal(own_key, dims, jnp.float32)
    if pieces:
        values = values * block_scale(own_key, dims, pieces, -0.22, 0.18)
    return jnp.clip(raised(values, jax.random.fold_in(own_key, 3), *heavy), -most, most).astype(kind)


def setup_inputs(seed: int = 0) -> dict:
    key_list = jax.random.split(jax.random.key(seed), 9)
    hidden_in = draw_hidden_in(jax.random.fold_in(key_list[8], 71), 0)
    gain = jnp.clip(1.0 + 0.15 * jax.random.normal(key_list[1], (N_SEGMENT, D), jnp.float32), 0.25, 1.75)
    w_query = draw_w_query(jax.random.fold_in(key_list[8], 71), 0)
    w_key = draw_w_key(jax.random.fold_in(key_list[8], 71), 0)
    w_value = bell_draw(key_list[4], (N_SEGMENT, D, KVH * HD), D ** -0.5, 0.0625, ((0, 8), (2, 64)))
    w_out = gaussian_with(key_list[5], (N_SEGMENT, HQ * HD, D), (HQ * HD) ** -0.5, 0.1875, ((0, 8), (2, 64)), (1, 2, 64, 4.0))
    length = jax.random.randint(key_list[6], (1,), SPAN + 1, 2 * SPAN + 1).astype(jnp.int32)
    placement = draw_placement(jax.random.fold_in(key_list[8], 71), 0)
    return {"hidden_in": hidden_in, "gain": gain, "w_query": w_query, "w_key": w_key, "w_value": w_value, "w_out": w_out, "length": length, "placement": placement}


epsilon = 1e-05
rope_base = 500000.0
masked_value = -1e+30

def rotate(values, angles):
    dims_in = values.shape
    paired = values.reshape(dims_in[:-1] + (dims_in[-1] // 2, 2))
    cosine = jnp.cos(angles)
    sine_part = jnp.sin(angles)
    first_half = paired[..., 0]
    second_half = paired[..., 1]
    turned = jnp.stack([first_half * cosine - second_half * sine_part, first_half * sine_part + second_half * cosine], axis=-1)
    return turned.reshape(dims_in)

def pair_freq(pair_index, head_dim):
    return jnp.power(rope_base, -2.0 * pair_index.astype(jnp.float32) / head_dim)

def reference(hidden_in, gain, w_query, w_key, w_value, w_out, length, placement):
    row_total = NSPAN * SPAN
    positions = jnp.arange(row_total, dtype=jnp.int32)
    group_size = HQ // KVH
    angles_all = positions.astype(jnp.float32)[:, None] * pair_freq(jnp.arange(HD // 2, dtype=jnp.int32), HD)[None, :]
    allowed = (positions[None, :] <= positions[:, None]) & (positions[None, :] < length[0])
    score_scale = 1.0 / math.sqrt(HD)
    owners = placement[:, 0]
    order_index = jnp.arange(NITEM, dtype=jnp.int32)
    earlier = order_index[None, :] < order_index[:, None]
    same_owner = owners[:, None] == owners[None, :]
    item_order = lax.optimization_barrier(jnp.sum((earlier & same_owner).astype(jnp.int32), axis=1))
    slot_index = (owners * CAP + item_order).astype(jnp.int32)
    hidden = hidden_in
    layer_rows = []
    cache_rows = []
    for layer in range(N_SEGMENT):
        widened = hidden.astype(jnp.float32)
        normed = (widened * lax.rsqrt(lax.optimization_barrier(jnp.mean(widened * widened, axis=-1, keepdims=True)) + epsilon) * gain[layer]).astype(jnp.bfloat16)
        query = jnp.dot(normed, w_query[layer], preferred_element_type=jnp.float32).reshape(row_total, HQ, HD)
        query = rotate(query, angles_all[:, None, :]).astype(jnp.bfloat16)
        key_rows = jnp.dot(normed, w_key[layer], preferred_element_type=jnp.float32).reshape(row_total, KVH, HD)
        key_rows = rotate(key_rows, angles_all[:, None, :]).astype(jnp.bfloat16)
        value_rows = jnp.dot(normed, w_value[layer], preferred_element_type=jnp.float32).reshape(row_total, KVH, HD).astype(jnp.bfloat16)
        key_wide = jnp.repeat(key_rows, group_size, axis=1).astype(jnp.float32)
        value_wide = jnp.repeat(value_rows, group_size, axis=1).astype(jnp.float32)
        scores = jnp.einsum('qhd,khd->hqk', query.astype(jnp.float32), key_wide) * score_scale
        scores = jnp.where(allowed[None, :, :], scores, masked_value)
        row_max = lax.optimization_barrier(jnp.max(scores, axis=-1, keepdims=True))
        weights = jnp.exp(scores - row_max)
        probabilities = (weights / lax.optimization_barrier(jnp.sum(weights, axis=-1, keepdims=True))).astype(jnp.bfloat16)
        context = jnp.einsum('hqk,khd->qhd', probabilities.astype(jnp.float32), value_wide).astype(jnp.bfloat16)
        context = context.reshape(row_total, HQ * HD)
        update = jnp.dot(context, w_out[layer], preferred_element_type=jnp.float32)
        hidden = (hidden.astype(jnp.float32) + update).astype(jnp.bfloat16)
        layer_rows.append(hidden)
        kv_rows = jnp.concatenate([key_rows, value_rows], axis=-1)
        item_rows = kv_rows.reshape(NBLK, BLOCK, KVH, 2 * HD).transpose(0, 2, 1, 3).reshape(NITEM, BLOCK, 2 * HD)
        empty_cache = jnp.zeros((N_WIDE * CAP, BLOCK, 2 * HD), jnp.bfloat16)
        cache_rows.append(empty_cache.at[slot_index].set(item_rows))
    return (jnp.stack(layer_rows), jnp.stack(cache_rows))
```

```python
import functools
import math

import jax
import jax.numpy as jnp
from jax import lax
from jax.experimental import pallas as pl
from jax.experimental.pallas import tpu as pltpu
from jax.sharding import PartitionSpec as P

HD = 128
BLOCK = 8
NY, NZ, NX, NC = 4, 2, 4, 2
NG = NY * NZ
CHIP = NC * HD
WIDE = NG * NX * NC
SECTIONS = 8
HALF = 128
EPS = 1e-05
ROPE_BASE = 500000.0
MASKED = -1e30
VMEM = 32 * 1024 * 1024

OVER_X = [[g * 8 + x * 2 + c for x in range(NX)] for g in range(NG) for c in range(NC)]
OVER_G = [[g * 8 + x * 2 + c for g in range(NG)] for x in range(NX) for c in range(NC)]
OVER_Y = [
    [(y * 2 + z) * 8 + x * 2 + c for y in range(NY)]
    for z in range(NZ)
    for x in range(NX)
    for c in range(NC)
]
CORE_SWAP = [(w, w ^ 1) for w in range(WIDE)]
CORE_UP = [(w, w + 1) for w in range(0, WIDE, 2)]


def exchange(value, groups):
    return lax.all_to_all(value, "wide", 0, 0, axis_index_groups=groups, tiled=True)


def swap_cores(value):
    return lax.ppermute(value, "wide", CORE_SWAP)


def by_core(core, own, other, axis):
    first = jnp.where(core == 0, own, other)
    second = jnp.where(core == 0, other, own)
    return jnp.concatenate([first, second], axis=axis)


def relayout(weight, core):
    rows = weight.reshape(NG, NX, CHIP, HD).transpose(1, 0, 2, 3).reshape(NX, NG * CHIP, HD)
    mine = exchange(rows, OVER_X)
    return by_core(core, mine, swap_cores(mine), 2)


def relayout_kv(w_key, w_value, core):
    both = jnp.stack([w_key.T, w_value.T])
    width = both.shape[1]
    both = both.reshape(2, width, NG, NX, CHIP).transpose(3, 0, 1, 2, 4)
    mine = exchange(both.reshape(NX, 2 * width, NG * CHIP), OVER_X)
    other = swap_cores(mine)
    mine = mine.reshape(NX, 2, 1, width, NG * CHIP)
    other = other.reshape(NX, 2, 1, width, NG * CHIP)
    full = by_core(core, mine, other, 2)
    return full.transpose(1, 0, 2, 3, 4).reshape(2 * HD, NG * CHIP)


def eye(n):
    return lax.broadcasted_iota(jnp.int32, (n, n), 0) == lax.broadcasted_iota(jnp.int32, (n, n), 1)


def project_kernel(h_ref, gain_ref, wq_ref, wkv_ref, out_ref, normed, kv, squares):
    @pl.when(pl.program_id(0) == 0)
    def _():
        total = jnp.zeros((HALF, 1), jnp.float32)
        for y in range(NY):
            part = h_ref[y].astype(jnp.float32)
            cols = slice(y * NZ * CHIP, (y + 1) * NZ * CHIP)
            normed[:, cols] = (part * gain_ref[:, cols]).astype(jnp.bfloat16)
            total = total + jnp.sum(part * part, axis=1, keepdims=True)
        row = jnp.sum(jnp.where(eye(HALF), total, 0.0), axis=0, keepdims=True)
        high = row.astype(jnp.bfloat16).astype(jnp.float32)
        upper = lax.broadcasted_iota(jnp.int32, (16, HALF), 0) < 8
        squares[...] = jnp.where(upper, high, row - high)
        kv[...] = lax.dot_general(
            normed[...], wkv_ref[...], (((1,), (1,)), ((), ())), preferred_element_type=jnp.float32
        )

    query = jnp.dot(normed[...], wq_ref[0], preferred_element_type=jnp.float32)
    out_ref[0, :HALF, :CHIP] = query.astype(jnp.bfloat16)
    out_ref[0, :HALF, CHIP:] = kv[...].astype(jnp.bfloat16)
    out_ref[0, HALF:, :] = jnp.zeros((16, 2 * CHIP), jnp.bfloat16)
    out_ref[0, HALF:, :HALF] = squares[...].astype(jnp.bfloat16)


def project(gathered, gain, wq, wkv):
    rows = NG * CHIP
    return pl.pallas_call(
        project_kernel,
        grid=(NX,),
        in_specs=[
            pl.BlockSpec((NY, HALF, NZ * CHIP), lambda i: (0, 0, 0)),
            pl.BlockSpec((1, rows), lambda i: (0, 0)),
            pl.BlockSpec((1, rows, CHIP), lambda i: (i, 0, 0)),
            pl.BlockSpec((2 * HD, rows), lambda i: (0, 0)),
        ],
        out_specs=pl.BlockSpec((1, HALF + 16, 2 * CHIP), lambda i: (i, 0, 0)),
        out_shape=jax.ShapeDtypeStruct((NX, HALF + 16, 2 * CHIP), jnp.bfloat16),
        scratch_shapes=[
            pltpu.VMEM((HALF, rows), jnp.bfloat16),
            pltpu.VMEM((HALF, CHIP), jnp.float32),
            pltpu.VMEM((16, HALF), jnp.float32),
        ],
        compiler_params=pltpu.CompilerParams(vmem_limit_bytes=VMEM),
        name="project",
    )(gathered, gain, wq, wkv)


def turn_kernel(features, part_ref, cos_ref, sin_ref, q_ref, kv_ref):
    total = jnp.zeros((HALF, 2 * CHIP), jnp.float32)
    squares = jnp.zeros((16, HALF), jnp.float32)
    for x in range(NX):
        total = total + part_ref[x, :HALF, :].astype(jnp.float32)
        squares = squares + part_ref[x, HALF:, :HALF].astype(jnp.float32)
    row = lax.rsqrt((squares[0:1] + squares[8:9]) / features + EPS)
    scale = jnp.sum(jnp.where(eye(HALF), row, 0.0), axis=1, keepdims=True)
    total = total * scale
    even = lax.broadcasted_iota(jnp.int32, (HALF, HD), 1) % 2 == 0

    def rope(part):
        swapped = jnp.where(even, pltpu.roll(part, HD - 1, 1), pltpu.roll(part, 1, 1))
        return (part * cos_ref[...] + swapped * sin_ref[...]).astype(jnp.bfloat16)

    for head in range(NC):
        cols = slice(head * HD, (head + 1) * HD)
        q_ref[:, cols] = rope(total[:, cols])
    kv_ref[:, :HD] = rope(total[:, CHIP : CHIP + HD])
    kv_ref[:, HD:] = total[:, CHIP + HD :].astype(jnp.bfloat16)


def turn(parts, cos, sin, features):
    return pl.pallas_call(
        functools.partial(turn_kernel, float(features)),
        out_shape=[jax.ShapeDtypeStruct((HALF, CHIP), jnp.bfloat16)] * 2,
        compiler_params=pltpu.CompilerParams(vmem_limit_bytes=VMEM),
        name="turn",
    )(parts, cos, sin)


def attend_kernel(info_ref, q_ref, own_ref, first_ref, out_ref):
    core = info_ref[0]
    length = info_ref[1]
    scale = 1.0 / math.sqrt(HD)
    row = lax.broadcasted_iota(jnp.int32, (HALF, HALF), 0)
    col = lax.broadcasted_iota(jnp.int32, (HALF, HALF), 1)
    seen_own = (col <= row) & (col + core * HALF < length)
    seen_first = col < jnp.where(core == 1, length, 0)
    contract = (((1,), (1,)), ((), ()))
    for head in range(NC):
        cols = slice(head * HD, (head + 1) * HD)
        query = q_ref[:, cols]
        own = lax.dot_general(query, own_ref[:, :HD], contract, preferred_element_type=jnp.float32)
        first = lax.dot_general(
            query, first_ref[:, :HD], contract, preferred_element_type=jnp.float32
        )
        own = jnp.where(seen_own, own * scale, MASKED)
        first = jnp.where(seen_first, first * scale, MASKED)
        top = jnp.maximum(
            jnp.max(own, axis=1, keepdims=True), jnp.max(first, axis=1, keepdims=True)
        )
        own = jnp.exp(own - top)
        first = jnp.exp(first - top)
        total = jnp.sum(own, axis=1, keepdims=True) + jnp.sum(first, axis=1, keepdims=True)
        own = (own / total).astype(jnp.bfloat16)
        first = (first / total).astype(jnp.bfloat16)
        context = jnp.dot(own, own_ref[:, HD:], preferred_element_type=jnp.float32)
        context += jnp.dot(first, first_ref[:, HD:], preferred_element_type=jnp.float32)
        context = context.astype(jnp.bfloat16)
        for g in range(NG):
            out_ref[g, :, cols] = context


def attend(info, query, own, first):
    vmem = pl.BlockSpec(memory_space=pltpu.VMEM)
    return pl.pallas_call(
        attend_kernel,
        in_specs=[pl.BlockSpec(memory_space=pltpu.SMEM), vmem, vmem, vmem],
        out_specs=vmem,
        out_shape=jax.ShapeDtypeStruct((NG, HALF, CHIP), jnp.bfloat16),
        compiler_params=pltpu.CompilerParams(vmem_limit_bytes=VMEM),
        name="attend",
    )(info, query, own, first)


def output_kernel(ctx_ref, w_ref, out_ref, rows):
    @pl.when(pl.program_id(0) == 0)
    def _():
        for g in range(NG):
            rows[:, g * CHIP : (g + 1) * CHIP] = ctx_ref[g]

    part = jnp.dot(rows[...], w_ref[0], preferred_element_type=jnp.float32)
    out_ref[0] = part.astype(jnp.bfloat16)


def output(context, wo):
    rows = NG * CHIP
    return pl.pallas_call(
        output_kernel,
        grid=(NX,),
        in_specs=[
            pl.BlockSpec((NG, HALF, CHIP), lambda i: (0, 0, 0)),
            pl.BlockSpec((1, rows, CHIP), lambda i: (i, 0, 0)),
        ],
        out_specs=pl.BlockSpec((1, HALF, CHIP), lambda i: (i, 0, 0)),
        out_shape=jax.ShapeDtypeStruct((NX, HALF, CHIP), jnp.bfloat16),
        scratch_shapes=[pltpu.VMEM((HALF, rows), jnp.bfloat16)],
        compiler_params=pltpu.CompilerParams(vmem_limit_bytes=VMEM),
        name="output",
    )(context, wo)


def relay_pairs(first):
    same, cross = [], []
    for s in range(first, SECTIONS - 1, 2):
        for w in range(WIDE):
            same.append((s * WIDE + w, (s + 1) * WIDE + w))
            cross.append((s * WIDE + w, (s + 1) * WIDE + (w ^ 8)))
    return same, cross


def shards(hidden_in, gain, w_query, w_key, w_value, w_out, length, placement):
    segment = lax.axis_index("segment")
    wide = lax.axis_index("wide")
    core = wide % 2
    z = wide // 8 % 2
    x = wide // 2 % NX
    features = gain.shape[1]

    halves = hidden_in.reshape(2, HALF, HD)
    kept = lax.dynamic_index_in_dim(halves, core, 0, keepdims=False)
    given = lax.dynamic_index_in_dim(halves, 1 - core, 0, keepdims=False)
    start = by_core(core, kept, swap_cores(given), 1)

    wq = relayout(w_query[0], core)
    wkv = relayout_kv(w_key[0], w_value[0], core)
    wo = relayout(w_out[0], core)
    gain_x = lax.dynamic_index_in_dim(gain.reshape(NG, NX, CHIP), x, 1, keepdims=False)
    gain_x = gain_x.reshape(1, NG * CHIP)

    lane = jnp.arange(HD, dtype=jnp.int32)
    freq = jnp.power(ROPE_BASE, -2.0 * (lane // 2).astype(jnp.float32) / HD)
    position = (core * HALF + jnp.arange(HALF, dtype=jnp.int32)).astype(jnp.float32)
    angle = position[:, None] * freq[None, :]
    cos = jnp.cos(angle)
    sin = jnp.where(lane[None, :] % 2 == 0, -1.0, 1.0) * jnp.sin(angle)
    info = jnp.stack([core.astype(jnp.int32), length[0]])

    def first_gather(value):
        sent = jnp.broadcast_to(value[None], (NG, HALF, CHIP))
        got = exchange(sent, OVER_G).reshape(NY, NZ, HALF, CHIP)
        return got.transpose(0, 2, 1, 3).reshape(NY, HALF, NZ * CHIP)

    def later_gather(same, cross):
        pair = jnp.concatenate(
            [jnp.where(z == 0, same, cross), jnp.where(z == 0, cross, same)], axis=1
        )
        return exchange(jnp.broadcast_to(pair[None], (NY, HALF, NZ * CHIP)), OVER_Y)

    def layer(own, gathered):
        parts = exchange(project(gathered, gain_x, wq, wkv), OVER_X)
        query, kv = turn(parts, cos, sin, features)
        first = lax.ppermute(kv, "wide", CORE_UP)
        context = exchange(attend(info, query, kv, first), OVER_G)
        parts = exchange(output(context, wo), OVER_X).astype(jnp.float32)
        result = own.astype(jnp.float32) + (parts[0] + parts[1] + parts[2] + parts[3])
        return result.astype(jnp.bfloat16), kv

    def send(pairs):
        same, cross = pairs

        def run(value):
            axes = ("segment", "wide")
            return lax.ppermute(value, axes, same), lax.ppermute(value, axes, cross)

        return run

    even, odd = send(relay_pairs(0)), send(relay_pairs(1))

    def tick(t, state):
        own, gathered, kv = state
        own, kv = lax.cond(
            segment == t, layer, lambda own, gathered: (own, kv), own, gathered
        )

        def hand_on(own, gathered):
            same, cross = lax.cond(t % 2 == 0, even, odd, own)
            return lax.cond(
                segment == t + 1,
                lambda: (same, later_gather(same, cross)),
                lambda: (own, gathered),
            )

        own, gathered = lax.cond(
            ((segment == t) | (segment == t + 1)) & (t < SECTIONS - 1),
            hand_on,
            lambda own, gathered: (own, gathered),
            own,
            gathered,
        )
        return own, gathered, kv

    gathered = lax.cond(
        segment == 0,
        first_gather,
        lambda value: jnp.zeros((NY, HALF, NZ * CHIP), jnp.bfloat16),
        start,
    )
    kv = jnp.zeros((HALF, CHIP), jnp.bfloat16)
    own, gathered, kv = lax.fori_loop(0, SECTIONS, tick, (start, gathered, kv))

    columns = own.reshape(HALF, NC, HD)
    kept = lax.dynamic_index_in_dim(columns, core, 1, keepdims=False)
    given = lax.dynamic_index_in_dim(columns, 1 - core, 1, keepdims=False)
    outputs = by_core(core, kept, swap_cores(given), 0)

    owners = placement[:, 0]
    items = owners.shape[0]
    order = jnp.arange(items, dtype=jnp.int32)
    earlier = (order[None, :] < order[:, None]) & (owners[:, None] == owners[None, :])
    rank = jnp.sum(earlier.astype(jnp.int32), axis=1)
    slots = 2 * items // WIDE
    blocks = HALF // BLOCK
    by_head = (jnp.arange(2 * blocks)[None, :] * NG + jnp.arange(NG)[:, None]).astype(jnp.int32)
    mine = lax.dynamic_slice_in_dim(by_head, core * blocks, blocks, 1).reshape(-1)
    match = mine[:, None] == order[None, :]
    item_owner = jnp.sum(jnp.where(match, owners[None, :], 0), axis=1)
    item_rank = jnp.sum(jnp.where(match, rank[None, :], 0), axis=1)
    slot = jnp.arange(slots, dtype=jnp.int32)

    sent = jnp.broadcast_to(kv[None], (NG, HALF, CHIP))
    rows = exchange(sent, OVER_G).reshape(NG * blocks, BLOCK * CHIP)

    def chosen(owner):
        wanted = (item_owner[None, :] == owner) & (item_rank[None, :] == slot[:, None])
        return jnp.dot(wanted.astype(jnp.bfloat16), rows, preferred_element_type=jnp.float32)

    here = chosen(wide)
    there = chosen(wide ^ 1).astype(jnp.bfloat16)
    cache = (here + swap_cores(there).astype(jnp.float32)).astype(jnp.bfloat16)
    return outputs[None], cache.reshape(1, slots, BLOCK, CHIP)


def solution(mesh):
    in_specs = (
        P(None, "wide"),
        P("segment", None),
        P("segment", None, "wide"),
        P("segment", None, "wide"),
        P("segment", None, "wide"),
        P("segment", None, "wide"),
        P(),
        P(),
    )
    out_specs = (P("segment", None, "wide"), P("segment", "wide", None, None))
    return jax.shard_map(shards, mesh=mesh, in_specs=in_specs, out_specs=out_specs, check_vma=False)
```

```python
import functools
import math

import jax
import jax.numpy as jnp
from jax import lax
from jax.experimental import pallas as pl
from jax.experimental.pallas import tpu as pltpu
from jax.sharding import PartitionSpec as P

HD = 128
BLOCK = 8
NY, NZ, NX, NC = 4, 2, 4, 2
NG = NY * NZ
CHIP = NC * HD
WIDE = NG * NX * NC
SECTIONS = 8
HALF = 128
EPS = 1e-05
ROPE_BASE = 500000.0
MASKED = -1e30
VMEM = 32 * 1024 * 1024

OVER_X = [[g * 8 + x * 2 + c for x in range(NX)] for g in range(NG) for c in range(NC)]
OVER_G = [[g * 8 + x * 2 + c for g in range(NG)] for x in range(NX) for c in range(NC)]
OVER_Y = [
    [(y * 2 + z) * 8 + x * 2 + c for y in range(NY)]
    for z in range(NZ)
    for x in range(NX)
    for c in range(NC)
]
Z_SWAP = [(w, w ^ 8) for w in range(WIDE)]
CORE_SWAP = [(w, w ^ 1) for w in range(WIDE)]
CORE_UP = [(w, w + 1) for w in range(0, WIDE, 2)]


def exchange(value, groups):
    return lax.all_to_all(value, "wide", 0, 0, axis_index_groups=groups, tiled=True)


def swap_cores(value):
    return lax.ppermute(value, "wide", CORE_SWAP)


def by_core(core, own, other, axis):
    first = jnp.where(core == 0, own, other)
    second = jnp.where(core == 0, other, own)
    return jnp.concatenate([first, second], axis=axis)


def relayout(weight):
    rows = weight.reshape(NG, NX, CHIP, HD).transpose(1, 0, 2, 3).reshape(NX, NG * CHIP, HD)
    mine = exchange(rows, OVER_X)
    return mine, swap_cores(mine)


def relayout_out(kept, given):
    near = exchange(kept, OVER_Y)
    far = exchange(lax.ppermute(given, "wide", Z_SWAP), OVER_Y)
    return near, swap_cores(near), far, swap_cores(far)


def relayout_kv(w_key, w_value, core):
    both = jnp.stack([w_key.T, w_value.T])
    width = both.shape[1]
    both = both.reshape(2, width, NG, NX, CHIP).transpose(3, 0, 1, 2, 4)
    mine = exchange(both.reshape(NX, 2 * width, NG * CHIP), OVER_X)
    other = swap_cores(mine)
    mine = mine.reshape(NX, 2, 1, width, NG * CHIP)
    other = other.reshape(NX, 2, 1, width, NG * CHIP)
    full = by_core(core, mine, other, 2)
    return full.transpose(1, 0, 2, 3, 4).reshape(2 * HD, NG * CHIP)


def eye(n):
    return lax.broadcasted_iota(jnp.int32, (n, n), 0) == lax.broadcasted_iota(jnp.int32, (n, n), 1)


def aligned(block, size=1):
    return pl.ds(pl.multiple_of(block * HD, HD), size * HD)


def project_kernel(
    info_ref, h_ref, gain_ref, own_ref, other_ref, wkv_ref, out_ref, normed, kv, squares
):
    @pl.when(pl.program_id(0) == 0)
    def _():
        total = jnp.zeros((HALF, 1), jnp.float32)
        for y in range(NY):
            part = h_ref[y].astype(jnp.float32)
            cols = slice(y * NZ * CHIP, (y + 1) * NZ * CHIP)
            normed[:, cols] = (part * gain_ref[:, cols]).astype(jnp.bfloat16)
            total = total + jnp.sum(part * part, axis=1, keepdims=True)
        row = jnp.sum(jnp.where(eye(HALF), total, 0.0), axis=0, keepdims=True)
        high = row.astype(jnp.bfloat16).astype(jnp.float32)
        upper = lax.broadcasted_iota(jnp.int32, (16, HALF), 0) < 8
        squares[...] = jnp.where(upper, high, row - high)
        kv[...] = lax.dot_general(
            normed[...], wkv_ref[...], (((1,), (1,)), ((), ())), preferred_element_type=jnp.float32
        )

    weight = jnp.concatenate([own_ref[0], other_ref[0]], axis=1)
    query = jnp.dot(normed[...], weight, preferred_element_type=jnp.float32).astype(jnp.bfloat16)
    core = info_ref[0]
    out_ref[0, :HALF, aligned(core)] = query[:, :HD]
    out_ref[0, :HALF, aligned(1 - core)] = query[:, HD:]
    out_ref[0, :HALF, CHIP:] = kv[...].astype(jnp.bfloat16)
    out_ref[0, HALF:, :] = jnp.zeros((16, 2 * CHIP), jnp.bfloat16)
    out_ref[0, HALF:, :HALF] = squares[...].astype(jnp.bfloat16)


def project(info, gathered, gain, wq, wkv):
    rows = NG * CHIP
    block = pl.BlockSpec((1, rows, HD), lambda i: (i, 0, 0))
    return pl.pallas_call(
        project_kernel,
        grid=(NX,),
        in_specs=[
            pl.BlockSpec(memory_space=pltpu.SMEM),
            pl.BlockSpec((NY, HALF, NZ * CHIP), lambda i: (0, 0, 0)),
            pl.BlockSpec((1, rows), lambda i: (0, 0)),
            block,
            block,
            pl.BlockSpec((2 * HD, rows), lambda i: (0, 0)),
        ],
        out_specs=pl.BlockSpec((1, HALF + 16, 2 * CHIP), lambda i: (i, 0, 0)),
        out_shape=jax.ShapeDtypeStruct((NX, HALF + 16, 2 * CHIP), jnp.bfloat16),
        scratch_shapes=[
            pltpu.VMEM((HALF, rows), jnp.bfloat16),
            pltpu.VMEM((HALF, CHIP), jnp.float32),
            pltpu.VMEM((16, HALF), jnp.float32),
        ],
        compiler_params=pltpu.CompilerParams(vmem_limit_bytes=VMEM),
        name="project",
    )(info, gathered, gain, *wq, wkv)


def turn_kernel(features, part_ref, cos_ref, sin_ref, q_ref, kv_ref):
    total = jnp.zeros((HALF, 2 * CHIP), jnp.float32)
    squares = jnp.zeros((16, HALF), jnp.float32)
    for x in range(NX):
        total = total + part_ref[x, :HALF, :].astype(jnp.float32)
        squares = squares + part_ref[x, HALF:, :HALF].astype(jnp.float32)
    row = lax.rsqrt((squares[0:1] + squares[8:9]) / features + EPS)
    scale = jnp.sum(jnp.where(eye(HALF), row, 0.0), axis=1, keepdims=True)
    total = total * scale
    even = lax.broadcasted_iota(jnp.int32, (HALF, HD), 1) % 2 == 0

    def rope(part):
        swapped = jnp.where(even, pltpu.roll(part, HD - 1, 1), pltpu.roll(part, 1, 1))
        return (part * cos_ref[...] + swapped * sin_ref[...]).astype(jnp.bfloat16)

    for head in range(NC):
        cols = slice(head * HD, (head + 1) * HD)
        q_ref[:, cols] = rope(total[:, cols])
    kv_ref[:, :HD] = rope(total[:, CHIP : CHIP + HD])
    kv_ref[:, HD:] = total[:, CHIP + HD :].astype(jnp.bfloat16)


def turn(parts, cos, sin, features):
    return pl.pallas_call(
        functools.partial(turn_kernel, float(features)),
        out_shape=[jax.ShapeDtypeStruct((HALF, CHIP), jnp.bfloat16)] * 2,
        compiler_params=pltpu.CompilerParams(vmem_limit_bytes=VMEM),
        name="turn",
    )(parts, cos, sin)


def attend_kernel(info_ref, q_ref, own_ref, first_ref, out_ref):
    core = info_ref[0]
    length = info_ref[1]
    scale = 1.0 / math.sqrt(HD)
    row = lax.broadcasted_iota(jnp.int32, (HALF, HALF), 0)
    col = lax.broadcasted_iota(jnp.int32, (HALF, HALF), 1)
    seen_own = (col <= row) & (col + core * HALF < length)
    seen_first = col < jnp.where(core == 1, length, 0)
    contract = (((1,), (1,)), ((), ()))
    for head in range(NC):
        cols = slice(head * HD, (head + 1) * HD)
        query = q_ref[:, cols]
        own = lax.dot_general(query, own_ref[:, :HD], contract, preferred_element_type=jnp.float32)
        first = lax.dot_general(
            query, first_ref[:, :HD], contract, preferred_element_type=jnp.float32
        )
        own = jnp.where(seen_own, own * scale, MASKED)
        first = jnp.where(seen_first, first * scale, MASKED)
        top = jnp.maximum(
            jnp.max(own, axis=1, keepdims=True), jnp.max(first, axis=1, keepdims=True)
        )
        own = jnp.exp(own - top)
        first = jnp.exp(first - top)
        total = jnp.sum(own, axis=1, keepdims=True) + jnp.sum(first, axis=1, keepdims=True)
        own = (own / total).astype(jnp.bfloat16)
        first = (first / total).astype(jnp.bfloat16)
        context = jnp.dot(own, own_ref[:, HD:], preferred_element_type=jnp.float32)
        context += jnp.dot(first, first_ref[:, HD:], preferred_element_type=jnp.float32)
        context = context.astype(jnp.bfloat16)
        for x in range(NX):
            out_ref[x, :, cols] = context


def attend(info, query, own, first):
    vmem = pl.BlockSpec(memory_space=pltpu.VMEM)
    return pl.pallas_call(
        attend_kernel,
        in_specs=[pl.BlockSpec(memory_space=pltpu.SMEM), vmem, vmem, vmem],
        out_specs=vmem,
        out_shape=jax.ShapeDtypeStruct((NX, HALF, CHIP), jnp.bfloat16),
        compiler_params=pltpu.CompilerParams(vmem_limit_bytes=VMEM),
        name="attend",
    )(info, query, own, first)


def output_kernel(info_ref, ctx_ref, near_ref, near_other, far_ref, far_other, out_ref, rows):
    @pl.when(pl.program_id(0) == 0)
    def _():
        for x in range(NX):
            rows[:, x * CHIP : (x + 1) * CHIP] = ctx_ref[x]

    core, z = info_ref[0], info_ref[2]
    for half, pair in ((z, (near_ref, near_other)), (1 - z, (far_ref, far_other))):
        weight = jnp.concatenate([pair[0][0], pair[1][0]], axis=1)
        part = jnp.dot(rows[...], weight, preferred_element_type=jnp.float32).astype(jnp.bfloat16)
        out_ref[0, :, aligned(half * NC + core)] = part[:, :HD]
        out_ref[0, :, aligned(half * NC + 1 - core)] = part[:, HD:]


def output(info, context, wo):
    rows = NX * CHIP
    block = pl.BlockSpec((1, rows, HD), lambda i: (i, 0, 0))
    return pl.pallas_call(
        output_kernel,
        grid=(NY,),
        in_specs=[
            pl.BlockSpec(memory_space=pltpu.SMEM),
            pl.BlockSpec((NX, HALF, CHIP), lambda i: (0, 0, 0)),
            block,
            block,
            block,
            block,
        ],
        out_specs=pl.BlockSpec((1, HALF, NZ * CHIP), lambda i: (i, 0, 0)),
        out_shape=jax.ShapeDtypeStruct((NY, HALF, NZ * CHIP), jnp.bfloat16),
        scratch_shapes=[pltpu.VMEM((HALF, rows), jnp.bfloat16)],
        compiler_params=pltpu.CompilerParams(vmem_limit_bytes=VMEM),
        name="output",
    )(info, context, *wo)


def relay_pairs(first):
    same, cross = [], []
    for s in range(first, SECTIONS - 1, 2):
        for w in range(WIDE):
            same.append((s * WIDE + w, (s + 1) * WIDE + w))
            cross.append((s * WIDE + w, (s + 1) * WIDE + (w ^ 8)))
    return same, cross


def shards(hidden_in, gain, w_query, w_key, w_value, w_out, length, placement):
    segment = lax.axis_index("segment")
    wide = lax.axis_index("wide")
    core = wide % 2
    z = wide // 8 % 2
    x = wide // 2 % NX
    y = wide // 16
    features = gain.shape[1]

    halves = hidden_in.reshape(2, HALF, HD)
    kept = lax.dynamic_index_in_dim(halves, core, 0, keepdims=False)
    given = lax.dynamic_index_in_dim(halves, 1 - core, 0, keepdims=False)
    start = by_core(core, kept, swap_cores(given), 1)

    gain_x = lax.dynamic_index_in_dim(gain.reshape(NG, NX, CHIP), x, 1, keepdims=False)
    gain_x = gain_x.reshape(1, NG * CHIP)

    lane = jnp.arange(HD, dtype=jnp.int32)
    freq = jnp.power(ROPE_BASE, -2.0 * (lane // 2).astype(jnp.float32) / HD)
    position = (core * HALF + jnp.arange(HALF, dtype=jnp.int32)).astype(jnp.float32)
    angle = position[:, None] * freq[None, :]
    cos = jnp.cos(angle)
    sin = jnp.where(lane[None, :] % 2 == 0, -1.0, 1.0) * jnp.sin(angle)
    info = jnp.stack([core, length[0], z]).astype(jnp.int32)

    def first_gather(value):
        sent = jnp.broadcast_to(value[None], (NG, HALF, CHIP))
        got = exchange(sent, OVER_G).reshape(NY, NZ, HALF, CHIP)
        return got.transpose(0, 2, 1, 3).reshape(NY, HALF, NZ * CHIP)

    out_rows = w_out[0].reshape(NY, NZ, NX * CHIP, HD)
    kept = lax.dynamic_index_in_dim(out_rows, z, 1, keepdims=False)
    given = lax.dynamic_index_in_dim(out_rows, 1 - z, 1, keepdims=False)

    def first_section(start, kept, given):
        wq = relayout(w_query[0])
        wkv = relayout_kv(w_key[0], w_value[0], core)
        return first_gather(start), wq, wkv, relayout_out(kept, given)

    def later_section(start, kept, given):
        wq = relayout(w_query[0])
        wkv = relayout_kv(w_key[0], w_value[0], core)
        given, wq, wkv = lax.optimization_barrier((given, wq, wkv))
        blank = jnp.zeros((NY, HALF, NZ * CHIP), jnp.bfloat16)
        return blank, wq, wkv, relayout_out(kept, given)

    gathered, wq, wkv, wo = lax.cond(
        segment == 0, first_section, later_section, start, kept, given
    )

    def later_gather(same, cross):
        pair = (same.astype(jnp.float32) + cross.astype(jnp.float32)).astype(jnp.bfloat16)
        return exchange(jnp.broadcast_to(pair[None], (NY, HALF, NZ * CHIP)), OVER_Y)

    def layer(gathered):
        parts = exchange(project(info, gathered, gain_x, wq, wkv), OVER_X)
        query, kv = turn(parts, cos, sin, features)
        first = lax.ppermute(kv, "wide", CORE_UP)
        context = exchange(attend(info, query, kv, first), OVER_X)
        parts = exchange(output(info, context, wo), OVER_Y).astype(jnp.float32)
        own = lax.dynamic_index_in_dim(gathered, y, 0, keepdims=False).astype(jnp.float32)
        total = parts[0] + parts[1] + parts[2] + parts[3]
        return (jnp.where(z == 0, own, 0.0) + total).astype(jnp.bfloat16), kv

    def send(pairs):
        same, cross = pairs

        def run(value):
            axes = ("segment", "wide")
            return lax.ppermute(value, axes, same), lax.ppermute(value, axes, cross)

        return run

    even, odd = send(relay_pairs(0)), send(relay_pairs(1))

    def tick(t, state):
        gathered, partial, kv = state
        partial, kv = lax.cond(segment == t, layer, lambda gathered: (partial, kv), gathered)

        def hand_on(partial, gathered):
            same, cross = lax.cond(t % 2 == 0, even, odd, partial)
            return lax.cond(
                segment == t + 1, later_gather, lambda same, cross: gathered, same, cross
            )

        gathered = lax.cond(
            ((segment == t) | (segment == t + 1)) & (t < SECTIONS - 1),
            hand_on,
            lambda partial, gathered: gathered,
            partial,
            gathered,
        )
        return gathered, partial, kv

    partial = jnp.zeros((HALF, NZ * CHIP), jnp.bfloat16)
    kv = jnp.zeros((HALF, CHIP), jnp.bfloat16)
    _, partial, kv = lax.fori_loop(0, SECTIONS, tick, (gathered, partial, kv))

    pair = partial.reshape(HALF, NZ, CHIP)
    kept = lax.dynamic_index_in_dim(pair, z, 1, keepdims=False)
    given = lax.dynamic_index_in_dim(pair, 1 - z, 1, keepdims=False)
    other = lax.ppermute(given, "wide", Z_SWAP)
    own = (kept.astype(jnp.float32) + other.astype(jnp.float32)).astype(jnp.bfloat16)
    columns = own.reshape(HALF, NC, HD)
    kept = lax.dynamic_index_in_dim(columns, core, 1, keepdims=False)
    given = lax.dynamic_index_in_dim(columns, 1 - core, 1, keepdims=False)
    outputs = by_core(core, kept, swap_cores(given), 0)

    owners = placement[:, 0]
    items = owners.shape[0]
    order = jnp.arange(items, dtype=jnp.int32)
    earlier = (order[None, :] < order[:, None]) & (owners[:, None] == owners[None, :])
    rank = jnp.sum(earlier.astype(jnp.int32), axis=1)
    slots = 2 * items // WIDE
    blocks = HALF // BLOCK
    by_head = (jnp.arange(2 * blocks)[None, :] * NG + jnp.arange(NG)[:, None]).astype(jnp.int32)
    mine = lax.dynamic_slice_in_dim(by_head, core * blocks, blocks, 1).reshape(-1)
    match = mine[:, None] == order[None, :]
    item_owner = jnp.sum(jnp.where(match, owners[None, :], 0), axis=1)
    item_rank = jnp.sum(jnp.where(match, rank[None, :], 0), axis=1)
    slot = jnp.arange(slots, dtype=jnp.int32)

    sent = jnp.broadcast_to(kv[None], (NG, HALF, CHIP))
    rows = exchange(sent, OVER_G).reshape(NG * blocks, BLOCK * CHIP)

    def chosen(owner):
        wanted = (item_owner[None, :] == owner) & (item_rank[None, :] == slot[:, None])
        return jnp.dot(wanted.astype(jnp.bfloat16), rows, preferred_element_type=jnp.float32)

    here = chosen(wide)
    there = chosen(wide ^ 1).astype(jnp.bfloat16)
    cache = (here + swap_cores(there).astype(jnp.float32)).astype(jnp.bfloat16)
    return outputs[None], cache.reshape(1, slots, BLOCK, CHIP)


def solution(mesh):
    in_specs = (
        P(None, "wide"),
        P("segment", None),
        P("segment", None, "wide"),
        P("segment", None, "wide"),
        P("segment", None, "wide"),
        P("segment", None, "wide"),
        P(),
        P(),
    )
    out_specs = (P("segment", None, "wide"), P("segment", "wide", None, None))
    return jax.shard_map(shards, mesh=mesh, in_specs=in_specs, out_specs=out_specs, check_vma=False)
```

```python
import functools
import math

import jax
import jax.numpy as jnp
from jax import lax
from jax.experimental import pallas as pl
from jax.experimental.pallas import tpu as pltpu
from jax.sharding import PartitionSpec as P

HD = 128
BLOCK = 8
NY, NZ, NX, NC = 4, 2, 4, 2
NG = NY * NZ
CHIP = NC * HD
WIDE = NG * NX * NC
SECTIONS = 8
HALF = 128
ITEMS_HERE = NG * HALF // BLOCK
EPS = 1e-05
ROPE_BASE = 500000.0
MASKED = -1e30
VMEM = 16 * 1024 * 1024

OVER_X = [[g * 8 + x * 2 + c for x in range(NX)] for g in range(NG) for c in range(NC)]
OVER_G = [[g * 8 + x * 2 + c for g in range(NG)] for x in range(NX) for c in range(NC)]
OVER_Y = [
    [(y * 2 + z) * 8 + x * 2 + c for y in range(NY)]
    for z in range(NZ)
    for x in range(NX)
    for c in range(NC)
]
Z_SWAP = [(w, w ^ 8) for w in range(WIDE)]
CORE_SWAP = [(w, w ^ 1) for w in range(WIDE)]
CORE_UP = [(w, w + 1) for w in range(0, WIDE, 2)]


def exchange(value, groups):
    return lax.all_to_all(value, "wide", 0, 0, axis_index_groups=groups, tiled=True)


def swap_cores(value):
    return lax.ppermute(value, "wide", CORE_SWAP)


def by_core(core, own, other, axis):
    first = jnp.where(core == 0, own, other)
    second = jnp.where(core == 0, other, own)
    return jnp.concatenate([first, second], axis=axis)


def x_blocks(weight):
    return weight.reshape(NG, NX, CHIP, HD).transpose(1, 0, 2, 3).reshape(NX, NG * CHIP, HD)


def over_y(piece, y):
    full = None
    for step in range(NY):
        block = piece((y + step) % NY)
        if step == 0:
            full = jnp.zeros((NY,) + block.shape[1:], block.dtype)
        else:
            pairs = [(w, (w + 16 * step) % WIDE) for w in range(WIDE)]
            block = lax.ppermute(block, "wide", pairs)
        full = lax.dynamic_update_slice_in_dim(full, block, (y - step) % NY, 0)
    return full


def relayout_kv(w_key, w_value, core, after):
    both = jnp.stack([w_key.T, w_value.T])
    width = both.shape[1]
    both = both.reshape(2, width, NG, NX, CHIP).transpose(3, 0, 1, 2, 4)
    mine = exchange(after(both.reshape(NX, 2 * width, NG * CHIP)), OVER_X)
    other = swap_cores(mine)
    mine = mine.reshape(NX, 2, 1, width, NG * CHIP)
    other = other.reshape(NX, 2, 1, width, NG * CHIP)
    full = by_core(core, mine, other, 2)
    return full.transpose(1, 0, 2, 3, 4).reshape(2 * HD, NG * CHIP)


def eye(n):
    return lax.broadcasted_iota(jnp.int32, (n, n), 0) == lax.broadcasted_iota(jnp.int32, (n, n), 1)


def aligned(block, size=1):
    return pl.ds(pl.multiple_of(block * HD, HD), size * HD)


def project_kernel(
    info_ref, h_ref, gain_ref, own_ref, other_ref, wkv_ref, out_ref, normed, kv, squares
):
    @pl.when(pl.program_id(0) == 0)
    def _():
        total = jnp.zeros((HALF, 1), jnp.float32)
        for y in range(NY):
            part = h_ref[y].astype(jnp.float32)
            cols = slice(y * NZ * CHIP, (y + 1) * NZ * CHIP)
            normed[:, cols] = (part * gain_ref[:, cols]).astype(jnp.bfloat16)
            total = total + jnp.sum(part * part, axis=1, keepdims=True)
        row = jnp.sum(jnp.where(eye(HALF), total, 0.0), axis=0, keepdims=True)
        high = row.astype(jnp.bfloat16).astype(jnp.float32)
        upper = lax.broadcasted_iota(jnp.int32, (16, HALF), 0) < 8
        squares[...] = jnp.where(upper, high, row - high)
        kv[...] = lax.dot_general(
            normed[...], wkv_ref[...], (((1,), (1,)), ((), ())), preferred_element_type=jnp.float32
        )

    weight = jnp.concatenate([own_ref[0], other_ref[0]], axis=1)
    query = jnp.dot(normed[...], weight, preferred_element_type=jnp.float32).astype(jnp.bfloat16)
    core = info_ref[0]
    out_ref[0, :HALF, aligned(core)] = query[:, :HD]
    out_ref[0, :HALF, aligned(1 - core)] = query[:, HD:]
    out_ref[0, :HALF, CHIP:] = kv[...].astype(jnp.bfloat16)
    out_ref[0, HALF:, :] = jnp.zeros((16, 2 * CHIP), jnp.bfloat16)
    out_ref[0, HALF:, :HALF] = squares[...].astype(jnp.bfloat16)


def project(info, gathered, gain, wq, wkv):
    rows = NG * CHIP
    block = pl.BlockSpec((1, rows, HD), lambda i: (i, 0, 0))
    return pl.pallas_call(
        project_kernel,
        grid=(NX,),
        in_specs=[
            pl.BlockSpec(memory_space=pltpu.SMEM),
            pl.BlockSpec((NY, HALF, NZ * CHIP), lambda i: (0, 0, 0)),
            pl.BlockSpec((1, rows), lambda i: (0, 0)),
            block,
            block,
            pl.BlockSpec((2 * HD, rows), lambda i: (0, 0)),
        ],
        out_specs=pl.BlockSpec((1, HALF + 16, 2 * CHIP), lambda i: (i, 0, 0)),
        out_shape=jax.ShapeDtypeStruct((NX, HALF + 16, 2 * CHIP), jnp.bfloat16),
        scratch_shapes=[
            pltpu.VMEM((HALF, rows), jnp.bfloat16),
            pltpu.VMEM((HALF, CHIP), jnp.float32),
            pltpu.VMEM((16, HALF), jnp.float32),
        ],
        compiler_params=pltpu.CompilerParams(vmem_limit_bytes=VMEM),
        name="project",
    )(info, gathered, gain, *wq, wkv)


def turn_kernel(features, part_ref, cos_ref, sin_ref, q_ref, kv_ref):
    total = jnp.zeros((HALF, 2 * CHIP), jnp.float32)
    squares = jnp.zeros((16, HALF), jnp.float32)
    for x in range(NX):
        total = total + part_ref[x, :HALF, :].astype(jnp.float32)
        squares = squares + part_ref[x, HALF:, :HALF].astype(jnp.float32)
    row = lax.rsqrt((squares[0:1] + squares[8:9]) / features + EPS)
    scale = jnp.sum(jnp.where(eye(HALF), row, 0.0), axis=1, keepdims=True)
    total = total * scale
    even = lax.broadcasted_iota(jnp.int32, (HALF, HD), 1) % 2 == 0

    def rope(part):
        swapped = jnp.where(even, pltpu.roll(part, HD - 1, 1), pltpu.roll(part, 1, 1))
        return (part * cos_ref[...] + swapped * sin_ref[...]).astype(jnp.bfloat16)

    for head in range(NC):
        cols = slice(head * HD, (head + 1) * HD)
        q_ref[:, cols] = rope(total[:, cols])
    kv_ref[:, :HD] = rope(total[:, CHIP : CHIP + HD])
    kv_ref[:, HD:] = total[:, CHIP + HD :].astype(jnp.bfloat16)


def turn(parts, cos, sin, features):
    return pl.pallas_call(
        functools.partial(turn_kernel, float(features)),
        out_shape=[jax.ShapeDtypeStruct((HALF, CHIP), jnp.bfloat16)] * 2,
        compiler_params=pltpu.CompilerParams(vmem_limit_bytes=VMEM),
        name="turn",
    )(parts, cos, sin)


def attend_kernel(info_ref, q_ref, own_ref, first_ref, out_ref):
    core = info_ref[0]
    length = info_ref[1]
    scale = 1.0 / math.sqrt(HD)
    row = lax.broadcasted_iota(jnp.int32, (HALF, HALF), 0)
    col = lax.broadcasted_iota(jnp.int32, (HALF, HALF), 1)
    seen_own = (col <= row) & (col + core * HALF < length)
    seen_first = col < jnp.where(core == 1, length, 0)
    contract = (((1,), (1,)), ((), ()))
    for head in range(NC):
        cols = slice(head * HD, (head + 1) * HD)
        query = q_ref[:, cols]
        own = lax.dot_general(query, own_ref[:, :HD], contract, preferred_element_type=jnp.float32)
        first = lax.dot_general(
            query, first_ref[:, :HD], contract, preferred_element_type=jnp.float32
        )
        own = jnp.where(seen_own, own * scale, MASKED)
        first = jnp.where(seen_first, first * scale, MASKED)
        top = jnp.maximum(
            jnp.max(own, axis=1, keepdims=True), jnp.max(first, axis=1, keepdims=True)
        )
        own = jnp.exp(own - top)
        first = jnp.exp(first - top)
        total = jnp.sum(own, axis=1, keepdims=True) + jnp.sum(first, axis=1, keepdims=True)
        own = (own / total).astype(jnp.bfloat16)
        first = (first / total).astype(jnp.bfloat16)
        context = jnp.dot(own, own_ref[:, HD:], preferred_element_type=jnp.float32)
        context += jnp.dot(first, first_ref[:, HD:], preferred_element_type=jnp.float32)
        context = context.astype(jnp.bfloat16)
        for x in range(NX):
            out_ref[x, :, cols] = context


def attend(info, query, own, first):
    vmem = pl.BlockSpec(memory_space=pltpu.VMEM)
    return pl.pallas_call(
        attend_kernel,
        in_specs=[pl.BlockSpec(memory_space=pltpu.SMEM), vmem, vmem, vmem],
        out_specs=vmem,
        out_shape=jax.ShapeDtypeStruct((NX, HALF, CHIP), jnp.bfloat16),
        compiler_params=pltpu.CompilerParams(vmem_limit_bytes=VMEM),
        name="attend",
    )(info, query, own, first)


def output_kernel(info_ref, ctx_ref, near_ref, near_other, far_ref, far_other, out_ref, rows):
    @pl.when(pl.program_id(0) == 0)
    def _():
        for x in range(NX):
            rows[:, x * CHIP : (x + 1) * CHIP] = ctx_ref[x]

    core, z = info_ref[0], info_ref[2]
    for half, pair in ((z, (near_ref, near_other)), (1 - z, (far_ref, far_other))):
        weight = jnp.concatenate([pair[0][0], pair[1][0]], axis=1)
        part = jnp.dot(rows[...], weight, preferred_element_type=jnp.float32).astype(jnp.bfloat16)
        out_ref[0, :, aligned(half * NC + core)] = part[:, :HD]
        out_ref[0, :, aligned(half * NC + 1 - core)] = part[:, HD:]


def output(info, context, wo):
    rows = NX * CHIP
    block = pl.BlockSpec((1, rows, HD), lambda i: (i, 0, 0))
    return pl.pallas_call(
        output_kernel,
        grid=(NY,),
        in_specs=[
            pl.BlockSpec(memory_space=pltpu.SMEM),
            pl.BlockSpec((NX, HALF, CHIP), lambda i: (0, 0, 0)),
            block,
            block,
            block,
            block,
        ],
        out_specs=pl.BlockSpec((1, HALF, NZ * CHIP), lambda i: (i, 0, 0)),
        out_shape=jax.ShapeDtypeStruct((NY, HALF, NZ * CHIP), jnp.bfloat16),
        scratch_shapes=[pltpu.VMEM((HALF, rows), jnp.bfloat16)],
        compiler_params=pltpu.CompilerParams(vmem_limit_bytes=VMEM),
        name="output",
    )(info, context, *wo)


def ranks(placement, core):
    owners = placement[:, 0]
    order = jnp.arange(owners.shape[0], dtype=jnp.int32)
    earlier = (order[None, :] < order[:, None]) & (owners[:, None] == owners[None, :])
    rank = jnp.sum(earlier.astype(jnp.int32), axis=1)
    blocks = HALF // BLOCK
    here = jnp.arange(ITEMS_HERE, dtype=jnp.int32)
    mine = (core * blocks + here % blocks) * NG + here // blocks
    match = mine[:, None] == order[None, :]
    item_owner = jnp.sum(jnp.where(match, owners[None, :], 0), axis=1)
    item_rank = jnp.sum(jnp.where(match, rank[None, :], 0), axis=1)
    return item_owner, item_rank


def relay_pairs(first):
    same, cross = [], []
    for s in range(first, SECTIONS - 1, 2):
        for w in range(WIDE):
            same.append((s * WIDE + w, (s + 1) * WIDE + w))
            cross.append((s * WIDE + w, (s + 1) * WIDE + (w ^ 8)))
    return same, cross


def shards(hidden_in, gain, w_query, w_key, w_value, w_out, length, placement):
    segment = lax.axis_index("segment")
    wide = lax.axis_index("wide")
    core = wide % 2
    z = wide // 8 % 2
    x = wide // 2 % NX
    y = wide // 16
    features = gain.shape[1]

    halves = hidden_in.reshape(2, HALF, HD)
    kept = lax.dynamic_index_in_dim(halves, core, 0, keepdims=False)
    given = lax.dynamic_index_in_dim(halves, 1 - core, 0, keepdims=False)
    start = by_core(core, kept, swap_cores(given), 1)

    gain_x = lax.dynamic_index_in_dim(gain.reshape(NG, NX, CHIP), x, 1, keepdims=False)
    gain_x = gain_x.reshape(1, NG * CHIP)

    lane = jnp.arange(HD, dtype=jnp.int32)
    freq = jnp.power(ROPE_BASE, -2.0 * (lane // 2).astype(jnp.float32) / HD)
    position = (core * HALF + jnp.arange(HALF, dtype=jnp.int32)).astype(jnp.float32)
    angle = position[:, None] * freq[None, :]
    cos = jnp.cos(angle)
    sin = jnp.where(lane[None, :] % 2 == 0, -1.0, 1.0) * jnp.sin(angle)
    info = jnp.stack([core, length[0], z]).astype(jnp.int32)

    def first_gather(value):
        sent = jnp.broadcast_to(value[None], (NG, HALF, CHIP))
        got = exchange(sent, OVER_G).reshape(NY, NZ, HALF, CHIP)
        return got.transpose(0, 2, 1, 3).reshape(NY, HALF, NZ * CHIP)

    out_rows = w_out[0].reshape(NY, NZ, NX * CHIP, HD)
    given = lax.dynamic_index_in_dim(out_rows, 1 - z, 1, keepdims=False)

    def kept(i):
        block = lax.dynamic_slice(out_rows, (i, z, 0, 0), (1, 1, NX * CHIP, HD))
        return block.reshape(1, NX * CHIP, HD)

    def prepare(given, before):
        rows = lax.optimization_barrier((x_blocks(w_query[0]), before))[0]
        query = exchange(rows, OVER_X)
        key_value = relayout_kv(
            w_key[0],
            w_value[0],
            core,
            lambda both: lax.optimization_barrier((both, query))[0],
        )
        near = over_y(kept, y)
        far = given(key_value)
        far = over_y(lambda i: lax.dynamic_slice_in_dim(far, i, 1, 0), y)
        out = (near, swap_cores(near), far, swap_cores(far))
        return (query, swap_cores(query)), key_value, out

    def first_section(start):
        far = lax.ppermute(given, "wide", Z_SWAP)
        gathered = first_gather(start)
        items = jnp.zeros((ITEMS_HERE,), jnp.int32)
        return gathered, prepare(lambda key_value: far, gathered), (items, items)

    def later_section(start):
        def far(key_value):
            return lax.ppermute(
                lax.optimization_barrier((given, key_value))[0], "wide", Z_SWAP
            )

        blank = jnp.zeros((NY, HALF, NZ * CHIP), jnp.bfloat16)
        return blank, prepare(far, start), ranks(placement, core)

    gathered, (wq, wkv, wo), items = lax.cond(segment == 0, first_section, later_section, start)

    def later_gather(same, cross):
        pair = (same.astype(jnp.float32) + cross.astype(jnp.float32)).astype(jnp.bfloat16)
        return exchange(jnp.broadcast_to(pair[None], (NY, HALF, NZ * CHIP)), OVER_Y)

    def layer(gathered):
        parts = exchange(project(info, gathered, gain_x, wq, wkv), OVER_X)
        query, kv = turn(parts, cos, sin, features)
        first = lax.ppermute(kv, "wide", CORE_UP)
        context = exchange(attend(info, query, kv, first), OVER_X)
        parts = exchange(output(info, context, wo), OVER_Y).astype(jnp.float32)
        own = lax.dynamic_index_in_dim(gathered, y, 0, keepdims=False).astype(jnp.float32)
        total = parts[0] + parts[1] + parts[2] + parts[3]
        return (jnp.where(z == 0, own, 0.0) + total).astype(jnp.bfloat16), kv

    def send(pairs):
        same, cross = pairs

        def run(value):
            axes = ("segment", "wide")
            return lax.ppermute(value, axes, cross), lax.ppermute(value, axes, same)

        return run

    even, odd = send(relay_pairs(0)), send(relay_pairs(1))

    def tick(t, state):
        gathered, partial, kv = state
        partial, kv = lax.cond(segment == t, layer, lambda gathered: (partial, kv), gathered)

        def hand_on(partial, gathered):
            cross, same = lax.cond(t % 2 == 0, even, odd, partial)
            return lax.cond(
                segment == t + 1, later_gather, lambda same, cross: gathered, same, cross
            )

        gathered = lax.cond(
            ((segment == t) | (segment == t + 1)) & (t < SECTIONS - 1),
            hand_on,
            lambda partial, gathered: gathered,
            partial,
            gathered,
        )
        return gathered, partial, kv

    partial = jnp.zeros((HALF, NZ * CHIP), jnp.bfloat16)
    kv = jnp.zeros((HALF, CHIP), jnp.bfloat16)
    _, partial, kv = lax.fori_loop(0, SECTIONS, tick, (gathered, partial, kv))

    pair = partial.reshape(HALF, NZ, CHIP)
    kept = lax.dynamic_index_in_dim(pair, z, 1, keepdims=False)
    given = lax.dynamic_index_in_dim(pair, 1 - z, 1, keepdims=False)
    other = lax.ppermute(given, "wide", Z_SWAP)
    own = (kept.astype(jnp.float32) + other.astype(jnp.float32)).astype(jnp.bfloat16)
    columns = own.reshape(HALF, NC, HD)
    kept = lax.dynamic_index_in_dim(columns, core, 1, keepdims=False)
    given = lax.dynamic_index_in_dim(columns, 1 - core, 1, keepdims=False)
    outputs = by_core(core, kept, swap_cores(given), 0)

    item_owner, item_rank = lax.cond(
        segment == 0, lambda: ranks(placement, core), lambda: items
    )
    blocks = HALF // BLOCK
    slots = 2 * placement.shape[0] // WIDE
    slot = jnp.arange(slots, dtype=jnp.int32)

    sent = jnp.broadcast_to(kv[None], (NG, HALF, CHIP))
    rows = exchange(sent, OVER_G).reshape(NG * blocks, BLOCK * CHIP)

    def chosen(owner):
        wanted = (item_owner[None, :] == owner) & (item_rank[None, :] == slot[:, None])
        return jnp.dot(wanted.astype(jnp.bfloat16), rows, preferred_element_type=jnp.float32)

    here = chosen(wide)
    there = chosen(wide ^ 1).astype(jnp.bfloat16)
    cache = (here + swap_cores(there).astype(jnp.float32)).astype(jnp.bfloat16)
    return outputs[None], cache.reshape(1, slots, BLOCK, CHIP)


def solution(mesh):
    in_specs = (
        P(None, "wide"),
        P("segment", None),
        P("segment", None, "wide"),
        P("segment", None, "wide"),
        P("segment", None, "wide"),
        P("segment", None, "wide"),
        P(),
        P(),
    )
    out_specs = (P("segment", None, "wide"), P("segment", "wide", None, None))
    return jax.shard_map(shards, mesh=mesh, in_specs=in_specs, out_specs=out_specs, check_vma=False)
```

```python
import functools
import math

import jax
import jax.numpy as jnp
from jax import lax
from jax.experimental import pallas as pl
from jax.experimental.pallas import tpu as pltpu
from jax.sharding import PartitionSpec as P

HD = 128
BLOCK = 8
NY, NZ, NX, NC = 4, 2, 4, 2
NG = NY * NZ
CHIP = NC * HD
WIDE = NG * NX * NC
SECTIONS = 8
HALF = 128
ITEMS_HERE = NG * HALF // BLOCK
EPS = 1e-05
ROPE_BASE = 500000.0
MASKED = -1e30
VMEM = 16 * 1024 * 1024

OVER_X = [[g * 8 + x * 2 + c for x in range(NX)] for g in range(NG) for c in range(NC)]
OVER_XZ = [
    [y * 16 + m * 2 + c for m in range(NZ * NX)] for y in range(NY) for c in range(NC)
]
OVER_G = [[g * 8 + x * 2 + c for g in range(NG)] for x in range(NX) for c in range(NC)]
OVER_Y = [
    [(y * 2 + z) * 8 + x * 2 + c for y in range(NY)]
    for z in range(NZ)
    for x in range(NX)
    for c in range(NC)
]
Z_SWAP = [(w, w ^ 8) for w in range(WIDE)]
LAST_TO_FIRST = [((SECTIONS - 1) * WIDE + w, w ^ 8) for w in range(WIDE)]
CORE_SWAP = [(w, w ^ 1) for w in range(WIDE)]
CORE_UP = [(w, w + 1) for w in range(0, WIDE, 2)]


def exchange(value, groups):
    return lax.all_to_all(value, "wide", 0, 0, axis_index_groups=groups, tiled=True)


def swap_cores(value):
    return lax.ppermute(value, "wide", CORE_SWAP)


def by_core(core, own, other, axis):
    first = jnp.where(core == 0, own, other)
    second = jnp.where(core == 0, other, own)
    return jnp.concatenate([first, second], axis=axis)


def x_blocks(weight):
    return weight.reshape(NG, NX, CHIP, HD).transpose(1, 0, 2, 3).reshape(NX, NG * CHIP, HD)


def relayout_kv(w_key, w_value, core, after):
    both = jnp.stack([w_key.T, w_value.T])
    width = both.shape[1]
    both = both.reshape(2, width, NG, NX, CHIP).transpose(3, 0, 1, 2, 4)
    mine = exchange(after(both.reshape(NX, 2 * width, NG * CHIP)), OVER_X)
    other = swap_cores(mine)
    mine = mine.reshape(NX, 2, 1, width, NG * CHIP)
    other = other.reshape(NX, 2, 1, width, NG * CHIP)
    full = by_core(core, mine, other, 2)
    return full.transpose(1, 0, 2, 3, 4).reshape(2 * HD, NG * CHIP)


def eye(n):
    return lax.broadcasted_iota(jnp.int32, (n, n), 0) == lax.broadcasted_iota(jnp.int32, (n, n), 1)


def aligned(block, size=1):
    return pl.ds(pl.multiple_of(block * HD, HD), size * HD)


def project_kernel(
    info_ref, h_ref, gain_ref, own_ref, other_ref, wkv_ref, out_ref, normed, kv, squares
):
    @pl.when(pl.program_id(0) == 0)
    def _():
        total = jnp.zeros((HALF, 1), jnp.float32)
        for y in range(NY):
            part = h_ref[y].astype(jnp.float32)
            cols = slice(y * NZ * CHIP, (y + 1) * NZ * CHIP)
            normed[:, cols] = (part * gain_ref[:, cols]).astype(jnp.bfloat16)
            total = total + jnp.sum(part * part, axis=1, keepdims=True)
        row = jnp.sum(jnp.where(eye(HALF), total, 0.0), axis=0, keepdims=True)
        high = row.astype(jnp.bfloat16).astype(jnp.float32)
        upper = lax.broadcasted_iota(jnp.int32, (16, HALF), 0) < 8
        squares[...] = jnp.where(upper, high, row - high)
        kv[...] = lax.dot_general(
            normed[...], wkv_ref[...], (((1,), (1,)), ((), ())), preferred_element_type=jnp.float32
        )

    weight = jnp.concatenate([own_ref[0], other_ref[0]], axis=1)
    query = jnp.dot(normed[...], weight, preferred_element_type=jnp.float32).astype(jnp.bfloat16)
    core = info_ref[0]
    out_ref[0, :HALF, aligned(core)] = query[:, :HD]
    out_ref[0, :HALF, aligned(1 - core)] = query[:, HD:]
    out_ref[0, :HALF, CHIP:] = kv[...].astype(jnp.bfloat16)
    out_ref[0, HALF:, :] = jnp.zeros((16, 2 * CHIP), jnp.bfloat16)
    out_ref[0, HALF:, :HALF] = squares[...].astype(jnp.bfloat16)


def project(info, gathered, gain, wq, wkv):
    rows = NG * CHIP
    block = pl.BlockSpec((1, rows, HD), lambda i: (i, 0, 0))
    return pl.pallas_call(
        project_kernel,
        grid=(NX,),
        in_specs=[
            pl.BlockSpec(memory_space=pltpu.SMEM),
            pl.BlockSpec((NY, HALF, NZ * CHIP), lambda i: (0, 0, 0)),
            pl.BlockSpec((1, rows), lambda i: (0, 0)),
            block,
            block,
            pl.BlockSpec((2 * HD, rows), lambda i: (0, 0)),
        ],
        out_specs=pl.BlockSpec((1, HALF + 16, 2 * CHIP), lambda i: (i, 0, 0)),
        out_shape=jax.ShapeDtypeStruct((NX, HALF + 16, 2 * CHIP), jnp.bfloat16),
        scratch_shapes=[
            pltpu.VMEM((HALF, rows), jnp.bfloat16),
            pltpu.VMEM((HALF, CHIP), jnp.float32),
            pltpu.VMEM((16, HALF), jnp.float32),
        ],
        compiler_params=pltpu.CompilerParams(vmem_limit_bytes=VMEM),
        name="project",
    )(info, gathered, gain, *wq, wkv)


def turn_kernel(features, part_ref, cos_ref, sin_ref, q_ref, kv_ref):
    total = jnp.zeros((HALF, 2 * CHIP), jnp.float32)
    squares = jnp.zeros((16, HALF), jnp.float32)
    for x in range(NX):
        total = total + part_ref[x, :HALF, :].astype(jnp.float32)
        squares = squares + part_ref[x, HALF:, :HALF].astype(jnp.float32)
    row = lax.rsqrt((squares[0:1] + squares[8:9]) / features + EPS)
    scale = jnp.sum(jnp.where(eye(HALF), row, 0.0), axis=1, keepdims=True)
    total = total * scale
    even = lax.broadcasted_iota(jnp.int32, (HALF, HD), 1) % 2 == 0

    def rope(part):
        swapped = jnp.where(even, pltpu.roll(part, HD - 1, 1), pltpu.roll(part, 1, 1))
        return (part * cos_ref[...] + swapped * sin_ref[...]).astype(jnp.bfloat16)

    for head in range(NC):
        cols = slice(head * HD, (head + 1) * HD)
        q_ref[:, cols] = rope(total[:, cols])
    kv_ref[:, :HD] = rope(total[:, CHIP : CHIP + HD])
    kv_ref[:, HD:] = total[:, CHIP + HD :].astype(jnp.bfloat16)


def turn(parts, cos, sin, features):
    return pl.pallas_call(
        functools.partial(turn_kernel, float(features)),
        out_shape=[jax.ShapeDtypeStruct((HALF, CHIP), jnp.bfloat16)] * 2,
        compiler_params=pltpu.CompilerParams(vmem_limit_bytes=VMEM),
        name="turn",
    )(parts, cos, sin)


def attend_kernel(info_ref, q_ref, own_ref, first_ref, out_ref):
    core = info_ref[0]
    length = info_ref[1]
    scale = 1.0 / math.sqrt(HD)
    row = lax.broadcasted_iota(jnp.int32, (HALF, HALF), 0)
    col = lax.broadcasted_iota(jnp.int32, (HALF, HALF), 1)
    seen_own = (col <= row) & (col + core * HALF < length)
    seen_first = col < jnp.where(core == 1, length, 0)
    contract = (((1,), (1,)), ((), ()))
    for head in range(NC):
        cols = slice(head * HD, (head + 1) * HD)
        query = q_ref[:, cols]
        own = lax.dot_general(query, own_ref[:, :HD], contract, preferred_element_type=jnp.float32)
        first = lax.dot_general(
            query, first_ref[:, :HD], contract, preferred_element_type=jnp.float32
        )
        own = jnp.where(seen_own, own * scale, MASKED)
        first = jnp.where(seen_first, first * scale, MASKED)
        top = jnp.maximum(
            jnp.max(own, axis=1, keepdims=True), jnp.max(first, axis=1, keepdims=True)
        )
        own = jnp.exp(own - top)
        first = jnp.exp(first - top)
        total = jnp.sum(own, axis=1, keepdims=True) + jnp.sum(first, axis=1, keepdims=True)
        own = (own / total).astype(jnp.bfloat16)
        first = (first / total).astype(jnp.bfloat16)
        context = jnp.dot(own, own_ref[:, HD:], preferred_element_type=jnp.float32)
        context += jnp.dot(first, first_ref[:, HD:], preferred_element_type=jnp.float32)
        context = context.astype(jnp.bfloat16)
        for x in range(NX):
            out_ref[x, :, cols] = context


def attend(info, query, own, first):
    vmem = pl.BlockSpec(memory_space=pltpu.VMEM)
    return pl.pallas_call(
        attend_kernel,
        in_specs=[pl.BlockSpec(memory_space=pltpu.SMEM), vmem, vmem, vmem],
        out_specs=vmem,
        out_shape=jax.ShapeDtypeStruct((NX, HALF, CHIP), jnp.bfloat16),
        compiler_params=pltpu.CompilerParams(vmem_limit_bytes=VMEM),
        name="attend",
    )(info, query, own, first)


def output_kernel(halves, info_ref, ctx_ref, own_ref, other_ref, out_ref, rows):
    depth = rows.shape[1]

    @pl.when(pl.program_id(0) == 0)
    def _():
        for i in range(depth // CHIP):
            rows[:, i * CHIP : (i + 1) * CHIP] = ctx_ref[i]

    core, z = info_ref[0], info_ref[2]
    for part in range(halves):
        cut = slice(part * depth, (part + 1) * depth)
        weight = jnp.concatenate([own_ref[0, cut], other_ref[0, cut]], axis=1)
        total = jnp.dot(rows[...], weight, preferred_element_type=jnp.float32)
        total = total.astype(jnp.bfloat16)
        first = (z if part == 0 else 1 - z) * NC if halves > 1 else 0
        out_ref[0, :, aligned(first + core)] = total[:, :HD]
        out_ref[0, :, aligned(first + 1 - core)] = total[:, HD:]


def output(info, context, wo):
    count = context.shape[0]
    halves = NG // count
    rows = NG * CHIP
    block = pl.BlockSpec((1, rows, HD), lambda i: (i, 0, 0))
    return pl.pallas_call(
        functools.partial(output_kernel, halves),
        grid=(NY,),
        in_specs=[
            pl.BlockSpec(memory_space=pltpu.SMEM),
            pl.BlockSpec((count, HALF, CHIP), lambda i: (0, 0, 0)),
            block,
            block,
        ],
        out_specs=pl.BlockSpec((1, HALF, halves * CHIP), lambda i: (i, 0, 0)),
        out_shape=jax.ShapeDtypeStruct((NY, HALF, halves * CHIP), jnp.bfloat16),
        scratch_shapes=[pltpu.VMEM((HALF, count * CHIP), jnp.bfloat16)],
        compiler_params=pltpu.CompilerParams(vmem_limit_bytes=VMEM),
        name="output",
    )(info, context, *wo)


def ranks(placement, core):
    owners = placement[:, 0]
    order = jnp.arange(owners.shape[0], dtype=jnp.int32)
    earlier = (order[None, :] < order[:, None]) & (owners[:, None] == owners[None, :])
    rank = jnp.sum(earlier.astype(jnp.int32), axis=1)
    blocks = HALF // BLOCK
    here = jnp.arange(ITEMS_HERE, dtype=jnp.int32)
    mine = (core * blocks + here % blocks) * NG + here // blocks
    match = mine[:, None] == order[None, :]
    item_owner = jnp.sum(jnp.where(match, owners[None, :], 0), axis=1)
    item_rank = jnp.sum(jnp.where(match, rank[None, :], 0), axis=1)
    return item_owner, item_rank


def relay_pairs(first):
    same, cross = [], []
    for s in range(first, SECTIONS - 1, 2):
        for w in range(WIDE):
            same.append((s * WIDE + w, (s + 1) * WIDE + w))
            cross.append((s * WIDE + w, (s + 1) * WIDE + (w ^ 8)))
    return same, cross


def shards(hidden_in, gain, w_query, w_key, w_value, w_out, length, placement):
    segment = lax.axis_index("segment")
    wide = lax.axis_index("wide")
    core = wide % 2
    z = wide // 8 % 2
    x = wide // 2 % NX
    y = wide // 16
    features = gain.shape[1]

    halves = hidden_in.reshape(2, HALF, HD)
    kept = lax.dynamic_index_in_dim(halves, core, 0, keepdims=False)
    given = lax.dynamic_index_in_dim(halves, 1 - core, 0, keepdims=False)
    start = by_core(core, kept, swap_cores(given), 1)

    gain_x = lax.dynamic_index_in_dim(gain.reshape(NG, NX, CHIP), x, 1, keepdims=False)
    gain_x = gain_x.reshape(1, NG * CHIP)

    lane = jnp.arange(HD, dtype=jnp.int32)
    freq = jnp.power(ROPE_BASE, -2.0 * (lane // 2).astype(jnp.float32) / HD)
    position = (core * HALF + jnp.arange(HALF, dtype=jnp.int32)).astype(jnp.float32)
    angle = position[:, None] * freq[None, :]
    cos = jnp.cos(angle)
    sin = jnp.where(lane[None, :] % 2 == 0, -1.0, 1.0) * jnp.sin(angle)
    info = jnp.stack([core, length[0], z]).astype(jnp.int32)

    def gather(pair):
        return exchange(jnp.broadcast_to(pair[None], (NY, HALF, NZ * CHIP)), OVER_Y)

    cross = lax.ppermute(start, ("segment", "wide"), LAST_TO_FIRST)
    raw = w_out[0].reshape(NY, NZ * NX * CHIP, HD)

    def prepare(before, out_rows):
        rows = lax.optimization_barrier((x_blocks(w_query[0]), before))[0]
        query = exchange(rows, OVER_X)
        key_value = relayout_kv(
            w_key[0],
            w_value[0],
            core,
            lambda both: lax.optimization_barrier((both, query))[0],
        )
        out = exchange(lax.optimization_barrier((out_rows, key_value))[0], OVER_Y)
        return (query, swap_cores(query)), key_value, (out, swap_cores(out))

    def first_section(start, cross):
        pair = jnp.where(
            z == 0,
            jnp.concatenate([start, cross], axis=1),
            jnp.concatenate([cross, start], axis=1),
        )
        gathered = gather(pair)
        items = jnp.zeros((ITEMS_HERE,), jnp.int32)
        return gathered, prepare(gathered, raw), (items, items)

    def later_section(start, cross):
        halves = raw.reshape(NY, NZ, NX * CHIP, HD)
        kept = lax.dynamic_index_in_dim(halves, z, 1, keepdims=False)
        given = lax.dynamic_index_in_dim(halves, 1 - z, 1, keepdims=False)
        far = lax.ppermute(given, "wide", Z_SWAP)
        out_rows = jnp.concatenate([kept, far], axis=1)
        blank = jnp.zeros((NY, HALF, NZ * CHIP), jnp.bfloat16)
        return blank, prepare(far, out_rows), ranks(placement, core)

    gathered, (wq, wkv, wo), items = lax.cond(
        segment == 0, first_section, later_section, start, cross
    )

    def later_gather(same, cross):
        return gather((same.astype(jnp.float32) + cross.astype(jnp.float32)).astype(jnp.bfloat16))

    def summed(parts, own):
        parts = parts.astype(jnp.float32)
        return own.astype(jnp.float32) + (parts[0] + parts[1] + parts[2] + parts[3])

    def whole_out(context, own):
        context = jnp.broadcast_to(context[:1], (NG, HALF, CHIP))
        parts = exchange(output(info, exchange(context, OVER_XZ), wo), OVER_Y)
        own = jnp.where(z == 0, own[:, :CHIP], own[:, CHIP:])
        result = summed(parts, own).astype(jnp.bfloat16)
        zero = jnp.zeros_like(result)
        return jnp.concatenate(
            [jnp.where(z == 0, result, zero), jnp.where(z == 0, zero, result)], axis=1
        )

    def half_out(context, own):
        parts = exchange(output(info, exchange(context, OVER_X), wo), OVER_Y)
        return summed(parts, jnp.where(z == 0, own, jnp.zeros_like(own))).astype(jnp.bfloat16)

    def layer(gathered):
        parts = exchange(project(info, gathered, gain_x, wq, wkv), OVER_X)
        query, kv = turn(parts, cos, sin, features)
        first = lax.ppermute(kv, "wide", CORE_UP)
        context = attend(info, query, kv, first)
        own = lax.dynamic_index_in_dim(gathered, y, 0, keepdims=False)
        return lax.cond(segment == 0, whole_out, half_out, context, own), kv

    def send(pairs):
        same, cross = pairs

        def run(value):
            axes = ("segment", "wide")
            return lax.ppermute(value, axes, cross), lax.ppermute(value, axes, same)

        return run

    even, odd = send(relay_pairs(0)), send(relay_pairs(1))

    def tick(t, state):
        gathered, partial, kv = state
        partial, kv = lax.cond(segment == t, layer, lambda gathered: (partial, kv), gathered)

        def hand_on(partial, gathered):
            cross, same = lax.cond(t % 2 == 0, even, odd, partial)
            return lax.cond(
                segment == t + 1, later_gather, lambda same, cross: gathered, same, cross
            )

        gathered = lax.cond(
            ((segment == t) | (segment == t + 1)) & (t < SECTIONS - 1),
            hand_on,
            lambda partial, gathered: gathered,
            partial,
            gathered,
        )
        return gathered, partial, kv

    partial = jnp.zeros((HALF, NZ * CHIP), jnp.bfloat16)
    kv = jnp.zeros((HALF, CHIP), jnp.bfloat16)
    _, partial, kv = lax.fori_loop(0, SECTIONS, tick, (gathered, partial, kv))

    pair = partial.reshape(HALF, NZ, CHIP)
    kept = lax.dynamic_index_in_dim(pair, z, 1, keepdims=False)
    given = lax.dynamic_index_in_dim(pair, 1 - z, 1, keepdims=False)
    other = lax.ppermute(given, "wide", Z_SWAP)
    own = (kept.astype(jnp.float32) + other.astype(jnp.float32)).astype(jnp.bfloat16)
    columns = own.reshape(HALF, NC, HD)
    kept = lax.dynamic_index_in_dim(columns, core, 1, keepdims=False)
    given = lax.dynamic_index_in_dim(columns, 1 - core, 1, keepdims=False)
    outputs = by_core(core, kept, swap_cores(given), 0)

    item_owner, item_rank = lax.cond(
        segment == 0, lambda: ranks(placement, core), lambda: items
    )
    blocks = HALF // BLOCK
    slots = 2 * placement.shape[0] // WIDE
    slot = jnp.arange(slots, dtype=jnp.int32)

    sent = jnp.broadcast_to(kv[None], (NG, HALF, CHIP))
    rows = exchange(sent, OVER_G).reshape(NG * blocks, BLOCK * CHIP)

    def chosen(owner):
        wanted = (item_owner[None, :] == owner) & (item_rank[None, :] == slot[:, None])
        return jnp.dot(wanted.astype(jnp.bfloat16), rows, preferred_element_type=jnp.float32)

    here = chosen(wide)
    there = chosen(wide ^ 1).astype(jnp.bfloat16)
    cache = (here + swap_cores(there).astype(jnp.float32)).astype(jnp.bfloat16)
    return outputs[None], cache.reshape(1, slots, BLOCK, CHIP)


def solution(mesh):
    in_specs = (
        P(None, "wide"),
        P("segment", None),
        P("segment", None, "wide"),
        P("segment", None, "wide"),
        P("segment", None, "wide"),
        P("segment", None, "wide"),
        P(),
        P(),
    )
    out_specs = (P("segment", None, "wide"), P("segment", "wide", None, None))
    return jax.shard_map(shards, mesh=mesh, in_specs=in_specs, out_specs=out_specs, check_vma=False)
```

```python
import functools
import math

import jax
import jax.numpy as jnp
from jax import lax
from jax.experimental import pallas as pl
from jax.experimental.pallas import tpu as pltpu
from jax.sharding import PartitionSpec as P

HD = 128
BLOCK = 8
NY, NZ, NX, NC = 4, 2, 4, 2
NG = NY * NZ
CHIP = NC * HD
WIDE = NG * NX * NC
SECTIONS = 8
HALF = 128
ITEMS_HERE = NG * HALF // BLOCK
EPS = 1e-05
ROPE_BASE = 500000.0
MASKED = -1e30
VMEM = 16 * 1024 * 1024

OVER_X = [[g * 8 + x * 2 + c for x in range(NX)] for g in range(NG) for c in range(NC)]
OVER_XZ = [
    [y * 16 + m * 2 + c for m in range(NZ * NX)] for y in range(NY) for c in range(NC)
]
OVER_G = [[g * 8 + x * 2 + c for g in range(NG)] for x in range(NX) for c in range(NC)]
OVER_Y = [
    [(y * 2 + z) * 8 + x * 2 + c for y in range(NY)]
    for z in range(NZ)
    for x in range(NX)
    for c in range(NC)
]
Z_SWAP = [(w, w ^ 8) for w in range(WIDE)]
CORE_SWAP = [(w, w ^ 1) for w in range(WIDE)]
CORE_UP = [(w, w + 1) for w in range(0, WIDE, 2)]


def exchange(value, groups):
    return lax.all_to_all(value, "wide", 0, 0, axis_index_groups=groups, tiled=True)


def swap_cores(value):
    return lax.ppermute(value, "wide", CORE_SWAP)


def by_core(core, own, other, axis):
    first = jnp.where(core == 0, own, other)
    second = jnp.where(core == 0, other, own)
    return jnp.concatenate([first, second], axis=axis)


def x_blocks(weight):
    return weight.reshape(NG, NX, CHIP, HD).transpose(1, 0, 2, 3).reshape(NX, NG * CHIP, HD)


def moved(w, stride, step):
    at = w // stride % 4
    return w + ((at + step) % 4 - at) * stride


def from_ring(piece, at, stride):
    blocks = [piece(at)]
    for step in range(1, 4):
        pairs = [(w, moved(w, stride, step)) for w in range(WIDE)]
        blocks.append(lax.ppermute(piece((at + step) % 4), "wide", pairs))
    return jnp.concatenate(blocks, axis=0)


def in_order(blocks, at):
    return jnp.concatenate(
        [lax.dynamic_slice_in_dim(blocks, (at + 4 - i) % 4, 1, 0) for i in range(4)], axis=0
    )


def relayout_kv(w_key, w_value, core, x):
    both = jnp.stack([w_key.T, w_value.T])
    width = both.shape[1]
    both = both.reshape(2, width, NG, NX, CHIP).transpose(3, 0, 1, 2, 4)
    both = both.reshape(NX, 2 * width, NG * CHIP)
    mine = from_ring(lambda i: lax.dynamic_slice_in_dim(both, i, 1, 0), x, NC)
    other = in_order(swap_cores(mine), x).reshape(NX, 2, 1, width, NG * CHIP)
    mine = in_order(mine, x).reshape(NX, 2, 1, width, NG * CHIP)
    full = by_core(core, mine, other, 2)
    return full.transpose(1, 0, 2, 3, 4).reshape(2 * HD, NG * CHIP)


def eye(n):
    return lax.broadcasted_iota(jnp.int32, (n, n), 0) == lax.broadcasted_iota(jnp.int32, (n, n), 1)


def aligned(block, size=1):
    return pl.ds(pl.multiple_of(block * HD, HD), size * HD)


def project_kernel(
    info_ref, h_ref, gain_ref, own_ref, other_ref, wkv_ref, out_ref, normed, kv, squares
):
    @pl.when(pl.program_id(0) == 0)
    def _():
        total = jnp.zeros((HALF, 1), jnp.float32)
        for y in range(NY):
            part = h_ref[y].astype(jnp.float32)
            cols = slice(y * NZ * CHIP, (y + 1) * NZ * CHIP)
            normed[:, cols] = (part * gain_ref[:, cols]).astype(jnp.bfloat16)
            total = total + jnp.sum(part * part, axis=1, keepdims=True)
        row = jnp.sum(jnp.where(eye(HALF), total, 0.0), axis=0, keepdims=True)
        high = row.astype(jnp.bfloat16).astype(jnp.float32)
        upper = lax.broadcasted_iota(jnp.int32, (16, HALF), 0) < 8
        squares[...] = jnp.where(upper, high, row - high)
        kv[...] = lax.dot_general(
            normed[...], wkv_ref[...], (((1,), (1,)), ((), ())), preferred_element_type=jnp.float32
        )

    weight = jnp.concatenate([own_ref[0], other_ref[0]], axis=1)
    query = jnp.dot(normed[...], weight, preferred_element_type=jnp.float32).astype(jnp.bfloat16)
    core = info_ref[0]
    out_ref[0, :HALF, aligned(core)] = query[:, :HD]
    out_ref[0, :HALF, aligned(1 - core)] = query[:, HD:]
    out_ref[0, :HALF, CHIP:] = kv[...].astype(jnp.bfloat16)
    out_ref[0, HALF:, :] = jnp.zeros((16, 2 * CHIP), jnp.bfloat16)
    out_ref[0, HALF:, :HALF] = squares[...].astype(jnp.bfloat16)


def project(info, gathered, gain, wq, wkv):
    rows = NG * CHIP
    block = pl.BlockSpec((1, rows, HD), lambda i: (i, 0, 0))
    return pl.pallas_call(
        project_kernel,
        grid=(NX,),
        in_specs=[
            pl.BlockSpec(memory_space=pltpu.SMEM),
            pl.BlockSpec((NY, HALF, NZ * CHIP), lambda i: (0, 0, 0)),
            pl.BlockSpec((1, rows), lambda i: (0, 0)),
            block,
            block,
            pl.BlockSpec((2 * HD, rows), lambda i: (0, 0)),
        ],
        out_specs=pl.BlockSpec((1, HALF + 16, 2 * CHIP), lambda i: (i, 0, 0)),
        out_shape=jax.ShapeDtypeStruct((NX, HALF + 16, 2 * CHIP), jnp.bfloat16),
        scratch_shapes=[
            pltpu.VMEM((HALF, rows), jnp.bfloat16),
            pltpu.VMEM((HALF, CHIP), jnp.float32),
            pltpu.VMEM((16, HALF), jnp.float32),
        ],
        compiler_params=pltpu.CompilerParams(vmem_limit_bytes=VMEM),
        name="project",
    )(info, gathered, gain, *wq, wkv)


def turn_kernel(features, part_ref, cos_ref, sin_ref, q_ref, kv_ref):
    total = jnp.zeros((HALF, 2 * CHIP), jnp.float32)
    squares = jnp.zeros((16, HALF), jnp.float32)
    for x in range(NX):
        total = total + part_ref[x, :HALF, :].astype(jnp.float32)
        squares = squares + part_ref[x, HALF:, :HALF].astype(jnp.float32)
    row = lax.rsqrt((squares[0:1] + squares[8:9]) / features + EPS)
    scale = jnp.sum(jnp.where(eye(HALF), row, 0.0), axis=1, keepdims=True)
    total = total * scale
    even = lax.broadcasted_iota(jnp.int32, (HALF, HD), 1) % 2 == 0

    def rope(part):
        swapped = jnp.where(even, pltpu.roll(part, HD - 1, 1), pltpu.roll(part, 1, 1))
        return (part * cos_ref[...] + swapped * sin_ref[...]).astype(jnp.bfloat16)

    for head in range(NC):
        cols = slice(head * HD, (head + 1) * HD)
        q_ref[:, cols] = rope(total[:, cols])
    kv_ref[:, :HD] = rope(total[:, CHIP : CHIP + HD])
    kv_ref[:, HD:] = total[:, CHIP + HD :].astype(jnp.bfloat16)


def turn(parts, cos, sin, features):
    return pl.pallas_call(
        functools.partial(turn_kernel, float(features)),
        out_shape=[jax.ShapeDtypeStruct((HALF, CHIP), jnp.bfloat16)] * 2,
        compiler_params=pltpu.CompilerParams(vmem_limit_bytes=VMEM),
        name="turn",
    )(parts, cos, sin)


def attend_kernel(info_ref, q_ref, own_ref, first_ref, out_ref):
    core = info_ref[0]
    length = info_ref[1]
    scale = 1.0 / math.sqrt(HD)
    row = lax.broadcasted_iota(jnp.int32, (HALF, HALF), 0)
    col = lax.broadcasted_iota(jnp.int32, (HALF, HALF), 1)
    seen_own = (col <= row) & (col + core * HALF < length)
    seen_first = col < jnp.where(core == 1, length, 0)
    contract = (((1,), (1,)), ((), ()))
    for head in range(NC):
        cols = slice(head * HD, (head + 1) * HD)
        query = q_ref[:, cols]
        own = lax.dot_general(query, own_ref[:, :HD], contract, preferred_element_type=jnp.float32)
        first = lax.dot_general(
            query, first_ref[:, :HD], contract, preferred_element_type=jnp.float32
        )
        own = jnp.where(seen_own, own * scale, MASKED)
        first = jnp.where(seen_first, first * scale, MASKED)
        top = jnp.maximum(
            jnp.max(own, axis=1, keepdims=True), jnp.max(first, axis=1, keepdims=True)
        )
        own = jnp.exp(own - top)
        first = jnp.exp(first - top)
        total = jnp.sum(own, axis=1, keepdims=True) + jnp.sum(first, axis=1, keepdims=True)
        own = (own / total).astype(jnp.bfloat16)
        first = (first / total).astype(jnp.bfloat16)
        context = jnp.dot(own, own_ref[:, HD:], preferred_element_type=jnp.float32)
        context += jnp.dot(first, first_ref[:, HD:], preferred_element_type=jnp.float32)
        context = context.astype(jnp.bfloat16)
        for x in range(NX):
            out_ref[x, :, cols] = context


def attend(info, query, own, first):
    vmem = pl.BlockSpec(memory_space=pltpu.VMEM)
    return pl.pallas_call(
        attend_kernel,
        in_specs=[pl.BlockSpec(memory_space=pltpu.SMEM), vmem, vmem, vmem],
        out_specs=vmem,
        out_shape=jax.ShapeDtypeStruct((NX, HALF, CHIP), jnp.bfloat16),
        compiler_params=pltpu.CompilerParams(vmem_limit_bytes=VMEM),
        name="attend",
    )(info, query, own, first)


def output_kernel(halves, info_ref, ctx_ref, own_ref, other_ref, out_ref, rows):
    depth = rows.shape[1]

    @pl.when(pl.program_id(0) == 0)
    def _():
        for i in range(depth // CHIP):
            rows[:, i * CHIP : (i + 1) * CHIP] = ctx_ref[i]

    core, z = info_ref[0], info_ref[2]
    for part in range(halves):
        cut = slice(part * depth, (part + 1) * depth)
        weight = jnp.concatenate([own_ref[0, cut], other_ref[0, cut]], axis=1)
        total = jnp.dot(rows[...], weight, preferred_element_type=jnp.float32)
        total = total.astype(jnp.bfloat16)
        first = (z if part == 0 else 1 - z) * NC if halves > 1 else 0
        out_ref[0, :, aligned(first + core)] = total[:, :HD]
        out_ref[0, :, aligned(first + 1 - core)] = total[:, HD:]


def output(info, context, wo):
    count = context.shape[0]
    halves = NG // count
    rows = NG * CHIP
    block = pl.BlockSpec((1, rows, HD), lambda i, info: (i, 0, 0))
    return pl.pallas_call(
        functools.partial(output_kernel, halves),
        grid_spec=pltpu.PrefetchScalarGridSpec(
            num_scalar_prefetch=1,
            grid=(NY,),
            in_specs=[
                pl.BlockSpec((count, HALF, CHIP), lambda i, info: (0, 0, 0)),
                block,
                block,
            ],
            out_specs=pl.BlockSpec(
                (1, HALF, halves * CHIP), lambda i, info: (lax.rem(info[3] + NY - i, NY), 0, 0)
            ),
            scratch_shapes=[pltpu.VMEM((HALF, count * CHIP), jnp.bfloat16)],
        ),
        out_shape=jax.ShapeDtypeStruct((NY, HALF, halves * CHIP), jnp.bfloat16),
        compiler_params=pltpu.CompilerParams(vmem_limit_bytes=VMEM),
        name="output",
    )(info, context, *wo)


def ranks(placement, core):
    owners = placement[:, 0]
    order = jnp.arange(owners.shape[0], dtype=jnp.int32)
    earlier = (order[None, :] < order[:, None]) & (owners[:, None] == owners[None, :])
    rank = jnp.sum(earlier.astype(jnp.int32), axis=1)
    blocks = HALF // BLOCK
    here = jnp.arange(ITEMS_HERE, dtype=jnp.int32)
    mine = (core * blocks + here % blocks) * NG + here // blocks
    match = mine[:, None] == order[None, :]
    item_owner = jnp.sum(jnp.where(match, owners[None, :], 0), axis=1)
    item_rank = jnp.sum(jnp.where(match, rank[None, :], 0), axis=1)
    return item_owner, item_rank


def last_to_first(flip):
    return [((SECTIONS - 1) * WIDE + w, w ^ flip) for w in range(WIDE)]


def relay_pairs(first):
    same, cross = [], []
    for s in range(first, SECTIONS - 1, 2):
        for w in range(WIDE):
            same.append((s * WIDE + w, (s + 1) * WIDE + w))
            cross.append((s * WIDE + w, (s + 1) * WIDE + (w ^ 8)))
    return same, cross


def shards(hidden_in, gain, w_query, w_key, w_value, w_out, length, placement):
    segment = lax.axis_index("segment")
    wide = lax.axis_index("wide")
    core = wide % 2
    z = wide // 8 % 2
    x = wide // 2 % NX
    y = wide // 16
    features = gain.shape[1]

    halves = hidden_in.reshape(2, HALF, HD)
    kept = lax.dynamic_index_in_dim(halves, core, 0, keepdims=False)
    given = lax.dynamic_index_in_dim(halves, 1 - core, 0, keepdims=False)
    from_core = swap_cores(given)
    flat = ("segment", "wide")
    cross_own = lax.ppermute(kept, flat, last_to_first(8))
    cross_other = lax.ppermute(given, flat, last_to_first(9))
    start = by_core(core, kept, from_core, 1)
    cross = by_core(core, cross_own, cross_other, 1)

    gain_x = lax.dynamic_index_in_dim(gain.reshape(NG, NX, CHIP), x, 1, keepdims=False)
    gain_x = gain_x.reshape(1, NG * CHIP)

    lane = jnp.arange(HD, dtype=jnp.int32)
    freq = jnp.power(ROPE_BASE, -2.0 * (lane // 2).astype(jnp.float32) / HD)
    position = (core * HALF + jnp.arange(HALF, dtype=jnp.int32)).astype(jnp.float32)
    angle = position[:, None] * freq[None, :]
    cos = jnp.cos(angle)
    sin = jnp.where(lane[None, :] % 2 == 0, -1.0, 1.0) * jnp.sin(angle)
    info = jnp.stack([core, length[0], z, y]).astype(jnp.int32)

    def gather(pair):
        return exchange(jnp.broadcast_to(pair[None], (NY, HALF, NZ * CHIP)), OVER_Y)

    raw = w_out[0].reshape(NY, NZ * NX * CHIP, HD)

    def prepare(out_rows):
        query = exchange(x_blocks(w_query[0]), OVER_X)
        key_value = relayout_kv(w_key[0], w_value[0], core, x)
        out = from_ring(lambda i: lax.dynamic_slice_in_dim(out_rows, i, 1, 0), y, 16)
        return (query, swap_cores(query)), key_value, (out, swap_cores(out))

    def first_section(start, cross):
        pair = jnp.where(
            z == 0,
            jnp.concatenate([start, cross], axis=1),
            jnp.concatenate([cross, start], axis=1),
        )
        gathered = in_order(from_ring(lambda i: pair[None], y, 16), y)
        items = jnp.zeros((ITEMS_HERE,), jnp.int32)
        return gathered, prepare(raw), (items, items)

    def later_section(start, cross):
        halves = raw.reshape(NY, NZ, NX * CHIP, HD)
        kept = lax.dynamic_index_in_dim(halves, z, 1, keepdims=False)
        given = lax.dynamic_index_in_dim(halves, 1 - z, 1, keepdims=False)
        far = lax.ppermute(given, "wide", Z_SWAP)
        out_rows = jnp.concatenate([kept, far], axis=1)
        blank = jnp.zeros((NY, HALF, NZ * CHIP), jnp.bfloat16)
        return blank, prepare(out_rows), ranks(placement, core)

    gathered, (wq, wkv, wo), items = lax.cond(
        segment == 0, first_section, later_section, start, cross
    )

    def later_gather(same, cross):
        return gather((same.astype(jnp.float32) + cross.astype(jnp.float32)).astype(jnp.bfloat16))

    def summed(parts, own):
        parts = parts.astype(jnp.float32)
        return own.astype(jnp.float32) + (parts[0] + parts[1] + parts[2] + parts[3])

    def whole_out(context, own):
        context = jnp.broadcast_to(context[:1], (NG, HALF, CHIP))
        parts = exchange(output(info, exchange(context, OVER_XZ), wo), OVER_Y)
        own = jnp.where(z == 0, own[:, :CHIP], own[:, CHIP:])
        result = summed(parts, own).astype(jnp.bfloat16)
        zero = jnp.zeros_like(result)
        return jnp.concatenate(
            [jnp.where(z == 0, result, zero), jnp.where(z == 0, zero, result)], axis=1
        )

    def half_out(context, own):
        parts = exchange(output(info, exchange(context, OVER_X), wo), OVER_Y)
        return summed(parts, jnp.where(z == 0, own, jnp.zeros_like(own))).astype(jnp.bfloat16)

    def layer(gathered):
        parts = exchange(project(info, gathered, gain_x, wq, wkv), OVER_X)
        query, kv = turn(parts, cos, sin, features)
        first = lax.ppermute(kv, "wide", CORE_UP)
        context = attend(info, query, kv, first)
        own = lax.dynamic_index_in_dim(gathered, y, 0, keepdims=False)
        return lax.cond(segment == 0, whole_out, half_out, context, own), kv

    def send(pairs):
        same, cross = pairs

        def run(value):
            axes = ("segment", "wide")
            return lax.ppermute(value, axes, cross), lax.ppermute(value, axes, same)

        return run

    even, odd = send(relay_pairs(0)), send(relay_pairs(1))

    def tick(t, state):
        gathered, partial, kv = state
        partial, kv = lax.cond(segment == t, layer, lambda gathered: (partial, kv), gathered)

        def hand_on(partial, gathered):
            cross, same = lax.cond(t % 2 == 0, even, odd, partial)
            return lax.cond(
                segment == t + 1, later_gather, lambda same, cross: gathered, same, cross
            )

        gathered = lax.cond(
            ((segment == t) | (segment == t + 1)) & (t < SECTIONS - 1),
            hand_on,
            lambda partial, gathered: gathered,
            partial,
            gathered,
        )
        return gathered, partial, kv

    partial = jnp.zeros((HALF, NZ * CHIP), jnp.bfloat16)
    kv = jnp.zeros((HALF, CHIP), jnp.bfloat16)
    _, partial, kv = lax.fori_loop(0, SECTIONS, tick, (gathered, partial, kv))

    pair = partial.reshape(HALF, NZ, CHIP)
    kept = lax.dynamic_index_in_dim(pair, z, 1, keepdims=False)
    given = lax.dynamic_index_in_dim(pair, 1 - z, 1, keepdims=False)
    other = lax.ppermute(given, "wide", Z_SWAP)
    own = (kept.astype(jnp.float32) + other.astype(jnp.float32)).astype(jnp.bfloat16)
    columns = own.reshape(HALF, NC, HD)
    kept = lax.dynamic_index_in_dim(columns, core, 1, keepdims=False)
    given = lax.dynamic_index_in_dim(columns, 1 - core, 1, keepdims=False)
    outputs = by_core(core, kept, swap_cores(given), 0)

    item_owner, item_rank = lax.cond(
        segment == 0, lambda: ranks(placement, core), lambda: items
    )
    blocks = HALF // BLOCK
    slots = 2 * placement.shape[0] // WIDE
    slot = jnp.arange(slots, dtype=jnp.int32)

    sent = jnp.broadcast_to(kv[None], (NG, HALF, CHIP))
    rows = exchange(sent, OVER_G).reshape(NG * blocks, BLOCK * CHIP)

    def chosen(owner):
        wanted = (item_owner[None, :] == owner) & (item_rank[None, :] == slot[:, None])
        return jnp.dot(wanted.astype(jnp.bfloat16), rows, preferred_element_type=jnp.float32)

    here = chosen(wide)
    there = chosen(wide ^ 1).astype(jnp.bfloat16)
    cache = (here + swap_cores(there).astype(jnp.float32)).astype(jnp.bfloat16)
    return outputs[None], cache.reshape(1, slots, BLOCK, CHIP)


def solution(mesh):
    in_specs = (
        P(None, "wide"),
        P("segment", None),
        P("segment", None, "wide"),
        P("segment", None, "wide"),
        P("segment", None, "wide"),
        P("segment", None, "wide"),
        P(),
        P(),
    )
    out_specs = (P("segment", None, "wide"), P("segment", "wide", None, None))
    return jax.shard_map(shards, mesh=mesh, in_specs=in_specs, out_specs=out_specs, check_vma=False)
```

```python
import functools
import math

import jax
import jax.numpy as jnp
from jax import lax
from jax.experimental import pallas as pl
from jax.experimental.pallas import tpu as pltpu
from jax.sharding import PartitionSpec as P

HD = 128
BLOCK = 8
NY, NZ, NX, NC = 4, 2, 4, 2
NG = NY * NZ
CHIP = NC * HD
WIDE = NG * NX * NC
SECTIONS = 8
HALF = 128
ITEMS_HERE = NG * HALF // BLOCK
EPS = 1e-05
ROPE_BASE = 500000.0
MASKED = -1e30
VMEM = 16 * 1024 * 1024

OVER_X = [[g * 8 + x * 2 + c for x in range(NX)] for g in range(NG) for c in range(NC)]
OVER_XZ = [
    [y * 16 + m * 2 + c for m in range(NZ * NX)] for y in range(NY) for c in range(NC)
]
OVER_G = [[g * 8 + x * 2 + c for g in range(NG)] for x in range(NX) for c in range(NC)]
OVER_Y = [
    [(y * 2 + z) * 8 + x * 2 + c for y in range(NY)]
    for z in range(NZ)
    for x in range(NX)
    for c in range(NC)
]
Z_SWAP = [(w, w ^ 8) for w in range(WIDE)]
CORE_SWAP = [(w, w ^ 1) for w in range(WIDE)]
CORE_UP = [(w, w + 1) for w in range(0, WIDE, 2)]


def exchange(value, groups):
    return lax.all_to_all(value, "wide", 0, 0, axis_index_groups=groups, tiled=True)


def swap_cores(value):
    return lax.ppermute(value, "wide", CORE_SWAP)


def by_core(core, own, other, axis):
    first = jnp.where(core == 0, own, other)
    second = jnp.where(core == 0, other, own)
    return jnp.concatenate([first, second], axis=axis)


def x_blocks(weight):
    return weight.reshape(NG, NX, CHIP, HD).transpose(1, 0, 2, 3).reshape(NX, NG * CHIP, HD)


def moved(w, stride, step):
    at = w // stride % 4
    return w + ((at + step) % 4 - at) * stride


def from_ring(piece, at, stride):
    blocks = [piece(at)]
    for step in range(1, 4):
        pairs = [(w, moved(w, stride, step)) for w in range(WIDE)]
        blocks.append(lax.ppermute(piece((at + step) % 4), "wide", pairs))
    return jnp.concatenate(blocks, axis=0)


def in_order(blocks, at):
    return jnp.concatenate(
        [lax.dynamic_slice_in_dim(blocks, (at + 4 - i) % 4, 1, 0) for i in range(4)], axis=0
    )


def kv_blocks(w_key, w_value, x):
    both = jnp.stack([w_key.T, w_value.T])
    width = both.shape[1]
    both = both.reshape(2, width, NG, NX, CHIP).transpose(3, 0, 1, 2, 4)
    both = both.reshape(NX, 2 * width, NG * CHIP)
    return from_ring(lambda i: lax.dynamic_slice_in_dim(both, i, 1, 0), x, NC)


def relayout_kv(mine, core, x):
    width = mine.shape[1] // 2
    other = in_order(swap_cores(mine), x).reshape(NX, 2, 1, width, NG * CHIP)
    mine = in_order(mine, x).reshape(NX, 2, 1, width, NG * CHIP)
    full = by_core(core, mine, other, 2)
    return full.transpose(1, 0, 2, 3, 4).reshape(2 * HD, NG * CHIP)


def eye(n):
    return lax.broadcasted_iota(jnp.int32, (n, n), 0) == lax.broadcasted_iota(jnp.int32, (n, n), 1)


def aligned(block, size=1):
    return pl.ds(pl.multiple_of(block * HD, HD), size * HD)


def fetch(own_ref, other_ref, weights, sems):
    copies = []
    for i in range(weights.shape[1]):
        pair = []
        for k, ref in enumerate((own_ref, other_ref)):
            copy = pltpu.make_async_copy(ref.at[i], weights.at[k, i], sems.at[k, i])
            copy.start()
            pair.append(copy)
        copies.append(pair)
    return copies


def project_kernel(
    info_ref, h_ref, gain_ref, wkv_ref, own_ref, other_ref, out_ref, normed, weights, sems
):
    copies = fetch(own_ref, other_ref, weights, sems)
    total = jnp.zeros((HALF, 1), jnp.float32)
    for y in range(NY):
        part = h_ref[y].astype(jnp.float32)
        cols = slice(y * NZ * CHIP, (y + 1) * NZ * CHIP)
        normed[:, cols] = (part * gain_ref[:, cols]).astype(jnp.bfloat16)
        total = total + jnp.sum(part * part, axis=1, keepdims=True)
    row = jnp.sum(jnp.where(eye(HALF), total, 0.0), axis=0, keepdims=True)
    high = row.astype(jnp.bfloat16).astype(jnp.float32)
    upper = lax.broadcasted_iota(jnp.int32, (16, HALF), 0) < 8
    squares = jnp.where(upper, high, row - high).astype(jnp.bfloat16)
    kv = lax.dot_general(
        normed[...], wkv_ref[...], (((1,), (1,)), ((), ())), preferred_element_type=jnp.float32
    ).astype(jnp.bfloat16)
    core = info_ref[0]
    for i in range(NX):
        out_ref[i, :HALF, CHIP:] = kv
        out_ref[i, HALF:, :] = jnp.zeros((16, 2 * CHIP), jnp.bfloat16)
        out_ref[i, HALF:, :HALF] = squares
        for copy in copies[i]:
            copy.wait()
        weight = jnp.concatenate([weights[0, i], weights[1, i]], axis=1)
        query = jnp.dot(normed[...], weight, preferred_element_type=jnp.float32)
        query = query.astype(jnp.bfloat16)
        out_ref[i, :HALF, aligned(core)] = query[:, :HD]
        out_ref[i, :HALF, aligned(1 - core)] = query[:, HD:]


def weight_scratch():
    rows = NG * CHIP
    return [pltpu.VMEM((2, NX, rows, HD), jnp.bfloat16), pltpu.SemaphoreType.DMA((2, NX))]


def project(info, gathered, gain, wq, wkv):
    rows = NG * CHIP
    vmem = pl.BlockSpec(memory_space=pltpu.VMEM)
    return pl.pallas_call(
        project_kernel,
        in_specs=[
            pl.BlockSpec(memory_space=pltpu.SMEM),
            vmem,
            vmem,
            vmem,
            pl.BlockSpec(memory_space=pl.ANY),
            pl.BlockSpec(memory_space=pl.ANY),
        ],
        out_specs=vmem,
        out_shape=jax.ShapeDtypeStruct((NX, HALF + 16, 2 * CHIP), jnp.bfloat16),
        scratch_shapes=[pltpu.VMEM((HALF, rows), jnp.bfloat16)] + weight_scratch(),
        compiler_params=pltpu.CompilerParams(vmem_limit_bytes=VMEM),
        name="project",
    )(info, gathered, gain, wkv, *wq)


def turn_kernel(features, part_ref, cos_ref, sin_ref, q_ref, kv_ref):
    total = jnp.zeros((HALF, 2 * CHIP), jnp.float32)
    squares = jnp.zeros((16, HALF), jnp.float32)
    for x in range(NX):
        total = total + part_ref[x, :HALF, :].astype(jnp.float32)
        squares = squares + part_ref[x, HALF:, :HALF].astype(jnp.float32)
    row = lax.rsqrt((squares[0:1] + squares[8:9]) / features + EPS)
    scale = jnp.sum(jnp.where(eye(HALF), row, 0.0), axis=1, keepdims=True)
    total = total * scale
    even = lax.broadcasted_iota(jnp.int32, (HALF, HD), 1) % 2 == 0

    def rope(part):
        swapped = jnp.where(even, pltpu.roll(part, HD - 1, 1), pltpu.roll(part, 1, 1))
        return (part * cos_ref[...] + swapped * sin_ref[...]).astype(jnp.bfloat16)

    for head in range(NC):
        cols = slice(head * HD, (head + 1) * HD)
        q_ref[:, cols] = rope(total[:, cols])
    kv_ref[:, :HD] = rope(total[:, CHIP : CHIP + HD])
    kv_ref[:, HD:] = total[:, CHIP + HD :].astype(jnp.bfloat16)


def turn(parts, cos, sin, features):
    return pl.pallas_call(
        functools.partial(turn_kernel, float(features)),
        out_shape=[jax.ShapeDtypeStruct((HALF, CHIP), jnp.bfloat16)] * 2,
        compiler_params=pltpu.CompilerParams(vmem_limit_bytes=VMEM),
        name="turn",
    )(parts, cos, sin)


def attend_kernel(info_ref, q_ref, own_ref, first_ref, out_ref):
    core = info_ref[0]
    length = info_ref[1]
    scale = 1.0 / math.sqrt(HD)
    row = lax.broadcasted_iota(jnp.int32, (HALF, HALF), 0)
    col = lax.broadcasted_iota(jnp.int32, (HALF, HALF), 1)
    seen_own = (col <= row) & (col + core * HALF < length)
    seen_first = col < jnp.where(core == 1, length, 0)
    contract = (((1,), (1,)), ((), ()))
    for head in range(NC):
        cols = slice(head * HD, (head + 1) * HD)
        query = q_ref[:, cols]
        own = lax.dot_general(query, own_ref[:, :HD], contract, preferred_element_type=jnp.float32)
        first = lax.dot_general(
            query, first_ref[:, :HD], contract, preferred_element_type=jnp.float32
        )
        own = jnp.where(seen_own, own * scale, MASKED)
        first = jnp.where(seen_first, first * scale, MASKED)
        top = jnp.maximum(
            jnp.max(own, axis=1, keepdims=True), jnp.max(first, axis=1, keepdims=True)
        )
        own = jnp.exp(own - top)
        first = jnp.exp(first - top)
        total = jnp.sum(own, axis=1, keepdims=True) + jnp.sum(first, axis=1, keepdims=True)
        own = (own / total).astype(jnp.bfloat16)
        first = (first / total).astype(jnp.bfloat16)
        context = jnp.dot(own, own_ref[:, HD:], preferred_element_type=jnp.float32)
        context += jnp.dot(first, first_ref[:, HD:], preferred_element_type=jnp.float32)
        context = context.astype(jnp.bfloat16)
        for x in range(NX):
            out_ref[x, :, cols] = context


def attend(info, query, own, first):
    vmem = pl.BlockSpec(memory_space=pltpu.VMEM)
    return pl.pallas_call(
        attend_kernel,
        in_specs=[pl.BlockSpec(memory_space=pltpu.SMEM), vmem, vmem, vmem],
        out_specs=vmem,
        out_shape=jax.ShapeDtypeStruct((NX, HALF, CHIP), jnp.bfloat16),
        compiler_params=pltpu.CompilerParams(vmem_limit_bytes=VMEM),
        name="attend",
    )(info, query, own, first)


def output_kernel(
    halves, info_ref, ctx_ref, own_ref, other_ref, out_ref, rows, weights, sems
):
    copies = fetch(own_ref, other_ref, weights, sems)
    depth = rows.shape[1]
    for i in range(depth // CHIP):
        rows[:, i * CHIP : (i + 1) * CHIP] = ctx_ref[i]
    core, z, y = info_ref[0], info_ref[2], info_ref[3]
    for i in range(NY):
        for copy in copies[i]:
            copy.wait()
        source = lax.rem(y + NY - i, NY)
        for part in range(halves):
            cut = slice(part * depth, (part + 1) * depth)
            weight = jnp.concatenate([weights[0, i, cut], weights[1, i, cut]], axis=1)
            total = jnp.dot(rows[...], weight, preferred_element_type=jnp.float32)
            total = total.astype(jnp.bfloat16)
            first = (z if part == 0 else 1 - z) * NC if halves > 1 else 0
            out_ref[source, :, aligned(first + core)] = total[:, :HD]
            out_ref[source, :, aligned(first + 1 - core)] = total[:, HD:]


def output(info, context, wo):
    count = context.shape[0]
    halves = NG // count
    vmem = pl.BlockSpec(memory_space=pltpu.VMEM)
    return pl.pallas_call(
        functools.partial(output_kernel, halves),
        in_specs=[
            pl.BlockSpec(memory_space=pltpu.SMEM),
            vmem,
            pl.BlockSpec(memory_space=pl.ANY),
            pl.BlockSpec(memory_space=pl.ANY),
        ],
        out_specs=vmem,
        out_shape=jax.ShapeDtypeStruct((NY, HALF, halves * CHIP), jnp.bfloat16),
        scratch_shapes=[pltpu.VMEM((HALF, count * CHIP), jnp.bfloat16)] + weight_scratch(),
        compiler_params=pltpu.CompilerParams(vmem_limit_bytes=VMEM),
        name="output",
    )(info, context, *wo)


def ranks(placement, core):
    owners = placement[:, 0]
    order = jnp.arange(owners.shape[0], dtype=jnp.int32)
    earlier = (order[None, :] < order[:, None]) & (owners[:, None] == owners[None, :])
    rank = jnp.sum(earlier.astype(jnp.int32), axis=1)
    blocks = HALF // BLOCK
    here = jnp.arange(ITEMS_HERE, dtype=jnp.int32)
    mine = (core * blocks + here % blocks) * NG + here // blocks
    match = mine[:, None] == order[None, :]
    item_owner = jnp.sum(jnp.where(match, owners[None, :], 0), axis=1)
    item_rank = jnp.sum(jnp.where(match, rank[None, :], 0), axis=1)
    return item_owner, item_rank


def last_to_first(flip):
    return [((SECTIONS - 1) * WIDE + w, w ^ flip) for w in range(WIDE)]


def relay_pairs(first):
    same, cross = [], []
    for s in range(first, SECTIONS - 1, 2):
        for w in range(WIDE):
            same.append((s * WIDE + w, (s + 1) * WIDE + w))
            cross.append((s * WIDE + w, (s + 1) * WIDE + (w ^ 8)))
    return same, cross


def shards(hidden_in, gain, w_query, w_key, w_value, w_out, length, placement):
    segment = lax.axis_index("segment")
    wide = lax.axis_index("wide")
    core = wide % 2
    z = wide // 8 % 2
    x = wide // 2 % NX
    y = wide // 16
    features = gain.shape[1]

    halves = hidden_in.reshape(2, HALF, HD)
    kept = lax.dynamic_index_in_dim(halves, core, 0, keepdims=False)
    given = lax.dynamic_index_in_dim(halves, 1 - core, 0, keepdims=False)
    from_core = swap_cores(given)
    flat = ("segment", "wide")
    cross_own = lax.ppermute(kept, flat, last_to_first(8))
    cross_other = lax.ppermute(given, flat, last_to_first(9))
    start = by_core(core, kept, from_core, 1)
    cross = by_core(core, cross_own, cross_other, 1)

    gain_x = lax.dynamic_index_in_dim(gain.reshape(NG, NX, CHIP), x, 1, keepdims=False)
    gain_x = gain_x.reshape(1, NG * CHIP)

    lane = jnp.arange(HD, dtype=jnp.int32)
    freq = jnp.power(ROPE_BASE, -2.0 * (lane // 2).astype(jnp.float32) / HD)
    position = (core * HALF + jnp.arange(HALF, dtype=jnp.int32)).astype(jnp.float32)
    angle = position[:, None] * freq[None, :]
    cos = jnp.cos(angle)
    sin = jnp.where(lane[None, :] % 2 == 0, -1.0, 1.0) * jnp.sin(angle)
    info = jnp.stack([core, length[0], z, y]).astype(jnp.int32)

    def gather(pair):
        return exchange(jnp.broadcast_to(pair[None], (NY, HALF, NZ * CHIP)), OVER_Y)

    raw = w_out[0].reshape(NY, NZ * NX * CHIP, HD)

    def prepare(out_rows, before):
        query = exchange(x_blocks(w_query[0]), OVER_X)
        mine = kv_blocks(w_key[0], w_value[0], x)
        out_rows = lax.optimization_barrier((out_rows, mine, before))[0]
        key_value = relayout_kv(mine, core, x)
        out = from_ring(lambda i: lax.dynamic_slice_in_dim(out_rows, i, 1, 0), y, 16)
        return (query, swap_cores(query)), key_value, (out, swap_cores(out))

    def first_section(start, cross):
        pair = jnp.where(
            z == 0,
            jnp.concatenate([start, cross], axis=1),
            jnp.concatenate([cross, start], axis=1),
        )
        gathered = in_order(from_ring(lambda i: pair[None], y, 16), y)
        items = jnp.zeros((ITEMS_HERE,), jnp.int32)
        return gathered, prepare(raw, gathered), (items, items)

    def later_section(start, cross):
        halves = raw.reshape(NY, NZ, NX * CHIP, HD)
        kept = lax.dynamic_index_in_dim(halves, z, 1, keepdims=False)
        given = lax.dynamic_index_in_dim(halves, 1 - z, 1, keepdims=False)
        far = lax.ppermute(given, "wide", Z_SWAP)
        out_rows = jnp.concatenate([kept, far], axis=1)
        blank = jnp.zeros((NY, HALF, NZ * CHIP), jnp.bfloat16)
        return blank, prepare(out_rows, start), ranks(placement, core)

    gathered, (wq, wkv, wo), items = lax.cond(
        segment == 0, first_section, later_section, start, cross
    )

    def later_gather(same, cross):
        return gather((same.astype(jnp.float32) + cross.astype(jnp.float32)).astype(jnp.bfloat16))

    def summed(parts, own):
        parts = parts.astype(jnp.float32)
        return own.astype(jnp.float32) + (parts[0] + parts[1] + parts[2] + parts[3])

    def whole_out(context, own):
        context = jnp.broadcast_to(context[:1], (NG, HALF, CHIP))
        parts = exchange(output(info, exchange(context, OVER_XZ), wo), OVER_Y)
        own = jnp.where(z == 0, own[:, :CHIP], own[:, CHIP:])
        result = summed(parts, own).astype(jnp.bfloat16)
        zero = jnp.zeros_like(result)
        return jnp.concatenate(
            [jnp.where(z == 0, result, zero), jnp.where(z == 0, zero, result)], axis=1
        )

    def half_out(context, own):
        parts = exchange(output(info, exchange(context, OVER_X), wo), OVER_Y)
        return summed(parts, jnp.where(z == 0, own, jnp.zeros_like(own))).astype(jnp.bfloat16)

    def layer(gathered):
        parts = exchange(project(info, gathered, gain_x, wq, wkv), OVER_X)
        query, kv = turn(parts, cos, sin, features)
        first = lax.ppermute(kv, "wide", CORE_UP)
        context = attend(info, query, kv, first)
        own = lax.dynamic_index_in_dim(gathered, y, 0, keepdims=False)
        return lax.cond(segment == 0, whole_out, half_out, context, own), kv

    def send(pairs):
        same, cross = pairs

        def run(value):
            axes = ("segment", "wide")
            return lax.ppermute(value, axes, cross), lax.ppermute(value, axes, same)

        return run

    even, odd = send(relay_pairs(0)), send(relay_pairs(1))

    def tick(t, state):
        gathered, partial, kv = state
        partial, kv = lax.cond(segment == t, layer, lambda gathered: (partial, kv), gathered)

        def hand_on(partial, gathered):
            cross, same = lax.cond(t % 2 == 0, even, odd, partial)
            return lax.cond(
                segment == t + 1, later_gather, lambda same, cross: gathered, same, cross
            )

        gathered = lax.cond(
            ((segment == t) | (segment == t + 1)) & (t < SECTIONS - 1),
            hand_on,
            lambda partial, gathered: gathered,
            partial,
            gathered,
        )
        return gathered, partial, kv

    partial = jnp.zeros((HALF, NZ * CHIP), jnp.bfloat16)
    kv = jnp.zeros((HALF, CHIP), jnp.bfloat16)
    _, partial, kv = lax.fori_loop(0, SECTIONS, tick, (gathered, partial, kv))

    pair = partial.reshape(HALF, NZ, CHIP)
    kept = lax.dynamic_index_in_dim(pair, z, 1, keepdims=False)
    given = lax.dynamic_index_in_dim(pair, 1 - z, 1, keepdims=False)
    other = lax.ppermute(given, "wide", Z_SWAP)
    own = (kept.astype(jnp.float32) + other.astype(jnp.float32)).astype(jnp.bfloat16)
    columns = own.reshape(HALF, NC, HD)
    kept = lax.dynamic_index_in_dim(columns, core, 1, keepdims=False)
    given = lax.dynamic_index_in_dim(columns, 1 - core, 1, keepdims=False)
    outputs = by_core(core, kept, swap_cores(given), 0)

    item_owner, item_rank = lax.cond(
        segment == 0, lambda: ranks(placement, core), lambda: items
    )
    blocks = HALF // BLOCK
    slots = 2 * placement.shape[0] // WIDE
    slot = jnp.arange(slots, dtype=jnp.int32)

    sent = jnp.broadcast_to(kv[None], (NG, HALF, CHIP))
    rows = exchange(sent, OVER_G).reshape(NG * blocks, BLOCK * CHIP)

    def chosen(owner):
        wanted = (item_owner[None, :] == owner) & (item_rank[None, :] == slot[:, None])
        return jnp.dot(wanted.astype(jnp.bfloat16), rows, preferred_element_type=jnp.float32)

    here = chosen(wide)
    there = chosen(wide ^ 1).astype(jnp.bfloat16)
    cache = (here + swap_cores(there).astype(jnp.float32)).astype(jnp.bfloat16)
    return outputs[None], cache.reshape(1, slots, BLOCK, CHIP)


def solution(mesh):
    in_specs = (
        P(None, "wide"),
        P("segment", None),
        P("segment", None, "wide"),
        P("segment", None, "wide"),
        P("segment", None, "wide"),
        P("segment", None, "wide"),
        P(),
        P(),
    )
    out_specs = (P("segment", None, "wide"), P("segment", "wide", None, None))
    return jax.shard_map(shards, mesh=mesh, in_specs=in_specs, out_specs=out_specs, check_vma=False)
```

```python
import functools
import math

import jax
import jax.numpy as jnp
from jax import lax
from jax.experimental import pallas as pl
from jax.experimental.pallas import tpu as pltpu
from jax.sharding import PartitionSpec as P

HD = 128
BLOCK = 8
NY, NZ, NX, NC = 4, 2, 4, 2
NG = NY * NZ
CHIP = NC * HD
WIDE = NG * NX * NC
SECTIONS = 8
HALF = 128
ITEMS_HERE = NG * HALF // BLOCK
EPS = 1e-05
ROPE_BASE = 500000.0
MASKED = -1e30
VMEM = 16 * 1024 * 1024

OVER_X = [[g * 8 + x * 2 + c for x in range(NX)] for g in range(NG) for c in range(NC)]
OVER_G = [[g * 8 + x * 2 + c for g in range(NG)] for x in range(NX) for c in range(NC)]
OVER_Y = [
    [(y * 2 + z) * 8 + x * 2 + c for y in range(NY)]
    for z in range(NZ)
    for x in range(NX)
    for c in range(NC)
]
Z_SWAP = [(w, w ^ 8) for w in range(WIDE)]
CORE_SWAP = [(w, w ^ 1) for w in range(WIDE)]
CORE_UP = [(w, w + 1) for w in range(0, WIDE, 2)]


def exchange(value, groups):
    return lax.all_to_all(value, "wide", 0, 0, axis_index_groups=groups, tiled=True)


def swap_cores(value):
    return lax.ppermute(value, "wide", CORE_SWAP)


def by_core(core, own, other, axis):
    first = jnp.where(core == 0, own, other)
    second = jnp.where(core == 0, other, own)
    return jnp.concatenate([first, second], axis=axis)


def x_blocks(weight):
    return weight.reshape(NG, NX, CHIP, HD).transpose(1, 0, 2, 3).reshape(NX, NG * CHIP, HD)


def moved(w, stride, step):
    at = w // stride % 4
    return w + ((at + step) % 4 - at) * stride


def from_ring(piece, at, stride):
    blocks = [piece(at)]
    for step in range(1, 4):
        pairs = [(w, moved(w, stride, step)) for w in range(WIDE)]
        blocks.append(lax.ppermute(piece((at + step) % 4), "wide", pairs))
    return blocks


def in_order(blocks, at):
    return jnp.concatenate(
        [lax.dynamic_slice_in_dim(blocks, (at + 4 - i) % 4, 1, 0) for i in range(4)], axis=0
    )


def kv_blocks(w_key, w_value, x, after):
    both = jnp.stack([w_key.T, w_value.T])
    width = both.shape[1]
    both = both.reshape(2, width, NG, NX, CHIP).transpose(3, 0, 1, 2, 4)
    both = both.reshape(NX, 2 * width, NG * CHIP)
    both = lax.optimization_barrier((both, after))[0]
    blocks = from_ring(lambda i: lax.dynamic_slice_in_dim(both, i, 1, 0), x, NC)
    return jnp.concatenate(blocks, axis=0)


def relayout_kv(mine, core, x):
    width = mine.shape[1] // 2
    other = in_order(swap_cores(mine), x).reshape(NX, 2, 1, width, NG * CHIP)
    mine = in_order(mine, x).reshape(NX, 2, 1, width, NG * CHIP)
    full = by_core(core, mine, other, 2)
    return full.transpose(1, 0, 2, 3, 4).reshape(2 * HD, NG * CHIP)


def eye(n):
    return lax.broadcasted_iota(jnp.int32, (n, n), 0) == lax.broadcasted_iota(jnp.int32, (n, n), 1)


def aligned(block, size=1):
    return pl.ds(pl.multiple_of(block * HD, HD), size * HD)


def fetch(own_ref, other_ref, weights, sems):
    copies = []
    for i in range(weights.shape[1]):
        pair = []
        for k, ref in enumerate((own_ref, other_ref)):
            copy = pltpu.make_async_copy(ref.at[i], weights.at[k, i], sems.at[k, i])
            copy.start()
            pair.append(copy)
        copies.append(pair)
    return copies


def project_kernel(
    info_ref, h_ref, gain_ref, wkv_ref, own_ref, other_ref, out_ref, normed, weights, sems
):
    copies = fetch(own_ref, other_ref, weights, sems)
    total = jnp.zeros((HALF, 1), jnp.float32)
    for y in range(NY):
        part = h_ref[y].astype(jnp.float32)
        cols = slice(y * NZ * CHIP, (y + 1) * NZ * CHIP)
        normed[:, cols] = (part * gain_ref[:, cols]).astype(jnp.bfloat16)
        total = total + jnp.sum(part * part, axis=1, keepdims=True)
    row = jnp.sum(jnp.where(eye(HALF), total, 0.0), axis=0, keepdims=True)
    high = row.astype(jnp.bfloat16).astype(jnp.float32)
    upper = lax.broadcasted_iota(jnp.int32, (16, HALF), 0) < 8
    squares = jnp.where(upper, high, row - high).astype(jnp.bfloat16)
    kv = lax.dot_general(
        normed[...], wkv_ref[...], (((1,), (1,)), ((), ())), preferred_element_type=jnp.float32
    ).astype(jnp.bfloat16)
    core = info_ref[0]
    for i in range(NX):
        out_ref[i, :HALF, CHIP:] = kv
        out_ref[i, HALF:, :] = jnp.zeros((16, 2 * CHIP), jnp.bfloat16)
        out_ref[i, HALF:, :HALF] = squares
        for copy in copies[i]:
            copy.wait()
        weight = jnp.concatenate([weights[0, i], weights[1, i]], axis=1)
        query = jnp.dot(normed[...], weight, preferred_element_type=jnp.float32)
        query = query.astype(jnp.bfloat16)
        out_ref[i, :HALF, aligned(core)] = query[:, :HD]
        out_ref[i, :HALF, aligned(1 - core)] = query[:, HD:]


def weight_scratch():
    rows = NG * CHIP
    return [pltpu.VMEM((2, NX, rows, HD), jnp.bfloat16), pltpu.SemaphoreType.DMA((2, NX))]


def project(info, gathered, gain, wq, wkv):
    rows = NG * CHIP
    vmem = pl.BlockSpec(memory_space=pltpu.VMEM)
    return pl.pallas_call(
        project_kernel,
        in_specs=[
            pl.BlockSpec(memory_space=pltpu.SMEM),
            vmem,
            vmem,
            vmem,
            pl.BlockSpec(memory_space=pl.ANY),
            pl.BlockSpec(memory_space=pl.ANY),
        ],
        out_specs=vmem,
        out_shape=jax.ShapeDtypeStruct((NX, HALF + 16, 2 * CHIP), jnp.bfloat16),
        scratch_shapes=[pltpu.VMEM((HALF, rows), jnp.bfloat16)] + weight_scratch(),
        compiler_params=pltpu.CompilerParams(vmem_limit_bytes=VMEM),
        name="project",
    )(info, gathered, gain, wkv, *wq)


def turn_kernel(features, part_ref, cos_ref, sin_ref, q_ref, kv_ref):
    total = jnp.zeros((HALF, 2 * CHIP), jnp.float32)
    squares = jnp.zeros((16, HALF), jnp.float32)
    for x in range(NX):
        total = total + part_ref[x, :HALF, :].astype(jnp.float32)
        squares = squares + part_ref[x, HALF:, :HALF].astype(jnp.float32)
    row = lax.rsqrt((squares[0:1] + squares[8:9]) / features + EPS)
    scale = jnp.sum(jnp.where(eye(HALF), row, 0.0), axis=1, keepdims=True)
    total = total * scale
    even = lax.broadcasted_iota(jnp.int32, (HALF, HD), 1) % 2 == 0

    def rope(part):
        swapped = jnp.where(even, pltpu.roll(part, HD - 1, 1), pltpu.roll(part, 1, 1))
        return (part * cos_ref[...] + swapped * sin_ref[...]).astype(jnp.bfloat16)

    for head in range(NC):
        cols = slice(head * HD, (head + 1) * HD)
        q_ref[:, cols] = rope(total[:, cols])
    kv_ref[:, :HD] = rope(total[:, CHIP : CHIP + HD])
    kv_ref[:, HD:] = total[:, CHIP + HD :].astype(jnp.bfloat16)


def turn(parts, cos, sin, features):
    return pl.pallas_call(
        functools.partial(turn_kernel, float(features)),
        out_shape=[jax.ShapeDtypeStruct((HALF, CHIP), jnp.bfloat16)] * 2,
        compiler_params=pltpu.CompilerParams(vmem_limit_bytes=VMEM),
        name="turn",
    )(parts, cos, sin)


def attend_kernel(info_ref, q_ref, own_ref, first_ref, out_ref):
    core = info_ref[0]
    length = info_ref[1]
    scale = 1.0 / math.sqrt(HD)
    row = lax.broadcasted_iota(jnp.int32, (HALF, HALF), 0)
    col = lax.broadcasted_iota(jnp.int32, (HALF, HALF), 1)
    seen_own = (col <= row) & (col + core * HALF < length)
    seen_first = col < jnp.where(core == 1, length, 0)
    contract = (((1,), (1,)), ((), ()))
    for head in range(NC):
        cols = slice(head * HD, (head + 1) * HD)
        query = q_ref[:, cols]
        own = lax.dot_general(query, own_ref[:, :HD], contract, preferred_element_type=jnp.float32)
        first = lax.dot_general(
            query, first_ref[:, :HD], contract, preferred_element_type=jnp.float32
        )
        own = jnp.where(seen_own, own * scale, MASKED)
        first = jnp.where(seen_first, first * scale, MASKED)
        top = jnp.maximum(
            jnp.max(own, axis=1, keepdims=True), jnp.max(first, axis=1, keepdims=True)
        )
        own = jnp.exp(own - top)
        first = jnp.exp(first - top)
        total = jnp.sum(own, axis=1, keepdims=True) + jnp.sum(first, axis=1, keepdims=True)
        own = (own / total).astype(jnp.bfloat16)
        first = (first / total).astype(jnp.bfloat16)
        context = jnp.dot(own, own_ref[:, HD:], preferred_element_type=jnp.float32)
        context += jnp.dot(first, first_ref[:, HD:], preferred_element_type=jnp.float32)
        context = context.astype(jnp.bfloat16)
        for x in range(NX):
            out_ref[x, :, cols] = context


def attend(info, query, own, first):
    vmem = pl.BlockSpec(memory_space=pltpu.VMEM)
    return pl.pallas_call(
        attend_kernel,
        in_specs=[pl.BlockSpec(memory_space=pltpu.SMEM), vmem, vmem, vmem],
        out_specs=vmem,
        out_shape=jax.ShapeDtypeStruct((NX, HALF, CHIP), jnp.bfloat16),
        compiler_params=pltpu.CompilerParams(vmem_limit_bytes=VMEM),
        name="attend",
    )(info, query, own, first)


def output_kernel(info_ref, ctx_ref, own_ref, other_ref, out_ref, rows, weights, sems):
    copies = fetch(own_ref, other_ref, weights, sems)
    depth = rows.shape[1]
    for i in range(depth // CHIP):
        rows[:, i * CHIP : (i + 1) * CHIP] = ctx_ref[i]
    core, z, y = info_ref[0], info_ref[2], info_ref[3]
    for i in range(NY):
        for copy in copies[i]:
            copy.wait()
        source = lax.rem(y + NY - i, NY)
        for part in range(NZ):
            cut = slice(part * depth, (part + 1) * depth)
            weight = jnp.concatenate([weights[0, i, cut], weights[1, i, cut]], axis=1)
            total = jnp.dot(rows[...], weight, preferred_element_type=jnp.float32)
            total = total.astype(jnp.bfloat16)
            first = (z if part == 0 else 1 - z) * NC
            out_ref[source, :, aligned(first + core)] = total[:, :HD]
            out_ref[source, :, aligned(first + 1 - core)] = total[:, HD:]


def output(info, context, wo):
    vmem = pl.BlockSpec(memory_space=pltpu.VMEM)
    return pl.pallas_call(
        output_kernel,
        in_specs=[
            pl.BlockSpec(memory_space=pltpu.SMEM),
            vmem,
            pl.BlockSpec(memory_space=pl.ANY),
            pl.BlockSpec(memory_space=pl.ANY),
        ],
        out_specs=vmem,
        out_shape=jax.ShapeDtypeStruct((NY, HALF, NZ * CHIP), jnp.bfloat16),
        scratch_shapes=[pltpu.VMEM((HALF, NX * CHIP), jnp.bfloat16)] + weight_scratch(),
        compiler_params=pltpu.CompilerParams(vmem_limit_bytes=VMEM),
        name="output",
    )(info, context, *wo)


def ranks(placement, core):
    owners = placement[:, 0]
    order = jnp.arange(owners.shape[0], dtype=jnp.int32)
    earlier = (order[None, :] < order[:, None]) & (owners[:, None] == owners[None, :])
    rank = jnp.sum(earlier.astype(jnp.int32), axis=1)
    blocks = HALF // BLOCK
    here = jnp.arange(ITEMS_HERE, dtype=jnp.int32)
    mine = (core * blocks + here % blocks) * NG + here // blocks
    match = mine[:, None] == order[None, :]
    item_owner = jnp.sum(jnp.where(match, owners[None, :], 0), axis=1)
    item_rank = jnp.sum(jnp.where(match, rank[None, :], 0), axis=1)
    return item_owner, item_rank


def last_to_first(flip):
    return [((SECTIONS - 1) * WIDE + w, w ^ flip) for w in range(WIDE)]


def relay_pairs(first):
    same, cross = [], []
    for s in range(first, SECTIONS - 1, 2):
        for w in range(WIDE):
            same.append((s * WIDE + w, (s + 1) * WIDE + w))
            cross.append((s * WIDE + w, (s + 1) * WIDE + (w ^ 8)))
    return same, cross


def shards(hidden_in, gain, w_query, w_key, w_value, w_out, length, placement):
    segment = lax.axis_index("segment")
    wide = lax.axis_index("wide")
    core = wide % 2
    z = wide // 8 % 2
    x = wide // 2 % NX
    y = wide // 16
    features = gain.shape[1]

    halves = hidden_in.reshape(2, HALF, HD)
    kept = lax.dynamic_index_in_dim(halves, core, 0, keepdims=False)
    given = lax.dynamic_index_in_dim(halves, 1 - core, 0, keepdims=False)
    from_core = swap_cores(given)
    flat = ("segment", "wide")
    cross_own = lax.ppermute(kept, flat, last_to_first(8))
    cross_other = lax.ppermute(given, flat, last_to_first(9))
    start = by_core(core, kept, from_core, 1)
    cross = by_core(core, cross_own, cross_other, 1)

    gain_x = lax.dynamic_index_in_dim(gain.reshape(NG, NX, CHIP), x, 1, keepdims=False)
    gain_x = gain_x.reshape(1, NG * CHIP)

    lane = jnp.arange(HD, dtype=jnp.int32)
    freq = jnp.power(ROPE_BASE, -2.0 * (lane // 2).astype(jnp.float32) / HD)
    position = (core * HALF + jnp.arange(HALF, dtype=jnp.int32)).astype(jnp.float32)
    angle = position[:, None] * freq[None, :]
    cos = jnp.cos(angle)
    sin = jnp.where(lane[None, :] % 2 == 0, -1.0, 1.0) * jnp.sin(angle)
    info = jnp.stack([core, length[0], z, y]).astype(jnp.int32)

    def gather(pair):
        return exchange(jnp.broadcast_to(pair[None], (NY, HALF, NZ * CHIP)), OVER_Y)

    raw = w_out[0].reshape(NY, NZ * NX * CHIP, HD)

    halves = raw.reshape(NY, NZ, NX * CHIP, HD)

    def prepare(before, late):
        kept = lax.dynamic_index_in_dim(halves, z, 1, keepdims=False)
        given = lax.dynamic_index_in_dim(halves, 1 - z, 1, keepdims=False)
        rows = x_blocks(w_query[0])
        query = exchange(rows, OVER_X)
        mine = kv_blocks(w_key[0], w_value[0], x, query)
        if late:
            given = lax.optimization_barrier((given, query, mine))[0]
        far = lax.ppermute(given, "wide", Z_SWAP)
        key_value = relayout_kv(mine, core, x)
        out_rows = jnp.concatenate([kept, far], axis=1)
        out_rows = lax.optimization_barrier((out_rows, before))[0]
        blocks = from_ring(lambda i: lax.dynamic_slice_in_dim(out_rows, i, 1, 0), y, 16)
        out = jnp.concatenate(lax.optimization_barrier((blocks, mine))[0], axis=0)
        return (query, swap_cores(query)), key_value, (out, swap_cores(out))

    def early_section(start, cross):
        pair = jnp.where(
            z == 0,
            jnp.concatenate([start, cross], axis=1),
            jnp.concatenate([cross, start], axis=1),
        )
        gathered = in_order(jnp.concatenate(from_ring(lambda i: pair[None], y, 16)), y)
        items = jnp.zeros((ITEMS_HERE,), jnp.int32)
        return gathered, prepare(gathered, False), (items, items)

    def late_section(start, cross):
        blank = jnp.zeros((NY, HALF, NZ * CHIP), jnp.bfloat16)
        return blank, prepare(start, True), ranks(placement, core)

    gathered, (wq, wkv, wo), items = lax.cond(
        segment <= 1, early_section, late_section, start, cross
    )
    cos, sin = lax.optimization_barrier((cos, sin))

    def later_gather(same, cross):
        return gather((same.astype(jnp.float32) + cross.astype(jnp.float32)).astype(jnp.bfloat16))

    def summed(parts, own):
        parts = parts.astype(jnp.float32)
        return own.astype(jnp.float32) + (parts[0] + parts[1] + parts[2] + parts[3])

    def half_out(context, own):
        parts = exchange(output(info, exchange(context, OVER_X), wo), OVER_Y)
        return summed(parts, jnp.where(z == 0, own, jnp.zeros_like(own))).astype(jnp.bfloat16)

    def layer(gathered):
        parts = exchange(project(info, gathered, gain_x, wq, wkv), OVER_X)
        query, kv = turn(parts, cos, sin, features)
        first = lax.ppermute(kv, "wide", CORE_UP)
        context = attend(info, query, kv, first)
        own = lax.dynamic_index_in_dim(gathered, y, 0, keepdims=False)
        return half_out(context, own), kv

    def send(pairs):
        same, cross = pairs

        def run(value):
            axes = ("segment", "wide")
            return lax.ppermute(value, axes, cross), lax.ppermute(value, axes, same)

        return run

    even, odd = send(relay_pairs(0)), send(relay_pairs(1))

    def tick(t, state):
        gathered, partial, kv = state
        partial, kv = lax.cond(segment == t, layer, lambda gathered: (partial, kv), gathered)

        def hand_on(partial, gathered):
            cross, same = lax.cond(t % 2 == 0, even, odd, partial)
            return lax.cond(
                segment == t + 1, later_gather, lambda same, cross: gathered, same, cross
            )

        gathered = lax.cond(
            ((segment == t) | (segment == t + 1)) & (t < SECTIONS - 1),
            hand_on,
            lambda partial, gathered: gathered,
            partial,
            gathered,
        )
        return gathered, partial, kv

    partial = jnp.zeros((HALF, NZ * CHIP), jnp.bfloat16)
    kv = jnp.zeros((HALF, CHIP), jnp.bfloat16)
    _, partial, kv = lax.fori_loop(0, SECTIONS, tick, (gathered, partial, kv))

    pair = partial.reshape(HALF, NZ, CHIP)
    kept = lax.dynamic_index_in_dim(pair, z, 1, keepdims=False)
    given = lax.dynamic_index_in_dim(pair, 1 - z, 1, keepdims=False)
    other = lax.ppermute(given, "wide", Z_SWAP)
    own = (kept.astype(jnp.float32) + other.astype(jnp.float32)).astype(jnp.bfloat16)
    columns = own.reshape(HALF, NC, HD)
    kept = lax.dynamic_index_in_dim(columns, core, 1, keepdims=False)
    given = lax.dynamic_index_in_dim(columns, 1 - core, 1, keepdims=False)
    outputs = by_core(core, kept, swap_cores(given), 0)

    item_owner, item_rank = lax.cond(
        segment <= 1, lambda: ranks(placement, core), lambda: items
    )
    blocks = HALF // BLOCK
    slots = 2 * placement.shape[0] // WIDE
    slot = jnp.arange(slots, dtype=jnp.int32)

    sent = jnp.broadcast_to(kv[None], (NG, HALF, CHIP))
    rows = exchange(sent, OVER_G).reshape(NG * blocks, BLOCK * CHIP)

    def chosen(owner):
        wanted = (item_owner[None, :] == owner) & (item_rank[None, :] == slot[:, None])
        return jnp.dot(wanted.astype(jnp.bfloat16), rows, preferred_element_type=jnp.float32)

    here = chosen(wide)
    there = chosen(wide ^ 1).astype(jnp.bfloat16)
    cache = (here + swap_cores(there).astype(jnp.float32)).astype(jnp.bfloat16)
    return outputs[None], cache.reshape(1, slots, BLOCK, CHIP)


def solution(mesh):
    in_specs = (
        P(None, "wide"),
        P("segment", None),
        P("segment", None, "wide"),
        P("segment", None, "wide"),
        P("segment", None, "wide"),
        P("segment", None, "wide"),
        P(),
        P(),
    )
    out_specs = (P("segment", None, "wide"), P("segment", "wide", None, None))
    return jax.shard_map(shards, mesh=mesh, in_specs=in_specs, out_specs=out_specs, check_vma=False)
```

```python
import functools
import math

import jax
import jax.numpy as jnp
from jax import lax
from jax.experimental import pallas as pl
from jax.experimental.pallas import tpu as pltpu
from jax.sharding import PartitionSpec as P

HD = 128
BLOCK = 8
NY, NZ, NX, NC = 4, 2, 4, 2
NG = NY * NZ
CHIP = NC * HD
WIDE = NG * NX * NC
SECTIONS = 8
HALF = 128
ITEMS_HERE = NG * HALF // BLOCK
EPS = 1e-05
ROPE_BASE = 500000.0
MASKED = -1e30
VMEM = 16 * 1024 * 1024

OVER_X = [[g * 8 + x * 2 + c for x in range(NX)] for g in range(NG) for c in range(NC)]
OVER_G = [[g * 8 + x * 2 + c for g in range(NG)] for x in range(NX) for c in range(NC)]
OVER_Y = [
    [(y * 2 + z) * 8 + x * 2 + c for y in range(NY)]
    for z in range(NZ)
    for x in range(NX)
    for c in range(NC)
]
Z_SWAP = [(w, w ^ 8) for w in range(WIDE)]
CORE_SWAP = [(w, w ^ 1) for w in range(WIDE)]
CORE_UP = [(w, w + 1) for w in range(0, WIDE, 2)]


def exchange(value, groups):
    return lax.all_to_all(value, "wide", 0, 0, axis_index_groups=groups, tiled=True)


def swap_cores(value):
    return lax.ppermute(value, "wide", CORE_SWAP)


def by_core(core, own, other, axis):
    first = jnp.where(core == 0, own, other)
    second = jnp.where(core == 0, other, own)
    return jnp.concatenate([first, second], axis=axis)


def x_blocks(weight):
    return weight.reshape(NG, NX, CHIP, HD).transpose(1, 0, 2, 3).reshape(NX, NG * CHIP, HD)


def moved(w, stride, step):
    at = w // stride % 4
    return w + ((at + step) % 4 - at) * stride


def from_ring(piece, at, stride):
    blocks = [piece(at)]
    for step in range(1, 4):
        pairs = [(w, moved(w, stride, step)) for w in range(WIDE)]
        blocks.append(lax.ppermute(piece((at + step) % 4), "wide", pairs))
    return blocks


def in_order(blocks, at):
    return jnp.concatenate(
        [lax.dynamic_slice_in_dim(blocks, (at + 4 - i) % 4, 1, 0) for i in range(4)], axis=0
    )


def kv_blocks(w_key, w_value):
    both = jnp.stack([w_key.T, w_value.T])
    width = both.shape[1]
    both = both.reshape(2, width, NG, NX, CHIP).transpose(3, 0, 1, 2, 4)
    return both.reshape(NX, 2 * width * NG * NC, HD)


def whole_head(mine, other, core):
    rows = NG * CHIP
    mine = mine.reshape(NX, 2, 1, -1, rows)
    other = other.reshape(NX, 2, 1, -1, rows)
    full = by_core(core, mine, other, 2)
    return full.transpose(1, 0, 2, 3, 4).reshape(2 * HD, rows)


def eye(n):
    return lax.broadcasted_iota(jnp.int32, (n, n), 0) == lax.broadcasted_iota(jnp.int32, (n, n), 1)


def aligned(block, size=1):
    return pl.ds(pl.multiple_of(block * HD, HD), size * HD)


def fetch(own_ref, other_ref, weights, sems):
    copies = []
    for i in range(weights.shape[1]):
        pair = []
        for k, ref in enumerate((own_ref, other_ref)):
            source = ref.at[i, pl.ds(0, weights.shape[2])]
            copy = pltpu.make_async_copy(source, weights.at[k, i], sems.at[k, i])
            copy.start()
            pair.append(copy)
        copies.append(pair)
    return copies


def project_kernel(
    info_ref, h_ref, gain_ref, wkv_ref, own_ref, other_ref, out_ref, normed, weights, sems
):
    copies = fetch(own_ref, other_ref, weights, sems)
    total = jnp.zeros((HALF, 1), jnp.float32)
    for y in range(NY):
        part = h_ref[y].astype(jnp.float32)
        cols = slice(y * NZ * CHIP, (y + 1) * NZ * CHIP)
        normed[:, cols] = (part * gain_ref[:, cols]).astype(jnp.bfloat16)
        total = total + jnp.sum(part * part, axis=1, keepdims=True)
    row = jnp.sum(jnp.where(eye(HALF), total, 0.0), axis=0, keepdims=True)
    high = row.astype(jnp.bfloat16).astype(jnp.float32)
    upper = lax.broadcasted_iota(jnp.int32, (16, HALF), 0) < 8
    squares = jnp.where(upper, high, row - high).astype(jnp.bfloat16)
    kv = lax.dot_general(
        normed[...], wkv_ref[...], (((1,), (1,)), ((), ())), preferred_element_type=jnp.float32
    ).astype(jnp.bfloat16)
    core = info_ref[0]
    for i in range(NX):
        out_ref[i, :HALF, CHIP:] = kv
        out_ref[i, HALF:, :] = jnp.zeros((16, 2 * CHIP), jnp.bfloat16)
        out_ref[i, HALF:, :HALF] = squares
        for copy in copies[i]:
            copy.wait()
        weight = jnp.concatenate([weights[0, i], weights[1, i]], axis=1)
        query = jnp.dot(normed[...], weight, preferred_element_type=jnp.float32)
        query = query.astype(jnp.bfloat16)
        out_ref[i, :HALF, aligned(core)] = query[:, :HD]
        out_ref[i, :HALF, aligned(1 - core)] = query[:, HD:]


def weight_scratch():
    rows = NG * CHIP
    return [pltpu.VMEM((2, NX, rows, HD), jnp.bfloat16), pltpu.SemaphoreType.DMA((2, NX))]


def project(info, gathered, gain, wq, wkv):
    rows = NG * CHIP
    vmem = pl.BlockSpec(memory_space=pltpu.VMEM)
    return pl.pallas_call(
        project_kernel,
        in_specs=[
            pl.BlockSpec(memory_space=pltpu.SMEM),
            vmem,
            vmem,
            vmem,
            pl.BlockSpec(memory_space=pl.ANY),
            pl.BlockSpec(memory_space=pl.ANY),
        ],
        out_specs=vmem,
        out_shape=jax.ShapeDtypeStruct((NX, HALF + 16, 2 * CHIP), jnp.bfloat16),
        scratch_shapes=[pltpu.VMEM((HALF, rows), jnp.bfloat16)] + weight_scratch(),
        compiler_params=pltpu.CompilerParams(vmem_limit_bytes=VMEM),
        name="project",
    )(info, gathered, gain, wkv, *wq)


def turn_kernel(features, part_ref, cos_ref, sin_ref, q_ref, kv_ref):
    total = jnp.zeros((HALF, 2 * CHIP), jnp.float32)
    squares = jnp.zeros((16, HALF), jnp.float32)
    for x in range(NX):
        total = total + part_ref[x, :HALF, :].astype(jnp.float32)
        squares = squares + part_ref[x, HALF:, :HALF].astype(jnp.float32)
    row = lax.rsqrt((squares[0:1] + squares[8:9]) / features + EPS)
    scale = jnp.sum(jnp.where(eye(HALF), row, 0.0), axis=1, keepdims=True)
    total = total * scale
    even = lax.broadcasted_iota(jnp.int32, (HALF, HD), 1) % 2 == 0

    def rope(part):
        swapped = jnp.where(even, pltpu.roll(part, HD - 1, 1), pltpu.roll(part, 1, 1))
        return (part * cos_ref[...] + swapped * sin_ref[...]).astype(jnp.bfloat16)

    for head in range(NC):
        cols = slice(head * HD, (head + 1) * HD)
        q_ref[:, cols] = rope(total[:, cols])
    kv_ref[:, :HD] = rope(total[:, CHIP : CHIP + HD])
    kv_ref[:, HD:] = total[:, CHIP + HD :].astype(jnp.bfloat16)


def turn(parts, cos, sin, features):
    return pl.pallas_call(
        functools.partial(turn_kernel, float(features)),
        out_shape=[jax.ShapeDtypeStruct((HALF, CHIP), jnp.bfloat16)] * 2,
        compiler_params=pltpu.CompilerParams(vmem_limit_bytes=VMEM),
        name="turn",
    )(parts, cos, sin)


def attend_kernel(info_ref, q_ref, own_ref, first_ref, out_ref):
    core = info_ref[0]
    length = info_ref[1]
    scale = 1.0 / math.sqrt(HD)
    row = lax.broadcasted_iota(jnp.int32, (HALF, HALF), 0)
    col = lax.broadcasted_iota(jnp.int32, (HALF, HALF), 1)
    seen_own = (col <= row) & (col + core * HALF < length)
    seen_first = col < jnp.where(core == 1, length, 0)
    contract = (((1,), (1,)), ((), ()))
    for head in range(NC):
        cols = slice(head * HD, (head + 1) * HD)
        query = q_ref[:, cols]
        own = lax.dot_general(query, own_ref[:, :HD], contract, preferred_element_type=jnp.float32)
        first = lax.dot_general(
            query, first_ref[:, :HD], contract, preferred_element_type=jnp.float32
        )
        own = jnp.where(seen_own, own * scale, MASKED)
        first = jnp.where(seen_first, first * scale, MASKED)
        top = jnp.maximum(
            jnp.max(own, axis=1, keepdims=True), jnp.max(first, axis=1, keepdims=True)
        )
        own = jnp.exp(own - top)
        first = jnp.exp(first - top)
        total = jnp.sum(own, axis=1, keepdims=True) + jnp.sum(first, axis=1, keepdims=True)
        own = (own / total).astype(jnp.bfloat16)
        first = (first / total).astype(jnp.bfloat16)
        context = jnp.dot(own, own_ref[:, HD:], preferred_element_type=jnp.float32)
        context += jnp.dot(first, first_ref[:, HD:], preferred_element_type=jnp.float32)
        context = context.astype(jnp.bfloat16)
        for x in range(NX):
            out_ref[x, :, cols] = context


def attend(info, query, own, first):
    vmem = pl.BlockSpec(memory_space=pltpu.VMEM)
    return pl.pallas_call(
        attend_kernel,
        in_specs=[pl.BlockSpec(memory_space=pltpu.SMEM), vmem, vmem, vmem],
        out_specs=vmem,
        out_shape=jax.ShapeDtypeStruct((NX, HALF, CHIP), jnp.bfloat16),
        compiler_params=pltpu.CompilerParams(vmem_limit_bytes=VMEM),
        name="attend",
    )(info, query, own, first)


def output_kernel(info_ref, ctx_ref, own_ref, other_ref, out_ref, rows, weights, sems):
    copies = fetch(own_ref, other_ref, weights, sems)
    depth = rows.shape[1]
    for i in range(depth // CHIP):
        rows[:, i * CHIP : (i + 1) * CHIP] = ctx_ref[i]
    core, z, y = info_ref[0], info_ref[2], info_ref[3]
    for i in range(NY):
        for copy in copies[i]:
            copy.wait()
        source = lax.rem(y + NY - i, NY)
        for part in range(NZ):
            cut = slice(part * depth, (part + 1) * depth)
            weight = jnp.concatenate([weights[0, i, cut], weights[1, i, cut]], axis=1)
            total = jnp.dot(rows[...], weight, preferred_element_type=jnp.float32)
            total = total.astype(jnp.bfloat16)
            first = (z if part == 0 else 1 - z) * NC
            out_ref[source, :, aligned(first + core)] = total[:, :HD]
            out_ref[source, :, aligned(first + 1 - core)] = total[:, HD:]


def output(info, context, wo):
    vmem = pl.BlockSpec(memory_space=pltpu.VMEM)
    return pl.pallas_call(
        output_kernel,
        in_specs=[
            pl.BlockSpec(memory_space=pltpu.SMEM),
            vmem,
            pl.BlockSpec(memory_space=pl.ANY),
            pl.BlockSpec(memory_space=pl.ANY),
        ],
        out_specs=vmem,
        out_shape=jax.ShapeDtypeStruct((NY, HALF, NZ * CHIP), jnp.bfloat16),
        scratch_shapes=[pltpu.VMEM((HALF, NX * CHIP), jnp.bfloat16)] + weight_scratch(),
        compiler_params=pltpu.CompilerParams(vmem_limit_bytes=VMEM),
        name="output",
    )(info, context, *wo)


def ranks(placement, core):
    owners = placement[:, 0]
    order = jnp.arange(owners.shape[0], dtype=jnp.int32)
    earlier = (order[None, :] < order[:, None]) & (owners[:, None] == owners[None, :])
    rank = jnp.sum(earlier.astype(jnp.int32), axis=1)
    blocks = HALF // BLOCK
    here = jnp.arange(ITEMS_HERE, dtype=jnp.int32)
    mine = (core * blocks + here % blocks) * NG + here // blocks
    match = mine[:, None] == order[None, :]
    item_owner = jnp.sum(jnp.where(match, owners[None, :], 0), axis=1)
    item_rank = jnp.sum(jnp.where(match, rank[None, :], 0), axis=1)
    return item_owner, item_rank


def last_to_first(flip):
    return [((SECTIONS - 1) * WIDE + w, w ^ flip) for w in range(WIDE)]


def relay_pairs(first):
    same, cross = [], []
    for s in range(first, SECTIONS - 1, 2):
        for w in range(WIDE):
            same.append((s * WIDE + w, (s + 1) * WIDE + w))
            cross.append((s * WIDE + w, (s + 1) * WIDE + (w ^ 8)))
    return same, cross


def shards(hidden_in, gain, w_query, w_key, w_value, w_out, length, placement):
    segment = lax.axis_index("segment")
    wide = lax.axis_index("wide")
    core = wide % 2
    z = wide // 8 % 2
    x = wide // 2 % NX
    y = wide // 16
    features = gain.shape[1]

    halves = hidden_in.reshape(2, HALF, HD)
    kept = lax.dynamic_index_in_dim(halves, core, 0, keepdims=False)
    given = lax.dynamic_index_in_dim(halves, 1 - core, 0, keepdims=False)
    from_core = swap_cores(given)
    flat = ("segment", "wide")
    cross_own = lax.ppermute(kept, flat, last_to_first(8))
    cross_other = lax.ppermute(given, flat, last_to_first(9))
    start = by_core(core, kept, from_core, 1)
    cross = by_core(core, cross_own, cross_other, 1)

    gain_x = lax.dynamic_index_in_dim(gain.reshape(NG, NX, CHIP), x, 1, keepdims=False)
    gain_x = gain_x.reshape(1, NG * CHIP)

    lane = jnp.arange(HD, dtype=jnp.int32)
    freq = jnp.power(ROPE_BASE, -2.0 * (lane // 2).astype(jnp.float32) / HD)
    position = (core * HALF + jnp.arange(HALF, dtype=jnp.int32)).astype(jnp.float32)
    angle = position[:, None] * freq[None, :]
    cos = jnp.cos(angle)
    sin = jnp.where(lane[None, :] % 2 == 0, -1.0, 1.0) * jnp.sin(angle)
    info = jnp.stack([core, length[0], z, y]).astype(jnp.int32)

    def gather(pair):
        return exchange(jnp.broadcast_to(pair[None], (NY, HALF, NZ * CHIP)), OVER_Y)

    raw = w_out[0].reshape(NY, NZ * NX * CHIP, HD)

    halves = raw.reshape(NY, NZ, NX * CHIP, HD)

    def prepare(before, late):
        kept = lax.dynamic_index_in_dim(halves, z, 1, keepdims=False)
        given = lax.dynamic_index_in_dim(halves, 1 - z, 1, keepdims=False)
        rows = jnp.concatenate([x_blocks(w_query[0]), kv_blocks(w_key[0], w_value[0])], axis=1)
        mine = exchange(rows, OVER_X)
        other = swap_cores(mine)
        if late:
            given = lax.optimization_barrier((given, mine))[0]
        far = lax.ppermute(given, "wide", Z_SWAP)
        depth = NG * CHIP
        key_value = whole_head(mine[:, depth:], other[:, depth:], core)
        out_rows = jnp.concatenate([kept, far], axis=1)
        out_rows = lax.optimization_barrier((out_rows, before))[0]
        blocks = from_ring(lambda i: lax.dynamic_slice_in_dim(out_rows, i, 1, 0), y, 16)
        out = jnp.concatenate(blocks, axis=0)
        return (mine, other), key_value, (out, swap_cores(out))

    def early_section(start, cross):
        pair = jnp.where(
            z == 0,
            jnp.concatenate([start, cross], axis=1),
            jnp.concatenate([cross, start], axis=1),
        )
        gathered = in_order(jnp.concatenate(from_ring(lambda i: pair[None], y, 16)), y)
        items = jnp.zeros((ITEMS_HERE,), jnp.int32)
        return gathered, prepare(gathered, False), (items, items)

    def late_section(start, cross):
        blank = jnp.zeros((NY, HALF, NZ * CHIP), jnp.bfloat16)
        return blank, prepare(start, True), ranks(placement, core)

    gathered, (wq, wkv, wo), items = lax.cond(
        segment <= 1, early_section, late_section, start, cross
    )
    cos, sin = lax.optimization_barrier((cos, sin))

    def later_gather(same, cross):
        return gather((same.astype(jnp.float32) + cross.astype(jnp.float32)).astype(jnp.bfloat16))

    def summed(parts, own):
        parts = parts.astype(jnp.float32)
        return own.astype(jnp.float32) + (parts[0] + parts[1] + parts[2] + parts[3])

    def half_out(context, own):
        parts = exchange(output(info, exchange(context, OVER_X), wo), OVER_Y)
        return summed(parts, jnp.where(z == 0, own, jnp.zeros_like(own))).astype(jnp.bfloat16)

    def layer(gathered):
        parts = exchange(project(info, gathered, gain_x, wq, wkv), OVER_X)
        query, kv = turn(parts, cos, sin, features)
        first = lax.ppermute(kv, "wide", CORE_UP)
        context = attend(info, query, kv, first)
        own = lax.dynamic_index_in_dim(gathered, y, 0, keepdims=False)
        return half_out(context, own), kv

    def send(pairs):
        same, cross = pairs

        def run(value):
            axes = ("segment", "wide")
            return lax.ppermute(value, axes, cross), lax.ppermute(value, axes, same)

        return run

    even, odd = send(relay_pairs(0)), send(relay_pairs(1))

    def tick(t, state):
        gathered, partial, kv = state
        partial, kv = lax.cond(segment == t, layer, lambda gathered: (partial, kv), gathered)

        def hand_on(partial, gathered):
            cross, same = lax.cond(t % 2 == 0, even, odd, partial)
            return lax.cond(
                segment == t + 1, later_gather, lambda same, cross: gathered, same, cross
            )

        gathered = lax.cond(
            ((segment == t) | (segment == t + 1)) & (t < SECTIONS - 1),
            hand_on,
            lambda partial, gathered: gathered,
            partial,
            gathered,
        )
        return gathered, partial, kv

    partial = jnp.zeros((HALF, NZ * CHIP), jnp.bfloat16)
    kv = jnp.zeros((HALF, CHIP), jnp.bfloat16)
    _, partial, kv = lax.fori_loop(0, SECTIONS, tick, (gathered, partial, kv))

    pair = partial.reshape(HALF, NZ, CHIP)
    kept = lax.dynamic_index_in_dim(pair, z, 1, keepdims=False)
    given = lax.dynamic_index_in_dim(pair, 1 - z, 1, keepdims=False)
    other = lax.ppermute(given, "wide", Z_SWAP)
    own = (kept.astype(jnp.float32) + other.astype(jnp.float32)).astype(jnp.bfloat16)
    columns = own.reshape(HALF, NC, HD)
    kept = lax.dynamic_index_in_dim(columns, core, 1, keepdims=False)
    given = lax.dynamic_index_in_dim(columns, 1 - core, 1, keepdims=False)
    outputs = by_core(core, kept, swap_cores(given), 0)

    item_owner, item_rank = lax.cond(
        segment <= 1, lambda: ranks(placement, core), lambda: items
    )
    blocks = HALF // BLOCK
    slots = 2 * placement.shape[0] // WIDE
    slot = jnp.arange(slots, dtype=jnp.int32)

    sent = jnp.broadcast_to(kv[None], (NG, HALF, CHIP))
    rows = exchange(sent, OVER_G).reshape(NG * blocks, BLOCK * CHIP)

    def chosen(owner):
        wanted = (item_owner[None, :] == owner) & (item_rank[None, :] == slot[:, None])
        return jnp.dot(wanted.astype(jnp.bfloat16), rows, preferred_element_type=jnp.float32)

    here = chosen(wide)
    there = chosen(wide ^ 1).astype(jnp.bfloat16)
    cache = (here + swap_cores(there).astype(jnp.float32)).astype(jnp.bfloat16)
    return outputs[None], cache.reshape(1, slots, BLOCK, CHIP)


def solution(mesh):
    in_specs = (
        P(None, "wide"),
        P("segment", None),
        P("segment", None, "wide"),
        P("segment", None, "wide"),
        P("segment", None, "wide"),
        P("segment", None, "wide"),
        P(),
        P(),
    )
    out_specs = (P("segment", None, "wide"), P("segment", "wide", None, None))
    return jax.shard_map(shards, mesh=mesh, in_specs=in_specs, out_specs=out_specs, check_vma=False)
```

```python
import functools
import math

import jax
import jax.numpy as jnp
from jax import lax
from jax.experimental import pallas as pl
from jax.experimental.pallas import tpu as pltpu
from jax.sharding import PartitionSpec as P

HD = 128
BLOCK = 8
NY, NZ, NX, NC = 4, 2, 4, 2
NG = NY * NZ
CHIP = NC * HD
WIDE = NG * NX * NC
SECTIONS = 8
HALF = 128
ITEMS_HERE = NG * HALF // BLOCK
EPS = 1e-05
ROPE_BASE = 500000.0
MASKED = -1e30
VMEM = 16 * 1024 * 1024

OVER_X = [[g * 8 + x * 2 + c for x in range(NX)] for g in range(NG) for c in range(NC)]
OVER_G = [[g * 8 + x * 2 + c for g in range(NG)] for x in range(NX) for c in range(NC)]
OVER_Y = [
    [(y * 2 + z) * 8 + x * 2 + c for y in range(NY)]
    for z in range(NZ)
    for x in range(NX)
    for c in range(NC)
]
Z_SWAP = [(w, w ^ 8) for w in range(WIDE)]
CORE_SWAP = [(w, w ^ 1) for w in range(WIDE)]
CORE_UP = [(w, w + 1) for w in range(0, WIDE, 2)]


def exchange(value, groups):
    return lax.all_to_all(value, "wide", 0, 0, axis_index_groups=groups, tiled=True)


def swap_cores(value):
    return lax.ppermute(value, "wide", CORE_SWAP)


def by_core(core, own, other, axis):
    first = jnp.where(core == 0, own, other)
    second = jnp.where(core == 0, other, own)
    return jnp.concatenate([first, second], axis=axis)


def x_blocks(weight):
    return weight.reshape(NG, NX, CHIP, HD).transpose(1, 0, 2, 3).reshape(NX, NG * CHIP, HD)


def moved(w, stride, step):
    at = w // stride % 4
    return w + ((at + step) % 4 - at) * stride


def from_ring(piece, at, stride):
    blocks = [piece(at)]
    for step in range(1, 4):
        pairs = [(w, moved(w, stride, step)) for w in range(WIDE)]
        blocks.append(lax.ppermute(piece((at + step) % 4), "wide", pairs))
    return blocks


def in_order(blocks, at):
    return jnp.concatenate(
        [lax.dynamic_slice_in_dim(blocks, (at + 4 - i) % 4, 1, 0) for i in range(4)], axis=0
    )


def kv_blocks(w_key, w_value):
    both = jnp.stack([w_key.T, w_value.T])
    width = both.shape[1]
    both = both.reshape(2, width, NG, NX, CHIP).transpose(3, 0, 1, 2, 4)
    return both.reshape(NX, 2 * width, NG * CHIP)


def kv_over_x(both, x, after):
    both = lax.optimization_barrier((both, after))[0]
    blocks = from_ring(lambda i: lax.dynamic_slice_in_dim(both, i, 1, 0), x, NC)
    return jnp.concatenate(blocks, axis=0)


def relayout_kv(mine, core, x):
    width = mine.shape[1] // 2
    other = in_order(swap_cores(mine), x).reshape(NX, 2, 1, width, NG * CHIP)
    mine = in_order(mine, x).reshape(NX, 2, 1, width, NG * CHIP)
    full = by_core(core, mine, other, 2)
    return full.transpose(1, 0, 2, 3, 4).reshape(2 * HD, NG * CHIP)


def eye(n):
    return lax.broadcasted_iota(jnp.int32, (n, n), 0) == lax.broadcasted_iota(jnp.int32, (n, n), 1)


def aligned(block, size=1):
    return pl.ds(pl.multiple_of(block * HD, HD), size * HD)


def fetch(own_ref, other_ref, weights, sems):
    copies = []
    for i in range(weights.shape[1]):
        pair = []
        for k, ref in enumerate((own_ref, other_ref)):
            copy = pltpu.make_async_copy(ref.at[i], weights.at[k, i], sems.at[k, i])
            copy.start()
            pair.append(copy)
        copies.append(pair)
    return copies


def project_kernel(
    info_ref, h_ref, gain_ref, wkv_ref, own_ref, other_ref, out_ref, normed, weights, sems
):
    copies = fetch(own_ref, other_ref, weights, sems)
    total = jnp.zeros((HALF, 1), jnp.float32)
    for y in range(NY):
        part = h_ref[y].astype(jnp.float32)
        cols = slice(y * NZ * CHIP, (y + 1) * NZ * CHIP)
        normed[:, cols] = (part * gain_ref[:, cols]).astype(jnp.bfloat16)
        total = total + jnp.sum(part * part, axis=1, keepdims=True)
    row = jnp.sum(jnp.where(eye(HALF), total, 0.0), axis=0, keepdims=True)
    high = row.astype(jnp.bfloat16).astype(jnp.float32)
    upper = lax.broadcasted_iota(jnp.int32, (16, HALF), 0) < 8
    squares = jnp.where(upper, high, row - high).astype(jnp.bfloat16)
    kv = lax.dot_general(
        normed[...], wkv_ref[...], (((1,), (1,)), ((), ())), preferred_element_type=jnp.float32
    ).astype(jnp.bfloat16)
    core = info_ref[0]
    for i in range(NX):
        out_ref[i, :HALF, CHIP:] = kv
        out_ref[i, HALF:, :] = jnp.zeros((16, 2 * CHIP), jnp.bfloat16)
        out_ref[i, HALF:, :HALF] = squares
        for copy in copies[i]:
            copy.wait()
        weight = jnp.concatenate([weights[0, i], weights[1, i]], axis=1)
        query = jnp.dot(normed[...], weight, preferred_element_type=jnp.float32)
        query = query.astype(jnp.bfloat16)
        out_ref[i, :HALF, aligned(core)] = query[:, :HD]
        out_ref[i, :HALF, aligned(1 - core)] = query[:, HD:]


def weight_scratch():
    rows = NG * CHIP
    return [pltpu.VMEM((2, NX, rows, HD), jnp.bfloat16), pltpu.SemaphoreType.DMA((2, NX))]


def project(info, gathered, gain, wq, wkv):
    rows = NG * CHIP
    vmem = pl.BlockSpec(memory_space=pltpu.VMEM)
    return pl.pallas_call(
        project_kernel,
        in_specs=[
            pl.BlockSpec(memory_space=pltpu.SMEM),
            vmem,
            vmem,
            vmem,
            pl.BlockSpec(memory_space=pl.ANY),
            pl.BlockSpec(memory_space=pl.ANY),
        ],
        out_specs=vmem,
        out_shape=jax.ShapeDtypeStruct((NX, HALF + 16, 2 * CHIP), jnp.bfloat16),
        scratch_shapes=[pltpu.VMEM((HALF, rows), jnp.bfloat16)] + weight_scratch(),
        compiler_params=pltpu.CompilerParams(vmem_limit_bytes=VMEM),
        name="project",
    )(info, gathered, gain, wkv, *wq)


def join_kernel(same_ref, cross_ref, out_ref):
    pair = same_ref[...].astype(jnp.float32) + cross_ref[...].astype(jnp.float32)
    for y in range(NY):
        out_ref[y] = pair.astype(jnp.bfloat16)


def join(same, cross):
    return pl.pallas_call(
        join_kernel,
        out_shape=jax.ShapeDtypeStruct((NY,) + same.shape, jnp.bfloat16),
        compiler_params=pltpu.CompilerParams(vmem_limit_bytes=VMEM),
        name="join",
    )(same, cross)


def turn_kernel(features, part_ref, cos_ref, sin_ref, q_ref, kv_ref):
    total = jnp.zeros((HALF, 2 * CHIP), jnp.float32)
    squares = jnp.zeros((16, HALF), jnp.float32)
    for x in range(NX):
        total = total + part_ref[x, :HALF, :].astype(jnp.float32)
        squares = squares + part_ref[x, HALF:, :HALF].astype(jnp.float32)
    row = lax.rsqrt((squares[0:1] + squares[8:9]) / features + EPS)
    scale = jnp.sum(jnp.where(eye(HALF), row, 0.0), axis=1, keepdims=True)
    total = total * scale
    even = lax.broadcasted_iota(jnp.int32, (HALF, HD), 1) % 2 == 0

    def rope(part):
        swapped = jnp.where(even, pltpu.roll(part, HD - 1, 1), pltpu.roll(part, 1, 1))
        return (part * cos_ref[...] + swapped * sin_ref[...]).astype(jnp.bfloat16)

    for head in range(NC):
        cols = slice(head * HD, (head + 1) * HD)
        q_ref[:, cols] = rope(total[:, cols])
    kv_ref[:, :HD] = rope(total[:, CHIP : CHIP + HD])
    kv_ref[:, HD:] = total[:, CHIP + HD :].astype(jnp.bfloat16)


def turn(parts, cos, sin, features):
    return pl.pallas_call(
        functools.partial(turn_kernel, float(features)),
        out_shape=[jax.ShapeDtypeStruct((HALF, CHIP), jnp.bfloat16)] * 2,
        compiler_params=pltpu.CompilerParams(vmem_limit_bytes=VMEM),
        name="turn",
    )(parts, cos, sin)


def attend_kernel(info_ref, q_ref, own_ref, first_ref, out_ref):
    core = info_ref[0]
    length = info_ref[1]
    scale = 1.0 / math.sqrt(HD)
    row = lax.broadcasted_iota(jnp.int32, (HALF, HALF), 0)
    col = lax.broadcasted_iota(jnp.int32, (HALF, HALF), 1)
    seen_own = (col <= row) & (col + core * HALF < length)
    seen_first = col < jnp.where(core == 1, length, 0)
    contract = (((1,), (1,)), ((), ()))
    for head in range(NC):
        cols = slice(head * HD, (head + 1) * HD)
        query = q_ref[:, cols]
        own = lax.dot_general(query, own_ref[:, :HD], contract, preferred_element_type=jnp.float32)
        first = lax.dot_general(
            query, first_ref[:, :HD], contract, preferred_element_type=jnp.float32
        )
        own = jnp.where(seen_own, own * scale, MASKED)
        first = jnp.where(seen_first, first * scale, MASKED)
        top = jnp.maximum(
            jnp.max(own, axis=1, keepdims=True), jnp.max(first, axis=1, keepdims=True)
        )
        own = jnp.exp(own - top)
        first = jnp.exp(first - top)
        total = jnp.sum(own, axis=1, keepdims=True) + jnp.sum(first, axis=1, keepdims=True)
        own = (own / total).astype(jnp.bfloat16)
        first = (first / total).astype(jnp.bfloat16)
        context = jnp.dot(own, own_ref[:, HD:], preferred_element_type=jnp.float32)
        context += jnp.dot(first, first_ref[:, HD:], preferred_element_type=jnp.float32)
        context = context.astype(jnp.bfloat16)
        for x in range(NX):
            out_ref[x, :, cols] = context


def attend(info, query, own, first):
    vmem = pl.BlockSpec(memory_space=pltpu.VMEM)
    return pl.pallas_call(
        attend_kernel,
        in_specs=[pl.BlockSpec(memory_space=pltpu.SMEM), vmem, vmem, vmem],
        out_specs=vmem,
        out_shape=jax.ShapeDtypeStruct((NX, HALF, CHIP), jnp.bfloat16),
        compiler_params=pltpu.CompilerParams(vmem_limit_bytes=VMEM),
        name="attend",
    )(info, query, own, first)


def output_kernel(info_ref, ctx_ref, own_ref, other_ref, out_ref, rows, weights, sems):
    copies = fetch(own_ref, other_ref, weights, sems)
    depth = rows.shape[1]
    for i in range(depth // CHIP):
        rows[:, i * CHIP : (i + 1) * CHIP] = ctx_ref[i]
    core, z, y = info_ref[0], info_ref[2], info_ref[3]
    for i in range(NY):
        for copy in copies[i]:
            copy.wait()
        source = lax.rem(y + NY - i, NY)
        for part in range(NZ):
            cut = slice(part * depth, (part + 1) * depth)
            weight = jnp.concatenate([weights[0, i, cut], weights[1, i, cut]], axis=1)
            total = jnp.dot(rows[...], weight, preferred_element_type=jnp.float32)
            total = total.astype(jnp.bfloat16)
            first = (z if part == 0 else 1 - z) * NC
            out_ref[source, :, aligned(first + core)] = total[:, :HD]
            out_ref[source, :, aligned(first + 1 - core)] = total[:, HD:]


def output(info, context, wo):
    vmem = pl.BlockSpec(memory_space=pltpu.VMEM)
    return pl.pallas_call(
        output_kernel,
        in_specs=[
            pl.BlockSpec(memory_space=pltpu.SMEM),
            vmem,
            pl.BlockSpec(memory_space=pl.ANY),
            pl.BlockSpec(memory_space=pl.ANY),
        ],
        out_specs=vmem,
        out_shape=jax.ShapeDtypeStruct((NY, HALF, NZ * CHIP), jnp.bfloat16),
        scratch_shapes=[pltpu.VMEM((HALF, NX * CHIP), jnp.bfloat16)] + weight_scratch(),
        compiler_params=pltpu.CompilerParams(vmem_limit_bytes=VMEM),
        name="output",
    )(info, context, *wo)


def ranks(placement, core):
    owners = placement[:, 0]
    order = jnp.arange(owners.shape[0], dtype=jnp.int32)
    earlier = (order[None, :] < order[:, None]) & (owners[:, None] == owners[None, :])
    rank = jnp.sum(earlier.astype(jnp.int32), axis=1)
    blocks = HALF // BLOCK
    here = jnp.arange(ITEMS_HERE, dtype=jnp.int32)
    mine = (core * blocks + here % blocks) * NG + here // blocks
    match = mine[:, None] == order[None, :]
    item_owner = jnp.sum(jnp.where(match, owners[None, :], 0), axis=1)
    item_rank = jnp.sum(jnp.where(match, rank[None, :], 0), axis=1)
    return item_owner, item_rank


def last_to_first(flip):
    return [((SECTIONS - 1) * WIDE + w, w ^ flip) for w in range(WIDE)]


def relay_pairs(first):
    same, cross = [], []
    for s in range(first, SECTIONS - 1, 2):
        for w in range(WIDE):
            same.append((s * WIDE + w, (s + 1) * WIDE + w))
            cross.append((s * WIDE + w, (s + 1) * WIDE + (w ^ 8)))
    return same, cross


def shards(hidden_in, gain, w_query, w_key, w_value, w_out, length, placement):
    segment = lax.axis_index("segment")
    wide = lax.axis_index("wide")
    core = wide % 2
    z = wide // 8 % 2
    x = wide // 2 % NX
    y = wide // 16
    features = gain.shape[1]

    halves = hidden_in.reshape(2, HALF, HD)
    kept = lax.dynamic_index_in_dim(halves, core, 0, keepdims=False)
    given = lax.dynamic_index_in_dim(halves, 1 - core, 0, keepdims=False)
    from_core = swap_cores(given)
    flat = ("segment", "wide")
    cross_own = lax.ppermute(kept, flat, last_to_first(8))
    cross_other = lax.ppermute(given, flat, last_to_first(9))
    start = by_core(core, kept, from_core, 1)
    cross = by_core(core, cross_own, cross_other, 1)

    lane = jnp.arange(HD, dtype=jnp.int32)
    freq = jnp.power(ROPE_BASE, -2.0 * (lane // 2).astype(jnp.float32) / HD)
    position = (core * HALF + jnp.arange(HALF, dtype=jnp.int32)).astype(jnp.float32)
    angle = position[:, None] * freq[None, :]
    cos = jnp.cos(angle)
    sin = jnp.where(lane[None, :] % 2 == 0, -1.0, 1.0) * jnp.sin(angle)
    info = jnp.stack([core, length[0], z, y]).astype(jnp.int32)

    raw = w_out[0].reshape(NY, NZ * NX * CHIP, HD)

    halves = raw.reshape(NY, NZ, NX * CHIP, HD)

    kept_rows = lax.dynamic_index_in_dim(halves, z, 1, keepdims=False)
    given_rows = lax.dynamic_index_in_dim(halves, 1 - z, 1, keepdims=False)
    blocks_x = x_blocks(w_query[0])
    both = kv_blocks(w_key[0], w_value[0])
    blocks_x, both, given_rows = lax.optimization_barrier((blocks_x, both, given_rows))

    def prepare(before, late):
        kept, given = kept_rows, given_rows
        query = exchange(blocks_x, OVER_X)
        mine = kv_over_x(both, x, query)
        if late:
            given = lax.optimization_barrier((given, query, mine))[0]
        far = lax.ppermute(given, "wide", Z_SWAP)
        rows_gain = lax.dynamic_index_in_dim(gain.reshape(NG, NX, CHIP), x, 1, keepdims=False)
        key_value = relayout_kv(mine, core, x)
        out_rows = jnp.concatenate([kept, far], axis=1)
        out_rows = lax.optimization_barrier((out_rows, before))[0]
        blocks = from_ring(lambda i: lax.dynamic_slice_in_dim(out_rows, i, 1, 0), y, 16)
        out = jnp.concatenate(lax.optimization_barrier((blocks, mine))[0], axis=0)
        gains = rows_gain.reshape(1, NG * CHIP)
        return (query, swap_cores(query)), key_value, (out, swap_cores(out)), gains

    def early_section(start, cross):
        pair = jnp.where(
            z == 0,
            jnp.concatenate([start, cross], axis=1),
            jnp.concatenate([cross, start], axis=1),
        )
        gathered = in_order(jnp.concatenate(from_ring(lambda i: pair[None], y, 16)), y)
        items = jnp.zeros((ITEMS_HERE,), jnp.int32)
        return gathered, prepare(gathered, False), (items, items)

    def late_section(start, cross):
        blank = jnp.zeros((NY, HALF, NZ * CHIP), jnp.bfloat16)
        return blank, prepare(start, True), ranks(placement, core)

    gathered, (wq, wkv, wo, gain_x), items = lax.cond(
        segment <= 1, early_section, late_section, start, cross
    )
    cos, sin = lax.optimization_barrier((cos, sin))

    def later_gather(same, cross):
        return exchange(join(same, cross), OVER_Y)

    def summed(parts, own):
        parts = parts.astype(jnp.float32)
        return own.astype(jnp.float32) + (parts[0] + parts[1] + parts[2] + parts[3])

    def half_out(context, own):
        parts = exchange(output(info, exchange(context, OVER_X), wo), OVER_Y)
        return summed(parts, jnp.where(z == 0, own, jnp.zeros_like(own))).astype(jnp.bfloat16)

    def layer(gathered):
        parts = exchange(project(info, gathered, gain_x, wq, wkv), OVER_X)
        query, kv = turn(parts, cos, sin, features)
        first = lax.ppermute(kv, "wide", CORE_UP)
        context = attend(info, query, kv, first)
        own = lax.dynamic_index_in_dim(gathered, y, 0, keepdims=False)
        return half_out(context, own), kv

    def send(pairs):
        same, cross = pairs

        def run(value):
            axes = ("segment", "wide")
            return lax.ppermute(value, axes, cross), lax.ppermute(value, axes, same)

        return run

    even, odd = send(relay_pairs(0)), send(relay_pairs(1))

    def tick(t, state):
        gathered, partial, kv = state
        partial, kv = lax.cond(segment == t, layer, lambda gathered: (partial, kv), gathered)

        def hand_on(partial, gathered):
            cross, same = lax.cond(t % 2 == 0, even, odd, partial)
            return lax.cond(
                segment == t + 1, later_gather, lambda same, cross: gathered, same, cross
            )

        gathered = lax.cond(
            ((segment == t) | (segment == t + 1)) & (t < SECTIONS - 1),
            hand_on,
            lambda partial, gathered: gathered,
            partial,
            gathered,
        )
        return gathered, partial, kv

    partial = jnp.zeros((HALF, NZ * CHIP), jnp.bfloat16)
    kv = jnp.zeros((HALF, CHIP), jnp.bfloat16)
    _, partial, kv = lax.fori_loop(0, SECTIONS, tick, (gathered, partial, kv))

    pair = partial.reshape(HALF, NZ, CHIP)
    kept = lax.dynamic_index_in_dim(pair, z, 1, keepdims=False)
    given = lax.dynamic_index_in_dim(pair, 1 - z, 1, keepdims=False)
    other = lax.ppermute(given, "wide", Z_SWAP)
    own = (kept.astype(jnp.float32) + other.astype(jnp.float32)).astype(jnp.bfloat16)
    columns = own.reshape(HALF, NC, HD)
    kept = lax.dynamic_index_in_dim(columns, core, 1, keepdims=False)
    given = lax.dynamic_index_in_dim(columns, 1 - core, 1, keepdims=False)
    outputs = by_core(core, kept, swap_cores(given), 0)

    item_owner, item_rank = lax.cond(
        segment <= 1, lambda: ranks(placement, core), lambda: items
    )
    blocks = HALF // BLOCK
    slots = 2 * placement.shape[0] // WIDE
    slot = jnp.arange(slots, dtype=jnp.int32)

    sent = jnp.broadcast_to(kv[None], (NG, HALF, CHIP))
    rows = exchange(sent, OVER_G).reshape(NG * blocks, BLOCK * CHIP)

    def chosen(owner):
        wanted = (item_owner[None, :] == owner) & (item_rank[None, :] == slot[:, None])
        return jnp.dot(wanted.astype(jnp.bfloat16), rows, preferred_element_type=jnp.float32)

    here = chosen(wide)
    there = chosen(wide ^ 1).astype(jnp.bfloat16)
    cache = (here + swap_cores(there).astype(jnp.float32)).astype(jnp.bfloat16)
    return outputs[None], cache.reshape(1, slots, BLOCK, CHIP)


def solution(mesh):
    in_specs = (
        P(None, "wide"),
        P("segment", None),
        P("segment", None, "wide"),
        P("segment", None, "wide"),
        P("segment", None, "wide"),
        P("segment", None, "wide"),
        P(),
        P(),
    )
    out_specs = (P("segment", None, "wide"), P("segment", "wide", None, None))
    return jax.shard_map(shards, mesh=mesh, in_specs=in_specs, out_specs=out_specs, check_vma=False)
```

```python
import functools
import math

import jax
import jax.numpy as jnp
from jax import lax
from jax.experimental import pallas as pl
from jax.experimental.pallas import tpu as pltpu
from jax.sharding import PartitionSpec as P

HD = 128
BLOCK = 8
NY, NZ, NX, NC = 4, 2, 4, 2
NG = NY * NZ
CHIP = NC * HD
WIDE = NG * NX * NC
SECTIONS = 8
HALF = 128
ITEMS_HERE = NG * HALF // BLOCK
EPS = 1e-05
ROPE_BASE = 500000.0
MASKED = -1e30
VMEM = 16 * 1024 * 1024

OVER_X = [[g * 8 + x * 2 + c for x in range(NX)] for g in range(NG) for c in range(NC)]
OVER_G = [[g * 8 + x * 2 + c for g in range(NG)] for x in range(NX) for c in range(NC)]
OVER_Y = [
    [(y * 2 + z) * 8 + x * 2 + c for y in range(NY)]
    for z in range(NZ)
    for x in range(NX)
    for c in range(NC)
]
Z_SWAP = [(w, w ^ 8) for w in range(WIDE)]
CORE_SWAP = [(w, w ^ 1) for w in range(WIDE)]
CORE_UP = [(w, w + 1) for w in range(0, WIDE, 2)]


def exchange(value, groups):
    return lax.all_to_all(value, "wide", 0, 0, axis_index_groups=groups, tiled=True)


def swap_cores(value):
    return lax.ppermute(value, "wide", CORE_SWAP)


def by_core(core, own, other, axis):
    first = jnp.where(core == 0, own, other)
    second = jnp.where(core == 0, other, own)
    return jnp.concatenate([first, second], axis=axis)


def x_blocks(weight):
    return weight.reshape(NG, NX, CHIP, HD).transpose(1, 0, 2, 3).reshape(NX, NG * CHIP, HD)


def moved(w, stride, step):
    at = w // stride % 4
    return w + ((at + step) % 4 - at) * stride


def from_ring(piece, at, stride):
    blocks = [piece(at)]
    for step in range(1, 4):
        pairs = [(w, moved(w, stride, step)) for w in range(WIDE)]
        blocks.append(lax.ppermute(piece((at + step) % 4), "wide", pairs))
    return blocks


def in_order(blocks, at):
    return jnp.concatenate(
        [lax.dynamic_slice_in_dim(blocks, (at + 4 - i) % 4, 1, 0) for i in range(4)], axis=0
    )


def kv_blocks(w_key, w_value, x, after):
    both = jnp.stack([w_key.T, w_value.T])
    width = both.shape[1]
    both = both.reshape(2, width, NG, NX, CHIP).transpose(3, 0, 1, 2, 4)
    both = both.reshape(NX, 2 * width, NG * CHIP)
    both = lax.optimization_barrier((both, after))[0]
    blocks = from_ring(lambda i: lax.dynamic_slice_in_dim(both, i, 1, 0), x, NC)
    return jnp.concatenate(blocks, axis=0)


def relayout_kv(mine, core, x):
    width = mine.shape[1] // 2
    other = in_order(swap_cores(mine), x).reshape(NX, 2, 1, width, NG * CHIP)
    mine = in_order(mine, x).reshape(NX, 2, 1, width, NG * CHIP)
    full = by_core(core, mine, other, 2)
    return full.transpose(1, 0, 2, 3, 4).reshape(2 * HD, NG * CHIP)


def eye(n):
    return lax.broadcasted_iota(jnp.int32, (n, n), 0) == lax.broadcasted_iota(jnp.int32, (n, n), 1)


def aligned(block, size=1):
    return pl.ds(pl.multiple_of(block * HD, HD), size * HD)


def fetch(own_ref, other_ref, weights, sems):
    copies = []
    for i in range(weights.shape[1]):
        pair = []
        for k, ref in enumerate((own_ref, other_ref)):
            copy = pltpu.make_async_copy(ref.at[i], weights.at[k, i], sems.at[k, i])
            copy.start()
            pair.append(copy)
        copies.append(pair)
    return copies


def project_kernel(
    info_ref, h_ref, gain_ref, wkv_ref, own_ref, other_ref, out_ref, normed, weights, sems
):
    copies = fetch(own_ref, other_ref, weights, sems)
    total = jnp.zeros((HALF, 1), jnp.float32)
    for y in range(NY):
        part = h_ref[y].astype(jnp.float32)
        cols = slice(y * NZ * CHIP, (y + 1) * NZ * CHIP)
        normed[:, cols] = (part * gain_ref[:, cols]).astype(jnp.bfloat16)
        total = total + jnp.sum(part * part, axis=1, keepdims=True)
    row = jnp.sum(jnp.where(eye(HALF), total, 0.0), axis=0, keepdims=True)
    high = row.astype(jnp.bfloat16).astype(jnp.float32)
    upper = lax.broadcasted_iota(jnp.int32, (16, HALF), 0) < 8
    squares = jnp.where(upper, high, row - high).astype(jnp.bfloat16)
    kv = lax.dot_general(
        normed[...], wkv_ref[...], (((1,), (1,)), ((), ())), preferred_element_type=jnp.float32
    ).astype(jnp.bfloat16)
    core = info_ref[0]
    for i in range(NX):
        out_ref[i, :HALF, CHIP:] = kv
        out_ref[i, HALF:, :] = jnp.zeros((16, 2 * CHIP), jnp.bfloat16)
        out_ref[i, HALF:, :HALF] = squares
        for copy in copies[i]:
            copy.wait()
        weight = jnp.concatenate([weights[0, i], weights[1, i]], axis=1)
        query = jnp.dot(normed[...], weight, preferred_element_type=jnp.float32)
        query = query.astype(jnp.bfloat16)
        out_ref[i, :HALF, aligned(core)] = query[:, :HD]
        out_ref[i, :HALF, aligned(1 - core)] = query[:, HD:]


def weight_scratch():
    rows = NG * CHIP
    return [pltpu.VMEM((2, NX, rows, HD), jnp.bfloat16), pltpu.SemaphoreType.DMA((2, NX))]


def project(info, gathered, gain, wq, wkv):
    rows = NG * CHIP
    vmem = pl.BlockSpec(memory_space=pltpu.VMEM)
    return pl.pallas_call(
        project_kernel,
        in_specs=[
            pl.BlockSpec(memory_space=pltpu.SMEM),
            vmem,
            vmem,
            vmem,
            pl.BlockSpec(memory_space=pl.ANY),
            pl.BlockSpec(memory_space=pl.ANY),
        ],
        out_specs=vmem,
        out_shape=jax.ShapeDtypeStruct((NX, HALF + 16, 2 * CHIP), jnp.bfloat16),
        scratch_shapes=[pltpu.VMEM((HALF, rows), jnp.bfloat16)] + weight_scratch(),
        compiler_params=pltpu.CompilerParams(vmem_limit_bytes=VMEM),
        name="project",
    )(info, gathered, gain, wkv, *wq)


def turn_kernel(features, part_ref, cos_ref, sin_ref, q_ref, kv_ref):
    total = jnp.zeros((HALF, 2 * CHIP), jnp.float32)
    squares = jnp.zeros((16, HALF), jnp.float32)
    for x in range(NX):
        total = total + part_ref[x, :HALF, :].astype(jnp.float32)
        squares = squares + part_ref[x, HALF:, :HALF].astype(jnp.float32)
    row = lax.rsqrt((squares[0:1] + squares[8:9]) / features + EPS)
    scale = jnp.sum(jnp.where(eye(HALF), row, 0.0), axis=1, keepdims=True)
    total = total * scale
    even = lax.broadcasted_iota(jnp.int32, (HALF, HD), 1) % 2 == 0

    def rope(part):
        swapped = jnp.where(even, pltpu.roll(part, HD - 1, 1), pltpu.roll(part, 1, 1))
        return (part * cos_ref[...] + swapped * sin_ref[...]).astype(jnp.bfloat16)

    for head in range(NC):
        cols = slice(head * HD, (head + 1) * HD)
        q_ref[:, cols] = rope(total[:, cols])
    kv_ref[:, :HD] = rope(total[:, CHIP : CHIP + HD])
    kv_ref[:, HD:] = total[:, CHIP + HD :].astype(jnp.bfloat16)


def turn(parts, cos, sin, features):
    return pl.pallas_call(
        functools.partial(turn_kernel, float(features)),
        out_shape=[jax.ShapeDtypeStruct((HALF, CHIP), jnp.bfloat16)] * 2,
        compiler_params=pltpu.CompilerParams(vmem_limit_bytes=VMEM),
        name="turn",
    )(parts, cos, sin)


def attend_kernel(info_ref, q_ref, own_ref, first_ref, out_ref):
    core = info_ref[0]
    length = info_ref[1]
    scale = 1.0 / math.sqrt(HD)
    row = lax.broadcasted_iota(jnp.int32, (HALF, HALF), 0)
    col = lax.broadcasted_iota(jnp.int32, (HALF, HALF), 1)
    seen_own = (col <= row) & (col + core * HALF < length)
    seen_first = col < jnp.where(core == 1, length, 0)
    contract = (((1,), (1,)), ((), ()))
    for head in range(NC):
        cols = slice(head * HD, (head + 1) * HD)
        query = q_ref[:, cols]
        own = lax.dot_general(query, own_ref[:, :HD], contract, preferred_element_type=jnp.float32)
        first = lax.dot_general(
            query, first_ref[:, :HD], contract, preferred_element_type=jnp.float32
        )
        own = jnp.where(seen_own, own * scale, MASKED)
        first = jnp.where(seen_first, first * scale, MASKED)
        top = jnp.maximum(
            jnp.max(own, axis=1, keepdims=True), jnp.max(first, axis=1, keepdims=True)
        )
        own = jnp.exp(own - top)
        first = jnp.exp(first - top)
        total = jnp.sum(own, axis=1, keepdims=True) + jnp.sum(first, axis=1, keepdims=True)
        own = (own / total).astype(jnp.bfloat16)
        first = (first / total).astype(jnp.bfloat16)
        context = jnp.dot(own, own_ref[:, HD:], preferred_element_type=jnp.float32)
        context += jnp.dot(first, first_ref[:, HD:], preferred_element_type=jnp.float32)
        context = context.astype(jnp.bfloat16)
        for x in range(NX):
            out_ref[x, :, cols] = context


def attend(info, query, own, first):
    vmem = pl.BlockSpec(memory_space=pltpu.VMEM)
    return pl.pallas_call(
        attend_kernel,
        in_specs=[pl.BlockSpec(memory_space=pltpu.SMEM), vmem, vmem, vmem],
        out_specs=vmem,
        out_shape=jax.ShapeDtypeStruct((NX, HALF, CHIP), jnp.bfloat16),
        compiler_params=pltpu.CompilerParams(vmem_limit_bytes=VMEM),
        name="attend",
    )(info, query, own, first)


def output_kernel(info_ref, ctx_ref, own_ref, other_ref, out_ref, rows, weights, sems):
    copies = fetch(own_ref, other_ref, weights, sems)
    depth = rows.shape[1]
    for i in range(depth // CHIP):
        rows[:, i * CHIP : (i + 1) * CHIP] = ctx_ref[i]
    core, z, y = info_ref[0], info_ref[2], info_ref[3]
    for i in range(NY):
        for copy in copies[i]:
            copy.wait()
        source = lax.rem(y + NY - i, NY)
        for part in range(NZ):
            cut = slice(part * depth, (part + 1) * depth)
            weight = jnp.concatenate([weights[0, i, cut], weights[1, i, cut]], axis=1)
            total = jnp.dot(rows[...], weight, preferred_element_type=jnp.float32)
            total = total.astype(jnp.bfloat16)
            first = (z if part == 0 else 1 - z) * NC
            out_ref[source, :, aligned(first + core)] = total[:, :HD]
            out_ref[source, :, aligned(first + 1 - core)] = total[:, HD:]


def output(info, context, wo):
    vmem = pl.BlockSpec(memory_space=pltpu.VMEM)
    return pl.pallas_call(
        output_kernel,
        in_specs=[
            pl.BlockSpec(memory_space=pltpu.SMEM),
            vmem,
            pl.BlockSpec(memory_space=pl.ANY),
            pl.BlockSpec(memory_space=pl.ANY),
        ],
        out_specs=vmem,
        out_shape=jax.ShapeDtypeStruct((NY, HALF, NZ * CHIP), jnp.bfloat16),
        scratch_shapes=[pltpu.VMEM((HALF, NX * CHIP), jnp.bfloat16)] + weight_scratch(),
        compiler_params=pltpu.CompilerParams(vmem_limit_bytes=VMEM),
        name="output",
    )(info, context, *wo)


def ranks(placement, core):
    owners = placement[:, 0]
    order = jnp.arange(owners.shape[0], dtype=jnp.int32)
    earlier = (order[None, :] < order[:, None]) & (owners[:, None] == owners[None, :])
    rank = jnp.sum(earlier.astype(jnp.int32), axis=1)
    blocks = HALF // BLOCK
    here = jnp.arange(ITEMS_HERE, dtype=jnp.int32)
    mine = (core * blocks + here % blocks) * NG + here // blocks
    match = mine[:, None] == order[None, :]
    item_owner = jnp.sum(jnp.where(match, owners[None, :], 0), axis=1)
    item_rank = jnp.sum(jnp.where(match, rank[None, :], 0), axis=1)
    return item_owner, item_rank


def last_to_first(flip):
    return [((SECTIONS - 1) * WIDE + w, w ^ flip) for w in range(WIDE)]


def relay_pairs(first):
    same, cross = [], []
    for s in range(first, SECTIONS - 1, 2):
        for w in range(WIDE):
            same.append((s * WIDE + w, (s + 1) * WIDE + w))
            cross.append((s * WIDE + w, (s + 1) * WIDE + (w ^ 8)))
    return same, cross


def shards(hidden_in, gain, w_query, w_key, w_value, w_out, length, placement):
    segment = lax.axis_index("segment")
    wide = lax.axis_index("wide")
    core = wide % 2
    z = wide // 8 % 2
    x = wide // 2 % NX
    y = wide // 16
    features = gain.shape[1]

    halves = hidden_in.reshape(2, HALF, HD)
    kept = lax.dynamic_index_in_dim(halves, core, 0, keepdims=False)
    given = lax.dynamic_index_in_dim(halves, 1 - core, 0, keepdims=False)
    from_core = swap_cores(given)
    flat = ("segment", "wide")
    cross_own = lax.ppermute(kept, flat, last_to_first(8))
    cross_other = lax.ppermute(given, flat, last_to_first(9))
    start = by_core(core, kept, from_core, 1)
    cross = by_core(core, cross_own, cross_other, 1)

    gain_x = lax.dynamic_index_in_dim(gain.reshape(NG, NX, CHIP), x, 1, keepdims=False)
    gain_x = gain_x.reshape(1, NG * CHIP)

    lane = jnp.arange(HD, dtype=jnp.int32)
    freq = jnp.power(ROPE_BASE, -2.0 * (lane // 2).astype(jnp.float32) / HD)
    position = (core * HALF + jnp.arange(HALF, dtype=jnp.int32)).astype(jnp.float32)
    angle = position[:, None] * freq[None, :]
    cos = jnp.cos(angle)
    sin = jnp.where(lane[None, :] % 2 == 0, -1.0, 1.0) * jnp.sin(angle)
    info = jnp.stack([core, length[0], z, y]).astype(jnp.int32)

    def gather(pair):
        return exchange(jnp.broadcast_to(pair[None], (NY, HALF, NZ * CHIP)), OVER_Y)

    raw = w_out[0].reshape(NY, NZ * NX * CHIP, HD)

    halves = raw.reshape(NY, NZ, NX * CHIP, HD)

    def prepare(before, late):
        kept = lax.dynamic_index_in_dim(halves, z, 1, keepdims=False)
        given = lax.dynamic_index_in_dim(halves, 1 - z, 1, keepdims=False)
        rows = x_blocks(w_query[0])
        query = exchange(rows, OVER_X)
        mine = kv_blocks(w_key[0], w_value[0], x, query)
        if late:
            given = lax.optimization_barrier((given, query, mine))[0]
        far = lax.ppermute(given, "wide", Z_SWAP)
        key_value = relayout_kv(mine, core, x)
        out_rows = jnp.concatenate([kept, far], axis=1)
        out_rows = lax.optimization_barrier((out_rows, before))[0]
        blocks = from_ring(lambda i: lax.dynamic_slice_in_dim(out_rows, i, 1, 0), y, 16)
        out = jnp.concatenate(lax.optimization_barrier((blocks, mine))[0], axis=0)
        return (query, swap_cores(query)), key_value, (out, swap_cores(out))

    def early_section(start, cross):
        pair = jnp.where(
            z == 0,
            jnp.concatenate([start, cross], axis=1),
            jnp.concatenate([cross, start], axis=1),
        )
        gathered = in_order(jnp.concatenate(from_ring(lambda i: pair[None], y, 16)), y)
        items = jnp.zeros((ITEMS_HERE,), jnp.int32)
        return gathered, prepare(gathered, False), (items, items)

    def late_section(start, cross):
        blank = jnp.zeros((NY, HALF, NZ * CHIP), jnp.bfloat16)
        return blank, prepare(start, True), ranks(placement, core)

    gathered, (wq, wkv, wo), items = lax.cond(
        segment <= 1, early_section, late_section, start, cross
    )
    cos, sin = lax.optimization_barrier((cos, sin))

    def later_gather(same, cross):
        return gather((same.astype(jnp.float32) + cross.astype(jnp.float32)).astype(jnp.bfloat16))

    def summed(parts, own):
        parts = parts.astype(jnp.float32)
        return own.astype(jnp.float32) + (parts[0] + parts[1] + parts[2] + parts[3])

    def half_out(context, own):
        parts = exchange(output(info, exchange(context, OVER_X), wo), OVER_Y)
        return summed(parts, jnp.where(z == 0, own, jnp.zeros_like(own))).astype(jnp.bfloat16)

    def layer(gathered):
        parts = exchange(project(info, gathered, gain_x, wq, wkv), OVER_X)
        query, kv = turn(parts, cos, sin, features)
        first = lax.ppermute(kv, "wide", CORE_UP)
        context = attend(info, query, kv, first)
        own = lax.dynamic_index_in_dim(gathered, y, 0, keepdims=False)
        return half_out(context, own), kv

    def send(pairs):
        same, cross = pairs

        def run(value):
            axes = ("segment", "wide")
            return lax.ppermute(value, axes, cross), lax.ppermute(value, axes, same)

        return run

    even, odd = send(relay_pairs(0)), send(relay_pairs(1))

    def tick(t, state):
        gathered, partial, kv = state
        partial, kv = lax.cond(segment == t, layer, lambda gathered: (partial, kv), gathered)

        def hand_on(partial, gathered):
            cross, same = lax.cond(t % 2 == 0, even, odd, partial)
            return lax.cond(
                segment == t + 1, later_gather, lambda same, cross: gathered, same, cross
            )

        gathered = lax.cond(
            ((segment == t) | (segment == t + 1)) & (t < SECTIONS - 1),
            hand_on,
            lambda partial, gathered: gathered,
            partial,
            gathered,
        )
        return gathered, partial, kv

    partial = jnp.zeros((HALF, NZ * CHIP), jnp.bfloat16)
    kv = jnp.zeros((HALF, CHIP), jnp.bfloat16)
    _, partial, kv = lax.fori_loop(0, SECTIONS, tick, (gathered, partial, kv))

    pair = partial.reshape(HALF, NZ, CHIP)
    by_half = jnp.broadcast_to(pair.transpose(1, 0, 2)[None], (NY, NZ, HALF, CHIP))
    sent = jnp.concatenate(
        [jnp.broadcast_to(kv[None], (NG, HALF, CHIP)), by_half.reshape(NG, HALF, CHIP)], axis=2
    )
    got = exchange(sent, OVER_G)

    kept = lax.dynamic_index_in_dim(pair, z, 1, keepdims=False)
    other = lax.dynamic_slice(got, (y * NZ + 1 - z, 0, CHIP), (1, HALF, CHIP))[0]
    own = (kept.astype(jnp.float32) + other.astype(jnp.float32)).astype(jnp.bfloat16)
    columns = own.reshape(HALF, NC, HD)
    kept = lax.dynamic_index_in_dim(columns, core, 1, keepdims=False)
    given = lax.dynamic_index_in_dim(columns, 1 - core, 1, keepdims=False)
    outputs = by_core(core, kept, swap_cores(given), 0)

    item_owner, item_rank = lax.cond(
        segment <= 1, lambda: ranks(placement, core), lambda: items
    )
    blocks = HALF // BLOCK
    slots = 2 * placement.shape[0] // WIDE
    slot = jnp.arange(slots, dtype=jnp.int32)

    rows = got[:, :, :CHIP].reshape(NG * blocks, BLOCK * CHIP)

    def chosen(owner):
        wanted = (item_owner[None, :] == owner) & (item_rank[None, :] == slot[:, None])
        return jnp.dot(wanted.astype(jnp.bfloat16), rows, preferred_element_type=jnp.float32)

    here = chosen(wide)
    there = chosen(wide ^ 1).astype(jnp.bfloat16)
    cache = (here + swap_cores(there).astype(jnp.float32)).astype(jnp.bfloat16)
    return outputs[None], cache.reshape(1, slots, BLOCK, CHIP)


def solution(mesh):
    in_specs = (
        P(None, "wide"),
        P("segment", None),
        P("segment", None, "wide"),
        P("segment", None, "wide"),
        P("segment", None, "wide"),
        P("segment", None, "wide"),
        P(),
        P(),
    )
    out_specs = (P("segment", None, "wide"), P("segment", "wide", None, None))
    return jax.shard_map(shards, mesh=mesh, in_specs=in_specs, out_specs=out_specs, check_vma=False)
```
